128 devices in a mesh: dp: 4 (over x_lo, core), blk: 32 (over y, z, x_hi).
Axes of the slice: x: 4 (x_hi: 2, x_lo: 2; x = x_hi * 2 + x_lo), y: 4, z: 4, core: 2. Of those that a mesh axis runs over, the one named last changes fastest.
Arguments:
- tokens: bfloat16 [32768, 768], P(('dp', 'blk')), may hold values from -6 to 6
- attn_gain: bfloat16 [768], replicated, may hold values from 0.099609375 to 1.8984375
- attn_bias: bfloat16 [768], replicated, may hold values from -3 to 3
- mlp_gain: bfloat16 [768], replicated, may hold values from 0.099609375 to 1.8984375
- mlp_bias: bfloat16 [768], replicated, may hold values from -3 to 3
- qkv_weight: bfloat16 [768, 2304], replicated, may hold values from -0.21875 to 0.21875
- qkv_bias: bfloat16 [2304], replicated, may hold values from -3 to 3
- out_weight: bfloat16 [768, 768], replicated, may hold values from -1.75 to 1.75
- out_bias: bfloat16 [768], replicated, may hold values from -3 to 3
- up_weight: bfloat16 [768, 3072], replicated, may hold values from -0.21875 to 0.21875
- up_bias: bfloat16 [3072], replicated, may hold values from -3 to 3
- down_weight: bfloat16 [3072, 768], replicated, may hold values from -0.109375 to 0.109375
- down_bias: bfloat16 [768], replicated, may hold values from -3 to 3
- cotangent: bfloat16 [32768, 768], P(('dp', 'blk')), may hold values from -6 to 6
- doc_lengths: int32 [4, 16], P('dp'), may hold values from 1 to 4096, as said below
- span_order: int32 [4, 64], P('dp'), may hold values from 0 to 63, as said below
Outputs:
- mixed: bfloat16 [32768, 768], P(('dp', 'blk'))
- tokens_grad: float32 [32768, 768], P(('dp', 'blk'))
- grad_attn_gain: float32 [768], replicated
- grad_attn_bias: float32 [768], replicated
- grad_mlp_gain: float32 [768], replicated
- grad_mlp_bias: float32 [768], replicated
- grad_qkv_weight: float32 [768, 2304], replicated
- grad_qkv_bias: float32 [2304], replicated
- grad_out_weight: float32 [768, 768], replicated
- grad_out_bias: float32 [768], replicated
- grad_up_weight: float32 [768, 3072], replicated
- grad_up_bias: float32 [3072], replicated
- grad_down_weight: float32 [3072, 768], replicated
- grad_down_bias: float32 [768], replicated
- rms_output: float32 [], replicated
- rms_attention: float32 [], replicated
- rms_mlp: float32 [], replicated
The draws below stay inside these ranges and needn't reach their ends.
Inputs may be any that keep to these rules, and one draw needn't show every extreme that they name: `doc_lengths`: in each row one sequence of 4096 tokens stands first or last; the other 15 hold at most 512 tokens each and together 4096, and one of them holds exactly 512. `span_order`: each row is a permutation of the 64 spans of 128 stream places; entries 2 i and 2 i + 1 are the spans of device i along blk, in that order in its rows; the first is under 64 / 2 and the two add up to 63.
All inputs are finite; a program needn't handle non-finite values.
Results may differ from the reference program's by a relative error of at most 0.011.
Values may be sent and summed in bfloat16 or wider, within the bound.
A program may use at most 192 MiB of HBM per device.

```python
import math
import jax
import jax.numpy as jnp
from jax import lax

D = 768
HEADS = 12
HEAD_DIM = 64
ROTARY = 16
FF = 3072
TOK_DEV = 256
MOST = 512
GROUPS = 4
TOKENS = 32768
HALF = 4096
PAIRS = 7
SPANS = 64


def draw_doc_lengths(key, part):
    key = jax.random.fold_in(key, 5)
    offset_key, shuffle_key, first_key = jax.random.split(key, 3)
    half_most = MOST // 2
    offsets = jax.random.randint(offset_key, (GROUPS, PAIRS), -(half_most - 1), half_most)
    paired = jnp.stack([half_most + offsets, half_most - offsets], axis=-1).reshape(GROUPS, 2 * PAIRS)
    shorts = jnp.concatenate([jnp.full((GROUPS, 1), MOST, jnp.int32), paired.astype(jnp.int32)], axis=1)
    ranks = jax.random.randint(shuffle_key, (GROUPS, 2 * PAIRS + 1), 0, 1 << 20) * (2 * PAIRS + 1) + jnp.arange(2 * PAIRS + 1)
    shuffle = jnp.argsort(ranks, axis=1)
    shorts = jnp.take_along_axis(shorts, shuffle, axis=1)
    longs = jnp.full((GROUPS, 1), HALF, jnp.int32)
    first = jax.random.randint(first_key, (GROUPS, 1), 0, 2)
    joined = jnp.where(first == 1, jnp.concatenate([longs, shorts], axis=1), jnp.concatenate([shorts, longs], axis=1))
    return joined.astype(jnp.int32)


def draw_span_order(key, part):
    key = jax.random.fold_in(key, 9)
    devices = SPANS // 2
    ranks = jax.random.randint(key, (GROUPS, devices), 0, 1 << 20) * devices + jnp.arange(devices)
    picked = jnp.argsort(ranks, axis=1).astype(jnp.int32)
    return jnp.stack([picked, SPANS - 1 - picked], axis=-1).reshape(GROUPS, SPANS).astype(jnp.int32)


def level_of(own_key, shape, shards, smallest, top_value):
    def one(axis_at, blocks):
        steps = jax.random.uniform(jax.random.fold_in(jax.random.fold_in(own_key, 6), axis_at), (blocks,), jnp.float32, smallest / len(shards), top_value / len(shards))
        return jnp.repeat(jnp.exp(steps), shape[axis_at] // blocks).reshape((-1,) + (1,) * (len(shape) - axis_at - 1))

    factor_of = one(*shards[0])
    for cut in shards[1:]:
        factor_of = factor_of * one(*cut)
    return factor_of


def gaussian(stream_key, extent, scale, limit, pieces=(), kind=jnp.bfloat16):
    level = level_of(stream_key, extent, pieces, -0.22, 0.18) if pieces else 1.0
    entries = jax.random.normal(stream_key, extent, jnp.float32) * scale * level
    return jnp.minimum(jnp.maximum(entries, -limit), limit).astype(kind)


def setup_inputs(seed: int = 0) -> dict:
    key_list = jax.random.split(jax.random.key(seed), 17)
    tokens = gaussian(key_list[0], (TOKENS, D), 1.0, 6.0, ((0, 128),))
    attn_gain = jnp.clip(1.0 + 0.18 * jax.random.normal(key_list[1], (D,), jnp.float32), 0.099609375, 1.8984375).astype(jnp.bfloat16)
    attn_bias = gaussian(key_list[2], (D,), 0.5, 3.0)
    mlp_gain = jnp.clip(1.0 + 0.18 * jax.random.normal(key_list[3], (D,), jnp.float32), 0.099609375, 1.8984375).astype(jnp.bfloat16)
    mlp_bias = gaussian(key_list[4], (D,), 0.5, 3.0)
    qkv_weight = gaussian(key_list[5], (D, 3 * D), D ** -0.5, 0.21875)
    qkv_bias = gaussian(key_list[6], (3 * D,), 0.5, 3.0)
    out_weight = gaussian(key_list[7], (D, D), (max(D // 64, 2)) ** -0.5, 1.75)
    out_bias = gaussian(key_list[8], (D,), 0.5, 3.0)
    up_weight = gaussian(key_list[9], (D, FF), D ** -0.5, 0.21875)
    up_bias = gaussian(key_list[10], (FF,), 0.5, 3.0)
    down_weight = gaussian(key_list[11], (FF, D), FF ** -0.5, 0.109375)
    down_bias = gaussian(key_list[12], (D,), 0.5, 3.0)
    cotangent = gaussian(key_list[13], (TOKENS, D), 1.0, 6.0, ((0, 128),))
    doc_lengths = draw_doc_lengths(jax.random.fold_in(key_list[16], 71), 0)
    span_order = draw_span_order(jax.random.fold_in(key_list[16], 71), 0)
    return {"tokens": tokens, "attn_gain": attn_gain, "attn_bias": attn_bias, "mlp_gain": mlp_gain, "mlp_bias": mlp_bias, "qkv_weight": qkv_weight, "qkv_bias": qkv_bias, "out_weight": out_weight, "out_bias": out_bias, "up_weight": up_weight, "up_bias": up_bias, "down_weight": down_weight, "down_bias": down_bias, "cotangent": cotangent, "doc_lengths": doc_lengths, "span_order": span_order}


@jax.custom_vjp
def low(v):
    return lax.optimization_barrier(v.astype(jnp.bfloat16)).astype(jnp.float32)

@jax.custom_vjp
def low_back(v):
    return v

def low_keep(v):
    return (low(v), None)

def low_pass(kept, grad):
    return (grad,)

def back_keep(v):
    return (v, None)

def back_low(kept, grad):
    return (low(grad),)
low.defvjp(low_keep, low_pass)
low_back.defvjp(back_keep, back_low)
epsilon = 1e-05
masked_score = -1e+30

def layer_norm(values, gain_vec, shift_vec):
    center = values - lax.optimization_barrier(jnp.mean(values, axis=-1, keepdims=True))
    spread = lax.optimization_barrier(jnp.mean(center * center, axis=-1, keepdims=True))
    return center * lax.rsqrt(spread + epsilon) * gain_vec + shift_vec

def rotary_tables(position, rotary_dims):
    half_dims = rotary_dims // 2
    steps_vec = jnp.arange(half_dims).astype(jnp.float32)
    inverse = jnp.exp(steps_vec * (-2.0 * math.log(10000.0) / rotary_dims))
    angles = position.astype(jnp.float32)[:, None] * inverse[None, :]
    return (jnp.cos(angles), jnp.sin(angles))

def rotate(values, cosine, sine_part):
    half_dims = cosine.shape[-1]
    first_half = values[..., :half_dims]
    second_half = values[..., half_dims:2 * half_dims]
    cos_rows = cosine[:, None, :]
    sin_rows = sine_part[:, None, :]
    return jnp.concatenate([first_half * cos_rows - second_half * sin_rows, second_half * cos_rows + first_half * sin_rows, values[..., 2 * half_dims:]], axis=-1)

def stream_rows(rows_global, order_row, piece_rows):
    slots = rows_global // piece_rows
    table = jnp.arange(order_row.shape[0], dtype=jnp.int32)
    span_ids = lax.optimization_barrier(jnp.sum(jnp.where(slots[:, None] == table[None, :], order_row[None, :], 0), axis=1)).astype(jnp.int32)
    return (span_ids * piece_rows + rows_global % piece_rows).astype(jnp.int32)

def segment_rows(stream, lengths_row):
    ends = jnp.cumsum(lengths_row).astype(jnp.int32)
    segment = lax.optimization_barrier(jnp.sum((ends[None, :] <= stream[:, None]).astype(jnp.int32), axis=1)).astype(jnp.int32)
    table = jnp.arange(lengths_row.shape[0], dtype=jnp.int32)
    starts = lax.optimization_barrier(jnp.sum(jnp.where(segment[:, None] == table[None, :], (ends - lengths_row)[None, :], 0), axis=1)).astype(jnp.int32)
    return (segment, (stream - starts).astype(jnp.int32))

def attend(queries, keys, values, segment, places):
    count_rows = queries.shape[0]
    block_rows = min(512, count_rows)
    scale_val = HEAD_DIM ** (-0.5)

    def one_block(block_inputs):
        query_block, segment_block, places_block = block_inputs
        scores = jnp.einsum('qhd,khd->hqk', query_block, keys, precision=lax.Precision.HIGHEST) * scale_val
        scores = low_back(scores)
        allowed = (segment_block[:, None] == segment[None, :]) & (places[None, :] <= places_block[:, None])
        scores = jnp.where(allowed[None], scores, masked_score)
        top_score = lax.optimization_barrier(jnp.max(scores, axis=-1, keepdims=True))
        raised = jnp.exp(scores - top_score)
        probs = low(raised / lax.optimization_barrier(jnp.sum(raised, axis=-1, keepdims=True)))
        return jnp.einsum('hqk,khd->qhd', probs, values, precision=lax.Precision.HIGHEST)
    blocks = count_rows // block_rows
    stacked = (queries.reshape(blocks, block_rows, HEADS, HEAD_DIM), segment.reshape(blocks, block_rows), places.reshape(blocks, block_rows))
    return lax.map(jax.checkpoint(one_block), stacked).reshape(count_rows, HEADS, HEAD_DIM)

def forward(weights, inputs, segment, places, position):
    attn_gain, attn_bias, mlp_gain, mlp_bias, qkv_weight, qkv_bias, out_weight, out_bias, up_weight, up_bias, down_weight, down_bias = weights
    row_count = inputs.shape[0]
    highest = lax.Precision.HIGHEST
    head_shape = (row_count, HEADS, HEAD_DIM)
    h_attn = layer_norm(inputs, attn_gain, attn_bias)
    h_mlp = layer_norm(inputs, mlp_gain, mlp_bias)
    mixed_qkv = low_back(jnp.dot(low(h_attn), qkv_weight, precision=highest) + qkv_bias)
    cosine, sine_part = rotary_tables(position, ROTARY)
    queries = low(rotate(mixed_qkv[:, :D].reshape(head_shape), cosine, sine_part))
    keys = low(rotate(mixed_qkv[:, D:2 * D].reshape(head_shape), cosine, sine_part))
    values = low(mixed_qkv[:, 2 * D:].reshape(head_shape))
    attended = attend(queries, keys, values, segment, places).reshape(row_count, D)
    attended = low(low_back(attended))
    attn_branch = jnp.dot(attended, out_weight, precision=highest) + out_bias
    pre_act = low_back(jnp.dot(low(h_mlp), up_weight, precision=highest) + up_bias)
    hidden = low(jax.nn.gelu(pre_act, approximate=False))
    mlp_branch = jnp.dot(hidden, down_weight, precision=highest) + down_bias
    return (inputs + attn_branch + mlp_branch, (attn_branch, mlp_branch))

def pick_rows(group_block, index_vec):
    return group_block[index_vec]

def reference(tokens, attn_gain, attn_bias, mlp_gain, mlp_bias, qkv_weight, qkv_bias, out_weight, out_bias, up_weight, up_bias, down_weight, down_bias, cotangent, doc_lengths, span_order):
    weights = tuple((item.astype(jnp.float32) for item in (attn_gain, attn_bias, mlp_gain, mlp_bias, qkv_weight, qkv_bias, out_weight, out_bias, up_weight, up_bias, down_weight, down_bias)))
    group_rows = 2 * HALF
    piece_rows = TOK_DEV // 2
    ordinal = jnp.arange(group_rows, dtype=jnp.int32)

    def layout(order_row, lengths_row):
        stream = stream_rows(ordinal, order_row, piece_rows)
        inverse = jnp.zeros((group_rows,), jnp.int32).at[stream].set(ordinal)
        segment, position = segment_rows(ordinal, lengths_row)
        return (stream, inverse, segment, position)
    stream, inverse, segment, position = jax.vmap(layout)(span_order, doc_lengths)
    halves = GROUPS * 2

    def to_stream(array):
        grouped = array.astype(jnp.float32).reshape(GROUPS, group_rows, D)
        return jax.vmap(pick_rows)(grouped, inverse).reshape(halves, HALF, D)
    inputs_all = to_stream(tokens)
    grads_all = to_stream(cotangent)
    segment_all = segment.reshape(halves, HALF)
    position_all = position.reshape(halves, HALF)
    places_half = jnp.arange(HALF, dtype=jnp.int32)
    zero_grads = tuple((jnp.zeros_like(item) for item in weights))

    def half_step(carry, slab):
        grad_sums, square_sums = carry
        inputs_now, grad_now, segment_now, position_now = slab

        def wrapped(weight_set, inputs_in):
            return forward(weight_set, inputs_in, segment_now, places_half, position_now)
        output, back_fn, branches = jax.vjp(wrapped, weights, inputs_now, has_aux=True)
        grad_weights, grad_inputs = back_fn(grad_now)
        grad_sums = jax.tree.map(jnp.add, grad_sums, grad_weights)
        squares = jnp.stack([jnp.sum(output * output), jnp.sum(branches[0] * branches[0]), jnp.sum(branches[1] * branches[1])])
        return ((grad_sums, square_sums + squares), (output, grad_inputs))
    (grad_sums, square_sums), (outputs, grad_inputs) = lax.scan(half_step, (zero_grads, jnp.zeros((3,), jnp.float32)), (inputs_all, grads_all, segment_all, position_all))

    def to_layout(array):
        grouped = array.reshape(GROUPS, group_rows, D)
        return jax.vmap(pick_rows)(grouped, stream).reshape(TOKENS, D)
    mixed = to_layout(outputs).astype(jnp.bfloat16)
    tokens_grad = to_layout(grad_inputs)
    roots = jnp.sqrt(square_sums / (TOKENS * D))
    return (mixed, tokens_grad, grad_sums[0], grad_sums[1], grad_sums[2], grad_sums[3], grad_sums[4], grad_sums[5], grad_sums[6], grad_sums[7], grad_sums[8], grad_sums[9], grad_sums[10], grad_sums[11], roots[0], roots[1], roots[2])
```

```python
import functools
import math

import jax
import jax.numpy as jnp
from jax import lax
from jax.experimental import pallas as pl
from jax.experimental.pallas import tpu as pltpu
from jax.sharding import PartitionSpec as P


D = 768
HEADS = 12
ROT = 16
FF = 3072
HALF = 4096
SPANS = 32
LROWS = 192
SROWS = 448
EPS = 1e-05
NEG = -1e30
SMALL = 80
BF = jnp.bfloat16
F32 = jnp.float32
MESH = pl.DeviceIdType.MESH
NT = (((1,), (1,)), ((), ()))
TN = (((0,), (0,)), ((), ()))


def mm(a, b):
    return jnp.dot(a, b, preferred_element_type=F32)


def mm_nt(a, b):
    return lax.dot_general(a, b, NT, preferred_element_type=F32)


def mm_tn(a, b):
    return lax.dot_general(a, b, TN, preferred_element_type=F32)


def halves(ref, off):
    first = ref[pl.ds(pl.multiple_of(off, 128), 128), :]
    second = ref[pl.ds(pl.multiple_of(128 - off, 128), 128), :]
    return jnp.concatenate([first, second], axis=0)


def low_lanes(shape):
    return lax.broadcasted_iota(jnp.int32, shape, 1) < 64


def swap64(v):
    return pltpu.roll(v, 64, 1)


def turn(v, c, s1, s2, sign):
    return v * c + sign * (pltpu.roll(v, 120, 1) * s1 + pltpu.roll(v, 8, 1) * s2)


def dp_shift(dp):
    return 2 * lax.rem(dp, 2) + dp // 2


def role(dp, me):
    y, z, part = me // 8, lax.rem(me // 2, 4), lax.rem(me, 2)
    q = lax.rem(z - y - dp_shift(dp) + 12, 4)
    return y, z, part, q


def pre_kernel(scal, tok, cot, again, abias, mgain, mbias, wqkv, bqkv, wout, c_ref, s1_ref, s2_ref,
               long_o, short_o, ha_o, hm_o):
    off = scal[0]
    x = halves(tok, off).astype(F32)
    dy = halves(cot, off)
    center = x - jnp.mean(x, axis=-1, keepdims=True)
    spread = jnp.mean(center * center, axis=-1, keepdims=True)
    z = center * lax.rsqrt(spread + EPS)
    ha = (z * again[...].astype(F32) + abias[...].astype(F32)).astype(BF)
    ha_o[...] = ha
    hm_o[...] = (z * mgain[...].astype(F32) + mbias[...].astype(F32)).astype(BF)
    cosine, s1, s2 = c_ref[...], s1_ref[...], s2_ref[...]
    low = low_lanes((256, 128))

    def put(head, kv, qg):
        long_o[2 * head, 0:128, :] = kv[0:128]
        long_o[2 * head + 1, 0:128, :] = kv[0:128]
        long_o[2 * head, 128:192, :] = qg[0:64]
        long_o[2 * head + 1, 128:192, :] = qg[64:128]
        pair, kind = head // 3, head % 3
        if kind == 1:
            for part in range(2):
                short_o[2 * pair + part, 256:384, :] = kv[128:256]
                short_o[2 * pair + part, 384:448, :] = qg[128 + 64 * part : 192 + 64 * part]
        else:
            slot = 2 * pair + kind // 2
            short_o[slot, 0:128, :] = kv[128:256]
            short_o[slot, 128:256, :] = qg[128:256]

    for wide in range(3):
        cols = slice(256 * wide, 256 * wide + 256)
        q2 = mm(ha, wqkv[:, cols]) + bqkv[:, cols].astype(F32)
        k2 = mm(ha, wqkv[:, 768 + 256 * wide : 1024 + 256 * wide])
        k2 = k2 + bqkv[:, 768 + 256 * wide : 1024 + 256 * wide].astype(F32)
        v2 = mm(ha, wqkv[:, 1536 + 256 * wide : 1792 + 256 * wide])
        v2 = v2 + bqkv[:, 1536 + 256 * wide : 1792 + 256 * wide].astype(F32)
        g2 = mm_nt(dy, wout[cols, :])
        for b in range(2):
            lanes = slice(128 * b, 128 * b + 128)
            q = turn(q2[:, lanes], cosine, s1, s2, 1.0).astype(BF).astype(F32) * 0.125
            k = turn(k2[:, lanes], cosine, s1, s2, 1.0)
            v, g = v2[:, lanes], g2[:, lanes]
            head = 4 * wide + 2 * b
            put(head, jnp.where(low, k, swap64(v)).astype(BF), jnp.where(low, q, swap64(g)).astype(BF))
            put(head + 1, jnp.where(low, swap64(k), v).astype(BF), jnp.where(low, swap64(q), g).astype(BF))


def vm(n):
    return [pl.BlockSpec(memory_space=pltpu.VMEM)] * n


def sm():
    return pl.BlockSpec(memory_space=pltpu.SMEM)


def pre_call(*args):
    return pl.pallas_call(
        pre_kernel,
        out_shape=(
            jax.ShapeDtypeStruct((24, LROWS, 128), BF),
            jax.ShapeDtypeStruct((8, SROWS, 128), BF),
            jax.ShapeDtypeStruct((256, D), BF),
            jax.ShapeDtypeStruct((256, D), BF),
        ),
        in_specs=[sm()] + vm(12),
        out_specs=vm(4),
        compiler_params=pltpu.CompilerParams(vmem_limit_bytes=48 << 20),
    )(*args)


def group_barrier(dp, me):
    bar = pltpu.get_barrier_semaphore()

    @pl.loop(1, 32)
    def _(i):
        pl.semaphore_signal(bar, inc=1, device_id=(dp, lax.rem(me + i, 32)), device_id_type=MESH)

    pl.semaphore_wait(bar, 31)


def walk(y, z, part, i):
    y2 = lax.rem(y + i // 8, 4)
    z2 = lax.rem(z + lax.rem(i // 2, 4), 4)
    p2 = lax.rem(part + lax.rem(i, 2), 2)
    return y2, z2, p2, y2 * 8 + z2 * 2 + p2


def out_kernel(l_ref, s_ref, lrx, srx, send_sem, recv_sem):
    dp, me = lax.axis_index("dp"), lax.axis_index("blk")
    shift = dp_shift(dp)
    group_barrier(dp, me)
    y, z, part, mine = role(dp, me)

    def copies(i, run):
        y2, z2, p2, d = walk(y, z, part, i)
        q = lax.rem(z2 - y2 - shift + 12, 4)

        @pl.when(q == 3)
        def _():
            run(s_ref.at[y2 * 2 + p2], srx.at[me], recv_sem.at[1], d)

        @pl.when(q != 3)
        def _():
            run(l_ref.at[(y2 * 3 + q) * 2 + p2], lrx.at[me], recv_sem.at[0], d)

    def remote(i, src, dst, sem, d):
        return pltpu.make_async_remote_copy(
            src, dst, send_sem.at[i], sem, device_id=(dp, d), device_id_type=MESH
        )

    copies(0, lambda src, dst, sem, d: pltpu.make_async_copy(src, dst, sem).start())

    @pl.loop(1, 32)
    def _(i):
        copies(i, lambda src, dst, sem, d: remote(i, src, dst, sem, d).start())

    @pl.when(mine == 3)
    def _():
        pltpu.make_async_copy(srx, srx, recv_sem.at[1]).wait()

    @pl.when(mine != 3)
    def _():
        pltpu.make_async_copy(lrx, lrx, recv_sem.at[0]).wait()

    @pl.loop(1, 32)
    def _(i):
        copies(i, lambda src, dst, sem, d: remote(i, src, dst, sem, d).wait_send())


def back_kernel(l_ref, s_ref, lrx, srx, send_sem, recv_sem):
    dp, me = lax.axis_index("dp"), lax.axis_index("blk")
    group_barrier(dp, me)
    y, z, part, mine = role(dp, me)

    def copies(i, run):
        y2, z2, p2, d = walk(y, z, part, i)

        @pl.when(mine == 3)
        def _():
            run(s_ref.at[d], srx.at[y * 2 + part], recv_sem.at[1], d)

        @pl.when(mine != 3)
        def _():
            run(l_ref.at[d], lrx.at[(y * 3 + mine) * 2 + part], recv_sem.at[0], d)

    def remote(i, src, dst, sem, d):
        return pltpu.make_async_remote_copy(
            src, dst, send_sem.at[i], sem, device_id=(dp, d), device_id_type=MESH
        )

    copies(0, lambda src, dst, sem, d: pltpu.make_async_copy(src, dst, sem).start())

    @pl.loop(1, 32)
    def _(i):
        copies(i, lambda src, dst, sem, d: remote(i, src, dst, sem, d).start())

    pltpu.make_async_copy(srx, srx, recv_sem.at[1]).wait()
    pltpu.make_async_copy(lrx, lrx, recv_sem.at[0]).wait()

    @pl.loop(1, 32)
    def _(i):
        copies(i, lambda src, dst, sem, d: remote(i, src, dst, sem, d).wait_send())


def exchange(kernel, cid, shapes, long_in, short_in):
    return pl.pallas_call(
        kernel,
        out_shape=tuple(jax.ShapeDtypeStruct(s, BF) for s in shapes),
        in_specs=vm(2),
        out_specs=vm(2),
        scratch_shapes=[pltpu.SemaphoreType.DMA((32,)), pltpu.SemaphoreType.DMA((2,))],
        compiler_params=pltpu.CompilerParams(
            collective_id=cid, has_side_effects=True, vmem_limit_bytes=40 << 20
        ),
    )(long_in, short_in)


def attend_kernel(scal, lrx, srx, starts_full, starts_half, ltx, stx, kv, kvt, qg, qo, dkv, sc):
    part = scal[2]
    lowq = low_lanes((256, 128))

    def fold(v, op):
        return op(v.reshape(v.shape[0] // 8, 8, v.shape[1]), axis=0)

    def load_tile(row):
        tile = qg[pl.ds(pl.multiple_of(row, 256), 256), :]
        zero = jnp.zeros_like(tile)
        gt = tile.astype(F32).T[64:128]
        return jnp.where(lowq, tile, zero), jnp.where(lowq, zero, tile), gt

    def store_tile(row, dqt, ot):
        both = jnp.concatenate([dqt * 0.125, ot], axis=0)
        qo[pl.ds(pl.multiple_of(row, 256), 256), :] = both.T.astype(BF)

    def key_rows(start, n):
        return lax.broadcasted_iota(jnp.int32, (n, 256), 0) + start

    def strided_places(t):
        col = lax.broadcasted_iota(jnp.int32, (1, 256), 1)
        return (4 * t + col // 64) * 128 + 64 * part + lax.rem(col, 64)

    def flip_all():
        @pl.loop(0, 32)
        def _(i):
            rows = pl.ds(pl.multiple_of(i * 128, 128), 128)
            kvt[:, rows] = kv[rows, :].astype(F32).T.astype(BF)

    @pl.when(scal[1] == 0)
    def _():
        @pl.loop(0, 32)
        def _(i):
            src = scal[8 + i]
            kv[pl.ds(pl.multiple_of(i * 128, 128), 128), :] = lrx[src, 0:128, :]
            qg[pl.ds(pl.multiple_of(i * 64, 64), 64), :] = lrx[src, 128:192, :]

        flip_all()
        dkv[...] = jnp.zeros_like(dkv)

        @pl.loop(0, 8)
        def _(t):
            qz, zg, gt = load_tile(t * 256)

            def chunk(c):
                return pl.ds(pl.multiple_of(c * 512, 512), 512)

            def score(c, m8):
                s = mm_nt(kv[chunk(c), :], qz)
                sc[chunk(c), :] = s
                return jnp.maximum(m8, fold(s, jnp.max))

            m8 = lax.fori_loop(0, t, score, jnp.full((8, 256), NEG, F32))
            s = mm_nt(kv[chunk(t), :], qz)
            s = jnp.where(key_rows(t * 512, 512) <= strided_places(t), s, NEG)
            sc[chunk(t), :] = s
            m8 = jnp.maximum(m8, fold(s, jnp.max))
            m = jnp.max(m8, axis=0, keepdims=True)

            def weigh(c, carry):
                l8, ot = carry
                p = jnp.exp(sc[chunk(c), :] - m)
                return l8 + fold(p, jnp.sum), ot + mm(kvt[64:128, chunk(c)], p.astype(BF))

            l8, ot = lax.fori_loop(
                0, t + 1, weigh, (jnp.zeros((8, 256), F32), jnp.zeros((64, 256), F32))
            )
            total = jnp.sum(l8, axis=0, keepdims=True)
            ot = ot * (1.0 / total)
            lse = m + jnp.log(total)
            delta = jnp.sum(gt * ot, axis=0, keepdims=True)

            def grads(c, dqt):
                p = jnp.exp(sc[chunk(c), :] - lse)
                ds = (p * (mm_nt(kv[chunk(c), :], zg) - delta)).astype(BF)
                dkv[chunk(c), :] += mm(ds, qz) + mm(p.astype(BF), zg)
                return dqt + mm(kvt[0:64, chunk(c)], ds)

            dqt = lax.fori_loop(0, t + 1, grads, jnp.zeros((64, 256), F32))
            store_tile(t * 256, dqt, ot)

        @pl.loop(0, 32)
        def _(i):
            rel = scal[40 + i]
            ltx[i, 0:128, :] = dkv[pl.ds(pl.multiple_of(rel * 128, 128), 128), :].astype(BF)
            ltx[i, 128:192, :] = qo[pl.ds(pl.multiple_of(rel * 64, 64), 64), :]

    def short_tile(row, start, n, places, begin):
        qz, zg, gt = load_tile(row)
        keys = pl.ds(pl.multiple_of(start, 256), n)
        k = kv[keys, :]
        place = key_rows(start, n)
        s = jnp.where((place <= places) & (place >= begin), mm_nt(k, qz), NEG)
        m = jnp.max(fold(s, jnp.max), axis=0, keepdims=True)
        e = jnp.exp(s - m)
        inv = 1.0 / jnp.sum(fold(e, jnp.sum), axis=0, keepdims=True)
        p = e * inv
        pb = p.astype(BF)
        ot = mm(kvt[64:128, keys], pb)
        delta = jnp.sum(gt * ot, axis=0, keepdims=True)
        ds = (p * (mm_nt(k, zg) - delta)).astype(BF)
        dkv[keys, :] += mm(ds, qz) + mm(pb, zg)
        dqt = mm(kvt[0:64, keys], ds)
        store_tile(row, dqt, ot)

    @pl.when(scal[1] == 1)
    def _():
        @pl.loop(0, 32)
        def _(i):
            src = scal[8 + 31 - i]
            kv[pl.ds(pl.multiple_of(i * 128, 128), 128), :] = srx[src, 0:128, :]
            qg[pl.ds(pl.multiple_of(i * 128, 128), 128), :] = srx[src, 128:256, :]

        flip_all()
        dkv[...] = jnp.zeros_like(dkv)

        @pl.loop(0, 16)
        def _(t):
            places = lax.broadcasted_iota(jnp.int32, (1, 256), 1) + 256 * t
            short_tile(t * 256, jnp.maximum(256 * t - 512, 0), 768, places, starts_full[pl.ds(t, 1), :])

        @pl.loop(0, 32)
        def _(i):
            rel = 31 - scal[40 + i]
            rows = pl.ds(pl.multiple_of(rel * 128, 128), 128)
            stx[i, 0:128, :] = dkv[rows, :].astype(BF)
            stx[i, 128:256, :] = qo[rows, :]

        @pl.loop(0, 32)
        def _(i):
            src = scal[8 + 31 - i]
            kv[pl.ds(pl.multiple_of(i * 128, 128), 128), :] = srx[src, 256:384, :]
            qg[pl.ds(pl.multiple_of(i * 64, 64), 64), :] = srx[src, 384:448, :]

        flip_all()
        dkv[...] = jnp.zeros_like(dkv)

        @pl.loop(0, 8)
        def _(t):
            short_tile(
                t * 256, jnp.maximum(512 * t - 512, 0), 1024, strided_places(t), starts_half[pl.ds(t, 1), :]
            )

        @pl.loop(0, 32)
        def _(i):
            rel = 31 - scal[40 + i]
            stx[i, 256:384, :] = dkv[pl.ds(pl.multiple_of(rel * 128, 128), 128), :].astype(BF)
            stx[i, 384:448, :] = qo[pl.ds(pl.multiple_of(rel * 64, 64), 64), :]


def attend_call(scal, lrx, srx, starts_full, starts_half):
    return pl.pallas_call(
        attend_kernel,
        out_shape=(
            jax.ShapeDtypeStruct((32, LROWS, 128), BF),
            jax.ShapeDtypeStruct((32, SROWS, 128), BF),
        ),
        in_specs=[sm()] + vm(4),
        out_specs=vm(2),
        scratch_shapes=[
            pltpu.VMEM((HALF, 128), BF),
            pltpu.VMEM((128, HALF), BF),
            pltpu.VMEM((HALF, 128), BF),
            pltpu.VMEM((HALF, 128), BF),
            pltpu.VMEM((HALF, 128), F32),
            pltpu.VMEM((HALF, 256), F32),
        ],
        compiler_params=pltpu.CompilerParams(vmem_limit_bytes=48 << 20),
    )(scal, lrx, srx, starts_full, starts_half)


def gelu_both(u):
    phi = 0.5 * (1.0 + lax.erf(u * (1.0 / math.sqrt(2.0))))
    density = jnp.exp(-0.5 * u * u) * (1.0 / math.sqrt(2.0 * math.pi))
    return u * phi, phi + u * density


def mlp_kernel(scal, hm, cot, up, upb, down, downb, grads_o, dh_o, branch_o, ub_o, hmt, dy):
    i = pl.program_id(0)

    @pl.when(i == 0)
    def _():
        hmt[...] = hm[...].astype(F32).T.astype(BF)
        dy[...] = halves(cot, scal[0])
        dh_o[...] = jnp.zeros_like(dh_o)
        branch_o[...] = jnp.broadcast_to(downb[...].astype(F32), branch_o.shape)

    u = mm(hm[...], up[...]) + upb[...].astype(F32)
    value, slope = gelu_both(u)
    hid = value.astype(BF)
    branch_o[...] += mm(hid, down[...])
    gu = mm_nt(dy[...], down[...]) * slope
    gub = gu.astype(BF)
    sums = jnp.sum(gub.astype(F32), axis=0, keepdims=True)
    for c in range(4):
        ub_o[pl.ds(4 * i + c, 1), :] = sums[:, 128 * c : 128 * c + 128]
    dh_o[...] += mm_nt(gub, up[...])
    gup = mm(hmt[...], gub).astype(BF)
    for c in range(4):
        grads_o[768 * c : 768 * c + 768, :] = gup[:, 128 * c : 128 * c + 128]
    gdown = mm_tn(hid, dy[...]).astype(BF)
    for c in range(6):
        grads_o[3072 + 512 * c : 3584 + 512 * c, :] = gdown[:, 128 * c : 128 * c + 128]


def mlp_call(scal, hm, cot, up, upb, down, downb):
    whole = lambda shape: pl.BlockSpec(shape, lambda i: (0, 0))
    return pl.pallas_call(
        mlp_kernel,
        grid=(6,),
        out_shape=(
            jax.ShapeDtypeStruct((36864, 128), BF),
            jax.ShapeDtypeStruct((256, D), F32),
            jax.ShapeDtypeStruct((256, D), F32),
            jax.ShapeDtypeStruct((24, 128), F32),
        ),
        in_specs=[
            sm(),
            whole((256, D)),
            whole((256, D)),
            pl.BlockSpec((D, 512), lambda i: (0, i)),
            pl.BlockSpec((1, 512), lambda i: (0, i)),
            pl.BlockSpec((512, D), lambda i: (i, 0)),
            whole((1, D)),
        ],
        out_specs=[
            pl.BlockSpec((6144, 128), lambda i: (i, 0)),
            whole((256, D)),
            whole((256, D)),
            whole((24, 128)),
        ],
        scratch_shapes=[pltpu.VMEM((D, 256), BF), pltpu.VMEM((256, D), BF)],
        compiler_params=pltpu.CompilerParams(vmem_limit_bytes=48 << 20),
    )(scal, hm, cot, up, upb, down, downb)


def post_kernel(scal, tok, cot, ha, again, mgain, wqkv, wout, outb, c_ref, s1_ref, s2_ref, lret, sret,
                dmlp, mlp, ub, mixed_o, tgrad_o, grads_o, small_o, gqkv, att):
    off = scal[0]
    cosine, s1, s2 = c_ref[...], s1_ref[...], s2_ref[...]
    low = low_lanes((256, 128))

    def f(v):
        return v.astype(F32)

    def gather(head):
        pair, kind = head // 3, head % 3
        kv_l = f(lret[2 * head, 0:128, :]) + f(lret[2 * head + 1, 0:128, :])
        qo_l = [f(lret[2 * head, 128:192, :]), f(lret[2 * head + 1, 128:192, :])]
        if kind == 1:
            kv_s = f(sret[2 * pair, 256:384, :]) + f(sret[2 * pair + 1, 256:384, :])
            qo_s = [f(sret[2 * pair, 384:448, :]), f(sret[2 * pair + 1, 384:448, :])]
        else:
            slot = 2 * pair + kind // 2
            kv_s = f(sret[slot, 0:128, :])
            qo_s = [f(sret[slot, 128:256, :])]
        return jnp.concatenate([kv_l, kv_s], axis=0), jnp.concatenate(qo_l + qo_s, axis=0)

    for j in range(6):
        kv_a, qo_a = gather(2 * j)
        kv_b, qo_b = gather(2 * j + 1)
        dq = jnp.where(low, qo_a, swap64(qo_b))
        ov = jnp.where(low, swap64(qo_a), qo_b)
        dk = jnp.where(low, kv_a, swap64(kv_b))
        dv = jnp.where(low, swap64(kv_a), kv_b)
        cols = slice(128 * j, 128 * j + 128)
        att[:, cols] = ov.astype(BF)
        gqkv[:, cols] = turn(dq, cosine, s1, s2, -1.0).astype(BF)
        gqkv[:, 768 + 128 * j : 896 + 128 * j] = turn(dk, cosine, s1, s2, -1.0).astype(BF)
        gqkv[:, 1536 + 128 * j : 1664 + 128 * j] = dv.astype(BF)

    x = f(halves(tok, off))
    dy_b = halves(cot, off)
    dy = f(dy_b)
    attn = mm(att[...], wout[...]) + f(outb[...])
    y = x + attn + mlp[...]
    mixed = y.astype(BF)
    first = pl.ds(pl.multiple_of(off, 128), 128)
    second = pl.ds(pl.multiple_of(128 - off, 128), 128)
    mixed_o[first, :] = mixed[0:128]
    mixed_o[second, :] = mixed[128:256]

    def rows(v, at, n):
        for c in range(n):
            small_o[at + c : at + c + 1, :] = v[:, 128 * c : 128 * c + 128]

    def square(v, at):
        s = jnp.sum(v * v, axis=0, keepdims=True)
        t = s[:, 0:128]
        for c in range(1, 6):
            t = t + s[:, 128 * c : 128 * c + 128]
        small_o[at : at + 1, :] = t

    small_o[72:80, :] = jnp.zeros((8, 128), F32)
    square(y, 72)
    square(attn, 73)
    square(mlp[...], 74)
    rows(jnp.sum(dy, axis=0, keepdims=True), 42, 6)
    small_o[48:72, :] = ub[...]

    attT = f(att[...]).T.astype(BF)
    haT = f(ha[...]).T.astype(BF)
    for w in range(3):
        t = mm(attT, dy_b[:, 256 * w : 256 * w + 256]).astype(BF)
        for b in range(2):
            grads_o[768 * (18 + 2 * w + b) : 768 * (19 + 2 * w + b), :] = t[:, 128 * b : 128 * b + 128]
    d_attn = jnp.zeros((256, D), F32)
    for w in range(9):
        cols = slice(256 * w, 256 * w + 256)
        part = gqkv[:, cols]
        rows(jnp.sum(f(part), axis=0, keepdims=True), 24 + 2 * w, 2)
        t = mm(haT, part).astype(BF)
        for b in range(2):
            grads_o[768 * (2 * w + b) : 768 * (2 * w + b + 1), :] = t[:, 128 * b : 128 * b + 128]
        d_attn = d_attn + mm_nt(part, wqkv[:, cols])

    center = x - jnp.mean(x, axis=-1, keepdims=True)
    r = lax.rsqrt(jnp.mean(center * center, axis=-1, keepdims=True) + EPS)
    z = center * r

    def norm_back(d, gain, at):
        rows(jnp.sum(d * z, axis=0, keepdims=True), at, 6)
        rows(jnp.sum(d, axis=0, keepdims=True), at + 6, 6)
        e = d * f(gain[...])
        return r * (
            e - jnp.mean(e, axis=-1, keepdims=True) - z * jnp.mean(e * z, axis=-1, keepdims=True)
        )

    total = dy + norm_back(d_attn, again, 0) + norm_back(dmlp[...], mgain, 12)
    tgrad_o[first, :] = total[0:128]
    tgrad_o[second, :] = total[128:256]


def post_call(*args):
    return pl.pallas_call(
        post_kernel,
        out_shape=(
            jax.ShapeDtypeStruct((256, D), BF),
            jax.ShapeDtypeStruct((256, D), F32),
            jax.ShapeDtypeStruct((18432, 128), BF),
            jax.ShapeDtypeStruct((SMALL, 128), F32),
        ),
        in_specs=[sm()] + vm(16),
        out_specs=vm(4),
        scratch_shapes=[pltpu.VMEM((256, 3 * D), BF), pltpu.VMEM((256, D), BF)],
        compiler_params=pltpu.CompilerParams(vmem_limit_bytes=56 << 20),
    )(*args)


def place_id(core, x, y, z):
    return (lax.rem(x, 2) * 2 + core, y * 8 + z * 2 + x // 2)


def cube_partners():
    dp, blk = lax.axis_index("dp"), lax.axis_index("blk")
    core = lax.rem(dp, 2)
    at = {"x": lax.rem(blk, 2) * 2 + dp // 2, "y": blk // 8, "z": lax.rem(blk // 2, 4)}
    out = []
    for axis in ("x", "y", "z"):
        v = at[axis]
        hi, lo = v // 2, lax.rem(v, 2)
        for nv, bit in ((v + 1 - 2 * lo, lax.rem(hi + lo, 2)), (3 - v, hi)):
            there = dict(at)
            there[axis] = nv
            out.append((place_id(core, there["x"], there["y"], there["z"]), bit))
    return core, place_id(1 - core, at["x"], at["y"], at["z"]), out


def sum_kernel(rows, steps, f_ref, s_ref, a_ref, so_ref, rx0, *rest):
    rxs, rxe, srx = rest[:steps], rest[steps], rest[steps + 1]
    (core_s, core_r, rs_s, rs_r, ex_s, ex_r, ag_s, ag_r, fin_s, fin_r, sm_s, sm_r, loc) = rest[steps + 2 :]
    part, half_rows = rows // 12, rows // 2
    core, other, partners = cube_partners()
    bar = pltpu.get_barrier_semaphore()
    for d in [other] + [q[0] for q in partners]:
        pl.semaphore_signal(bar, inc=1, device_id=d, device_id_type=MESH)
    pl.semaphore_wait(bar, 7)

    def remote(src, dst, ss, rs, d):
        return pltpu.make_async_remote_copy(src, dst, ss, rs, device_id=d, device_id_type=MESH)

    base = [pl.multiple_of(core * half_rows + p * part, 16) for p in range(6)]
    obase = [pl.multiple_of((1 - core) * half_rows + p * part, 16) for p in range(6)]

    def add(off, n, src):
        w = 96
        while n % w:
            w //= 2

        @pl.loop(0, n // w)
        def _(i):
            here = pl.ds(pl.multiple_of(off + i * w, 16), w)
            there = pl.ds(pl.multiple_of(i * w, 16), w)
            f_ref[here, :] = (f_ref[here, :].astype(F32) + src[there, :].astype(F32)).astype(BF)

    small_to = [other] + [q[0] for q in partners]
    so_ref[...] = s_ref[...]

    def small_copy(t):
        return remote(so_ref, srx.at[t], sm_s.at[t], sm_r.at[t], small_to[t])

    def small_finish(t):
        small_copy(t).wait()
        so_ref[...] += srx[t]

    pend = [
        remote(f_ref.at[pl.ds(obase[p], part)], rx0.at[p], core_s.at[p], core_r.at[p], other)
        for p in range(6)
    ]
    small_copy(0).start()
    for p in range(6):
        pend[p].start()
    offs, size = list(base), part
    for t in range(steps):
        h = size // 2
        for p in range(6):
            pend[p].wait_recv()
            add(offs[p], size, (rx0 if t == 0 else rxs[t - 1]).at[p])
            dev, bit = partners[(p + t) % 6]
            out = pl.multiple_of(offs[p] + (1 - bit) * h, 16)
            c = remote(f_ref.at[pl.ds(out, h)], rxs[t].at[p], rs_s.at[t, p], rs_r.at[t, p], dev)
            c.start()
            pend[p].wait_send()
            pend[p] = c
            offs[p] = pl.multiple_of(offs[p] + bit * h, 16)
        small_finish(t)
        small_copy(t + 1).start()
        size = h
    both = []
    for p in range(6):
        pend[p].wait_recv()
        add(offs[p], size, rxs[steps - 1].at[p])
        c = remote(
            f_ref.at[pl.ds(offs[p], size)], rxe.at[p], ex_s.at[p], ex_r.at[p], partners[(p + steps) % 6][0]
        )
        c.start()
        pend[p].wait_send()
        both.append(c)
    small_finish(steps)
    small_copy(steps + 1).start()
    own = []
    for p in range(6):
        both[p].wait()
        add(offs[p], size, rxe.at[p])
        here = pl.ds(offs[p], size)
        c = pltpu.make_async_copy(f_ref.at[here], a_ref.at[here], loc.at[p])
        c.start()
        own.append(c)
    for p in range(6):
        own[p].wait()
    prev = [None] * 6
    for t in reversed(range(steps)):
        for p in range(6):
            if prev[p] is not None:
                prev[p].wait()
            dev, bit = partners[(p + t) % 6]
            here = pl.ds(offs[p], size)
            prev[p] = remote(a_ref.at[here], a_ref.at[here], ag_s.at[t, p], ag_r.at[t, p], dev)
            prev[p].start()
            offs[p] = pl.multiple_of(offs[p] - bit * size, 16)
        size *= 2
    last = []
    for p in range(6):
        prev[p].wait()
        here = pl.ds(base[p], part)
        c = remote(a_ref.at[here], a_ref.at[here], fin_s.at[p], fin_r.at[p], other)
        c.start()
        last.append(c)
    small_finish(steps + 1)
    for p in range(6):
        last[p].wait()


def sum_call(f, s, cid):
    rows, steps = f.shape[0], 5
    part = rows // 12
    dma = pltpu.SemaphoreType.DMA
    return pl.pallas_call(
        functools.partial(sum_kernel, rows, steps),
        out_shape=(jax.ShapeDtypeStruct(f.shape, BF), jax.ShapeDtypeStruct(s.shape, F32)),
        in_specs=vm(2),
        out_specs=[pl.BlockSpec(memory_space=pl.ANY)] + vm(1),
        scratch_shapes=[pltpu.VMEM((6, part, 128), BF)]
        + [pltpu.VMEM((6, part >> (t + 1), 128), BF) for t in range(steps)]
        + [pltpu.VMEM((6, part >> steps, 128), BF), pltpu.VMEM((7,) + s.shape, F32)]
        + [dma((6,)), dma((6,)), dma((steps, 6)), dma((steps, 6)), dma((6,)), dma((6,))]
        + [dma((steps, 6)), dma((steps, 6)), dma((6,)), dma((6,)), dma((7,)), dma((7,)), dma((6,))],
        compiler_params=pltpu.CompilerParams(
            collective_id=cid, has_side_effects=True, vmem_limit_bytes=56 << 20
        ),
    )(f, s)


def unpack_mlp_kernel(a, up_o, down_o):
    for c in range(4):
        up_o[:, 128 * c : 128 * c + 128] = a[768 * c : 768 * c + 768, :].astype(F32)
    for c in range(6):
        down_o[:, 128 * c : 128 * c + 128] = a[3072 + 512 * c : 3584 + 512 * c, :].astype(F32)


def unpack_mlp(a):
    return pl.pallas_call(
        unpack_mlp_kernel,
        grid=(6,),
        out_shape=(jax.ShapeDtypeStruct((D, FF), F32), jax.ShapeDtypeStruct((FF, D), F32)),
        in_specs=[pl.BlockSpec((6144, 128), lambda i: (i, 0))],
        out_specs=[pl.BlockSpec((D, 512), lambda i: (0, i)), pl.BlockSpec((512, D), lambda i: (i, 0))],
        compiler_params=pltpu.CompilerParams(vmem_limit_bytes=48 << 20),
    )(a)


def unpack_attn_kernel(a, b, qkv_o, out_o):
    for c in range(6):
        qkv_o[:, 128 * c : 128 * c + 128] = a[768 * c : 768 * c + 768, :].astype(F32)
    for c in range(2):
        out_o[:, 128 * c : 128 * c + 128] = b[768 * c : 768 * c + 768, :].astype(F32)


def unpack_attn(a):
    return pl.pallas_call(
        unpack_attn_kernel,
        grid=(3,),
        out_shape=(jax.ShapeDtypeStruct((D, 3 * D), F32), jax.ShapeDtypeStruct((D, D), F32)),
        in_specs=[
            pl.BlockSpec((4608, 128), lambda i: (i, 0)),
            pl.BlockSpec((1536, 128), lambda i: (9 + i, 0)),
        ],
        out_specs=[pl.BlockSpec((D, 768), lambda i: (0, i)), pl.BlockSpec((D, 256), lambda i: (0, i))],
        compiler_params=pltpu.CompilerParams(vmem_limit_bytes=48 << 20),
    )(a, a)


def on_device(tokens, attn_gain, attn_bias, mlp_gain, mlp_bias, qkv_weight, qkv_bias, out_weight, out_bias,
              up_weight, up_bias, down_weight, down_bias, cotangent, doc_lengths, span_order):
    dp, me = lax.axis_index("dp"), lax.axis_index("blk")
    y, z, part, q = role(dp, me)
    lengths, order = doc_lengths[0], span_order[0]
    first_long = lengths[0] > 512
    spans = order.reshape(SPANS, 2)[:, 0]
    long_span = jnp.where(first_long, spans, 31 - spans)
    index = jnp.arange(SPANS, dtype=jnp.int32)
    source = jnp.sum(jnp.where(long_span[None, :] == index[:, None], index[None, :], 0), axis=1)
    mine = jnp.sum(jnp.where(index == me, long_span, 0))
    head = jnp.stack(
        [jnp.where(first_long, 0, 128), jnp.where(q == 3, 1, 0), part, mine, mine, mine, mine, mine]
    )
    scal = jnp.concatenate([head, source, long_span]).astype(jnp.int32)

    ends = jnp.cumsum(jnp.where(first_long, lengths[1:], lengths[:-1])).astype(jnp.int32)

    def begin_of(place):
        return jnp.max(jnp.where(ends[:, None] <= place[None, :], ends[:, None], 0), axis=0)

    starts = begin_of(jnp.arange(HALF, dtype=jnp.int32))
    starts_full = starts.reshape(16, 256)
    pieces = starts.reshape(32, 2, 64)
    starts_half = jnp.where(part == 0, pieces[:, 0], pieces[:, 1]).reshape(8, 256)

    lane = jnp.arange(128, dtype=jnp.int32)
    row = jnp.arange(128, dtype=jnp.int32)
    short_place = (31 - mine) * 128 + row
    position = jnp.concatenate([mine * 128 + row, short_place - begin_of(short_place)])
    inverse = jnp.exp((lane % 8).astype(F32) * (-2.0 * math.log(10000.0) / ROT))
    angle = position.astype(F32)[:, None] * inverse[None, :]
    dim = (lane % 64)[None, :]
    sine = jnp.sin(angle)
    c_tab = jnp.where(dim < ROT, jnp.cos(angle), 1.0)
    s1_tab = jnp.where(dim < ROT // 2, -sine, 0.0)
    s2_tab = jnp.where((dim >= ROT // 2) & (dim < ROT), sine, 0.0)

    line = lambda v: v.reshape(1, -1)
    again, abias, mgain, mbias = line(attn_gain), line(attn_bias), line(mlp_gain), line(mlp_bias)
    long_tx, short_tx, ha, hm = pre_call(
        scal, tokens, cotangent, again, abias, mgain, mbias, qkv_weight, line(qkv_bias), out_weight,
        c_tab, s1_tab, s2_tab,
    )
    long_rx, short_rx = exchange(out_kernel, 0, ((32, LROWS, 128), (32, SROWS, 128)), long_tx, short_tx)
    mlp_grads, dmlp, mlp_branch, ub = mlp_call(
        scal, hm, cotangent, up_weight, line(up_bias), down_weight, line(down_bias)
    )
    long_back, short_back = attend_call(scal, long_rx, short_rx, starts_full, starts_half)
    long_ret, short_ret = exchange(
        back_kernel, 1, ((24, LROWS, 128), (8, SROWS, 128)), long_back, short_back
    )
    mixed, tokens_grad, attn_grads, small = post_call(
        scal, tokens, cotangent, ha, again, mgain, qkv_weight, out_weight, line(out_bias), c_tab, s1_tab, s2_tab,
        long_ret, short_ret, dmlp, mlp_branch, ub,
    )
    mlp_sum, unused = sum_call(mlp_grads, jnp.zeros((8, 128), F32), 2)
    attn_sum, small_sum = sum_call(attn_grads, small, 3)
    grad_up, grad_down = unpack_mlp(mlp_sum)
    grad_qkv, grad_out = unpack_attn(attn_sum)

    def vector(at, n):
        return small_sum[at : at + n].reshape(128 * n)

    roots = jnp.sqrt(jnp.sum(small_sum[72:75], axis=1) / (D * 256 * 128))
    branch_bias = vector(42, 6)
    return (
        mixed, tokens_grad, vector(0, 6), vector(6, 6), vector(12, 6), vector(18, 6), grad_qkv, vector(24, 18),
        grad_out, branch_bias, grad_up, vector(48, 24), grad_down, branch_bias, roots[0], roots[1], roots[2],
    )


def solution(mesh):
    rows, split = P(("dp", "blk"), None), P("dp", None)
    return jax.shard_map(
        on_device,
        mesh=mesh,
        in_specs=(rows,) + (P(),) * 12 + (rows, split, split),
        out_specs=(rows, rows) + (P(),) * 15,
        check_vma=False,
    )
```

```python
import math

import jax
import jax.numpy as jnp
from jax import lax
from jax.experimental import pallas as pl
from jax.experimental.pallas import tpu as pltpu
from jax.sharding import PartitionSpec as P


D = 768
HEADS = 12
ROT = 16
FF = 3072
HALF = 4096
SPANS = 32
LROWS = 192
SROWS = 448
EPS = 1e-05
NEG = -1e30
SMALL = 80
STEPS = 5
BF = jnp.bfloat16
F32 = jnp.float32
MESH = pl.DeviceIdType.MESH
NT = (((1,), (1,)), ((), ()))
TN = (((0,), (0,)), ((), ()))


def mm(a, b):
    return jnp.dot(a, b, preferred_element_type=F32)


def mm_nt(a, b):
    return lax.dot_general(a, b, NT, preferred_element_type=F32)


def mm_tn(a, b):
    return lax.dot_general(a, b, TN, preferred_element_type=F32)


def halves(ref, first_long):
    top, bottom = ref[0:128, :], ref[128:256, :]
    return jnp.concatenate(
        [jnp.where(first_long, top, bottom), jnp.where(first_long, bottom, top)], axis=0
    )


def low_lanes(shape):
    return lax.broadcasted_iota(jnp.int32, shape, 1) < 64


def swap64(v):
    return pltpu.roll(v, 64, 1)


def turn(v, c, s1, s2, sign):
    return v * c + sign * (pltpu.roll(v, 120, 1) * s1 + pltpu.roll(v, 8, 1) * s2)


def role(dp, me):
    shift = 2 * lax.rem(dp, 2) + dp // 2
    y, z, part = me // 8, lax.rem(me // 2, 4), lax.rem(me, 2)
    return y, z, part, shift, lax.rem(z - y - shift + 12, 4)


def walk(y, z, part, i):
    y2 = lax.rem(y + i // 8, 4)
    z2 = lax.rem(z + lax.rem(i // 2, 4), 4)
    p2 = lax.rem(part + lax.rem(i, 2), 2)
    return y2, z2, p2, y2 * 8 + z2 * 2 + p2


def place_id(core, x, y, z):
    return (lax.rem(x, 2) * 2 + core, y * 8 + z * 2 + x // 2)


def cube_partners(dp, blk):
    core = lax.rem(dp, 2)
    at = {"x": lax.rem(blk, 2) * 2 + dp // 2, "y": blk // 8, "z": lax.rem(blk // 2, 4)}
    out = []
    for axis in ("x", "y", "z"):
        v = at[axis]
        hi, lo = v // 2, lax.rem(v, 2)
        for nv, bit in ((v + 1 - 2 * lo, lax.rem(hi + lo, 2)), (3 - v, hi)):
            there = dict(at)
            there[axis] = nv
            out.append((place_id(core, there["x"], there["y"], there["z"]), bit))
    return core, place_id(1 - core, at["x"], at["y"], at["z"]), out


def remote(src, dst, send, recv, d):
    return pltpu.make_async_remote_copy(src, dst, send, recv, device_id=d, device_id_type=MESH)


def sum_stages(rows, cube, f_ref, a_ref, rx0, rxs, rxe, sems, small):
    core_s, core_r, rs_s, rs_r, ex_s, ex_r, ag_s, ag_r, fin_s, fin_r, loc = sems
    part, half_rows, steps = rows // 12, rows // 2, STEPS
    core, other, partners = cube
    base = [pl.multiple_of(core * half_rows + p * part, 16) for p in range(6)]
    obase = [pl.multiple_of((1 - core) * half_rows + p * part, 16) for p in range(6)]

    def add(off, n, src):
        w = 96
        while n % w:
            w //= 2

        @pl.loop(0, n // w)
        def _(i):
            here = pl.ds(pl.multiple_of(off + i * w, 16), w)
            there = pl.ds(pl.multiple_of(i * w, 16), w)
            f_ref[here, :] = (f_ref[here, :].astype(F32) + src[there, :].astype(F32)).astype(BF)

    if small is not None:
        so_ref, srx, sm_s, sm_r = small
        to = [other] + [q[0] for q in partners]

        def small_copy(t):
            return remote(so_ref, srx.at[t], sm_s.at[t], sm_r.at[t], to[t])

    def small_start(t):
        if small is not None:
            small_copy(t).start()

    def small_next(t):
        if small is not None:
            small_copy(t).wait()
            so_ref[...] += srx[t]
            if t < 6:
                small_copy(t + 1).start()

    def landing(ref, p, n):
        return ref.at[p, pl.ds(0, n)]

    pend = [
        remote(f_ref.at[pl.ds(obase[p], part)], landing(rx0, p, part), core_s.at[p], core_r.at[p], other)
        for p in range(6)
    ]
    small_start(0)
    for p in range(6):
        pend[p].start()
    yield
    offs, size = list(base), part
    for t in range(steps):
        h = size // 2
        for p in range(6):
            pend[p].wait_recv()
            add(offs[p], size, (rx0 if t == 0 else rxs[t - 1]).at[p])
            dev, bit = partners[(p + t) % 6]
            out = pl.multiple_of(offs[p] + (1 - bit) * h, 16)
            c = remote(f_ref.at[pl.ds(out, h)], landing(rxs[t], p, h), rs_s.at[t, p], rs_r.at[t, p], dev)
            c.start()
            pend[p].wait_send()
            pend[p] = c
            offs[p] = pl.multiple_of(offs[p] + bit * h, 16)
        small_next(t)
        size = h
        yield
    both = []
    for p in range(6):
        pend[p].wait_recv()
        add(offs[p], size, rxs[steps - 1].at[p])
        here = f_ref.at[pl.ds(offs[p], size)]
        c = remote(here, landing(rxe, p, size), ex_s.at[p], ex_r.at[p], partners[(p + steps) % 6][0])
        c.start()
        pend[p].wait_send()
        both.append(c)
    small_next(steps)
    yield
    own = []
    for p in range(6):
        both[p].wait()
        add(offs[p], size, rxe.at[p])
        here = pl.ds(offs[p], size)
        c = pltpu.make_async_copy(f_ref.at[here], a_ref.at[here], loc.at[p])
        c.start()
        own.append(c)
    for p in range(6):
        own[p].wait()
    prev = [None] * 6
    for t in reversed(range(steps)):
        for p in range(6):
            if prev[p] is not None:
                prev[p].wait()
            dev, bit = partners[(p + t) % 6]
            here = a_ref.at[pl.ds(offs[p], size)]
            prev[p] = remote(here, here, ag_s.at[t, p], ag_r.at[t, p], dev)
            prev[p].start()
            offs[p] = pl.multiple_of(offs[p] - bit * size, 16)
        size *= 2
        yield
    last = []
    for p in range(6):
        prev[p].wait()
        here = a_ref.at[pl.ds(base[p], part)]
        c = remote(here, here, fin_s.at[p], fin_r.at[p], other)
        c.start()
        last.append(c)
    small_next(6)
    yield
    for p in range(6):
        last[p].wait()
    yield


def sine_cosine(angle):
    k = jnp.floor(angle * (2.0 / math.pi) + 0.5)
    r = angle - k * 1.5703125 - k * 4.837512969970703125e-4 - k * 7.54978995489188216e-8
    r2 = r * r
    s = r + r * r2 * (-1.6666654611e-1 + r2 * (8.3321608736e-3 - r2 * 1.9515295891e-4))
    c = 1.0 - 0.5 * r2 + r2 * r2 * (4.166664568298827e-2 + r2 * (-1.388731625493765e-3 + r2 * 2.443315711809948e-5))
    q = k - 4.0 * jnp.floor(k * 0.25)
    odd = (q == 1.0) | (q == 3.0)
    sine = jnp.where(odd, c, s)
    cosine = jnp.where(odd, s, c)
    return jnp.where(q >= 2.0, -sine, sine), jnp.where((q == 1.0) | (q == 2.0), -cosine, cosine)


def gelu_both(u):
    phi = 0.5 * (1.0 + lax.erf(u * (1.0 / math.sqrt(2.0))))
    density = jnp.exp(-0.5 * u * u) * (1.0 / math.sqrt(2.0 * math.pi))
    return u * phi, phi + u * density


def layer_kernel(
    source, order, lens, tok, cot, again, abias, mgain, mbias, bqkv, outb, upb, downb, wqkv_h, wout_h, up_h, down_h,
    mixed_o, tgrad_o, small_o, a_mlp, a_attn,
    wqkv, wout, up, down, tx_l, tx_s, rx_l, rx_s, ret_l, ret_s, ha_r, hm_r, hmt, tabs, branch, dh, ub, grads,
    kv, kvt, qg, qo, dkv, sc, gqkv, att, rx0, rxa, rxb, rxc, rxd, rxf, rxe, srx,
    wq_sem, wo_sem, up_sem, dn_sem, e1_s, e1_r, e2_s, e2_r, sm_s, sm_r, *sum_sems,
):
    dp, me = lax.axis_index("dp"), lax.axis_index("blk")
    y, z, part, shift, mine = role(dp, me)
    is_short, is_long = mine == 3, mine != 3
    cube = cube_partners(dp, me)
    sems_m, sems_a = sum_sems[:11], sum_sems[11:]
    rxs = [rxa, rxb, rxc, rxd, rxf]

    def f(v):
        return v.astype(F32)

    bar = pltpu.get_barrier_semaphore()

    @pl.loop(1, 32)
    def _(i):
        pl.semaphore_signal(bar, inc=1, device_id=(dp, lax.rem(me + i, 32)), device_id_type=MESH)

    for d in [cube[1], cube[2][0][0], cube[2][1][0]]:
        pl.semaphore_signal(bar, inc=1, device_id=d, device_id_type=MESH)

    def qkv_copy(c):
        cols = pl.ds(256 * c, 256)
        return pltpu.make_async_copy(wqkv_h.at[:, cols], wqkv.at[:, cols], wq_sem.at[c])

    out_copy = pltpu.make_async_copy(wout_h, wout, wo_sem)

    def ff_copies(i, slot):
        cols = pl.ds(pl.multiple_of(512 * i, 512), 512)
        return (
            pltpu.make_async_copy(up_h.at[:, cols], up.at[slot], up_sem.at[slot]),
            pltpu.make_async_copy(down_h.at[cols, :], down.at[slot], dn_sem.at[slot]),
        )

    for wide in range(3):
        for kind in range(3):
            qkv_copy(3 * kind + wide).start()
    out_copy.start()
    for i in range(3):
        for c in ff_copies(i, i):
            c.start()

    first_long = lens[0, 0] > 512

    def span_of(i):
        a = order[0, 2 * i]
        return jnp.where(first_long, a, 31 - a)

    def begin_of(place):
        end = jnp.int32(0)
        begin = jnp.zeros_like(place)
        for j in range(15):
            end = end + jnp.where(first_long, lens[0, j + 1], lens[0, j])
            begin = jnp.maximum(begin, jnp.where(end <= place, end, 0))
        return begin

    own_span = span_of(me)
    row = lax.broadcasted_iota(jnp.int32, (128, 128), 0)
    lane = lax.broadcasted_iota(jnp.int32, (256, 128), 1)
    short_place = (31 - own_span) * 128 + row
    position = jnp.concatenate([own_span * 128 + row, short_place - begin_of(short_place)], axis=0)
    dim = lax.rem(lane, 64)
    step = lax.rem(lane, 8)
    inverse = jnp.full((256, 128), 1.0, F32)
    for j in range(1, 8):
        inverse = jnp.where(step == j, 10000.0 ** (-2.0 * j / ROT), inverse)
    sine, cosine = sine_cosine(f(position) * inverse)
    tabs[0] = jnp.where(dim < ROT, cosine, 1.0)
    tabs[1] = jnp.where(dim < ROT // 2, -sine, 0.0)
    tabs[2] = jnp.where((dim >= ROT // 2) & (dim < ROT), sine, 0.0)
    low = lane < 64

    def norm_parts():
        x = f(halves(tok, first_long))
        center = x - jnp.mean(x, axis=-1, keepdims=True)
        r = lax.rsqrt(jnp.mean(center * center, axis=-1, keepdims=True) + EPS)
        return x, center * r, r

    unused_x, znorm, unused_r = norm_parts()
    ha_r[...] = (znorm * f(again[...]) + f(abias[...])).astype(BF)
    hm_r[...] = (znorm * f(mgain[...]) + f(mbias[...])).astype(BF)
    dyb = halves(cot, first_long)
    ha = ha_r[...]

    def put(head, kvb, qgb):
        tx_l[2 * head, 0:128, :] = kvb[0:128]
        tx_l[2 * head + 1, 0:128, :] = kvb[0:128]
        tx_l[2 * head, 128:192, :] = qgb[0:64]
        tx_l[2 * head + 1, 128:192, :] = qgb[64:128]
        pair, kind = head // 3, head % 3
        if kind == 1:
            for p in range(2):
                tx_s[2 * pair + p, 256:384, :] = kvb[128:256]
                tx_s[2 * pair + p, 384:448, :] = qgb[128 + 64 * p : 192 + 64 * p]
        else:
            slot = 2 * pair + kind // 2
            tx_s[slot, 0:128, :] = kvb[128:256]
            tx_s[slot, 128:256, :] = qgb[128:256]

    for wide in range(3):
        for kind in range(3):
            qkv_copy(3 * kind + wide).wait()
        if wide == 0:
            out_copy.wait()
        q2, k2, v2 = [
            mm(ha, wqkv[:, 768 * kind + 256 * wide : 768 * kind + 256 * wide + 256])
            + f(bqkv[:, 768 * kind + 256 * wide : 768 * kind + 256 * wide + 256])
            for kind in range(3)
        ]
        g2 = mm_nt(dyb, wout[256 * wide : 256 * wide + 256, :])
        for b in range(2):
            lanes = slice(128 * b, 128 * b + 128)
            q = f(turn(q2[:, lanes], tabs[0], tabs[1], tabs[2], 1.0).astype(BF)) * 0.125
            k = turn(k2[:, lanes], tabs[0], tabs[1], tabs[2], 1.0)
            v, g = v2[:, lanes], g2[:, lanes]
            head = 4 * wide + 2 * b
            put(head, jnp.where(low, k, swap64(v)).astype(BF), jnp.where(low, q, swap64(g)).astype(BF))
            put(head + 1, jnp.where(low, swap64(k), v).astype(BF), jnp.where(low, swap64(q), g).astype(BF))

    pl.semaphore_wait(bar, 34)

    def there(i, run):
        y2, z2, p2, d = walk(y, z, part, i)
        q = lax.rem(z2 - y2 - shift + 12, 4)

        @pl.when(q == 3)
        def _():
            run(tx_s.at[y2 * 2 + p2], rx_s.at[me], e1_r.at[1], d)

        @pl.when(q != 3)
        def _():
            run(tx_l.at[(y2 * 3 + q) * 2 + p2], rx_l.at[me], e1_r.at[0], d)

    there(0, lambda src, dst, sem, d: pltpu.make_async_copy(src, dst, sem).start())

    @pl.loop(1, 32)
    def _(i):
        there(i, lambda src, dst, sem, d: remote(src, dst, e1_s.at[i], sem, (dp, d)).start())

    hmt[...] = f(hm_r[...]).T.astype(BF)
    dh[...] = jnp.zeros_like(dh)
    branch[...] = jnp.broadcast_to(f(downb[...]), branch.shape)

    @pl.loop(0, 6)
    def _(i):
        slot = lax.rem(i, 3)
        for c in ff_copies(i, slot):
            c.wait()
        u = mm(hm_r[...], up[slot]) + f(upb[:, pl.ds(pl.multiple_of(512 * i, 512), 512)])
        value, slope = gelu_both(u)
        hid = value.astype(BF)
        branch[...] += mm(hid, down[slot])
        gub = (mm_nt(halves(cot, first_long), down[slot]) * slope).astype(BF)
        sums = jnp.sum(f(gub), axis=0, keepdims=True)
        for c in range(4):
            ub[pl.ds(4 * i + c, 1), :] = sums[:, 128 * c : 128 * c + 128]
        dh[...] += mm_nt(gub, up[slot])
        gup = mm(hmt[...], gub).astype(BF)
        at = pl.multiple_of(6144 * i, 512)
        for c in range(4):
            grads[pl.ds(at + 768 * c, 768), :] = gup[:, 128 * c : 128 * c + 128]
        gdown = mm_tn(hid, halves(cot, first_long)).astype(BF)
        for c in range(6):
            grads[pl.ds(at + 3072 + 512 * c, 512), :] = gdown[:, 128 * c : 128 * c + 128]

        @pl.when(i < 3)
        def _():
            for c in ff_copies(i + 3, slot):
                c.start()

    sum_mlp = sum_stages(36864, cube, grads, a_mlp, rx0, rxs, rxe, sems_m, None)
    next(sum_mlp)

    def fold(v, op):
        return op(v.reshape(v.shape[0] // 8, 8, v.shape[1]), axis=0)

    lowq = low_lanes((256, 128))

    def load_tile(at):
        tile = qg[pl.ds(pl.multiple_of(at, 256), 256), :]
        zero = jnp.zeros_like(tile)
        gt = f(tile).T[64:128]
        return jnp.where(lowq, tile, zero), jnp.where(lowq, zero, tile), gt

    def store_tile(at, dqt, ot):
        both = jnp.concatenate([dqt * 0.125, ot], axis=0)
        qo[pl.ds(at // 64, 4)] = both.T.astype(BF).reshape(4, 64, 128)

    def key_rows(start, n):
        return lax.broadcasted_iota(jnp.int32, (n, 256), 0) + start

    def strided_places(t):
        col = lax.broadcasted_iota(jnp.int32, (1, 256), 1)
        return (4 * t + col // 64) * 128 + 64 * part + lax.rem(col, 64)

    def get_keys(ref, at, rows, flip):
        @pl.loop(0, 32)
        def _(i):
            src = source[31 - i] if flip else source[i]
            kv[pl.ds(pl.multiple_of(i * 128, 128), 128), :] = ref[src, at : at + 128, :]
            qg[pl.ds(pl.multiple_of(i * rows, rows), rows), :] = ref[src, at + 128 : at + 128 + rows, :]

        @pl.loop(0, 32)
        def _(i):
            block = pl.ds(pl.multiple_of(i * 128, 128), 128)
            kvt[:, block] = f(kv[block, :]).T.astype(BF)

        dkv[...] = jnp.zeros_like(dkv)

    def put_back(ref, at, rows, flip):
        @pl.loop(0, 32)
        def _(i):
            rel = 31 - span_of(i) if flip else span_of(i)
            ref[i, at : at + 128, :] = dkv[rel].astype(BF)
            if rows == 64:
                ref[i, at + 128 : at + 192, :] = qo[rel]
            else:
                ref[i, at + 128 : at + 192, :] = qo[2 * rel]
                ref[i, at + 192 : at + 256, :] = qo[2 * rel + 1]

    def long_tile(t):
        qz, zg, gt = load_tile(t * 256)

        def chunk(c):
            return pl.ds(pl.multiple_of(c * 512, 512), 512)

        def score(c, m8):
            s = mm_nt(kv[chunk(c), :], qz)
            sc[chunk(c), :] = s
            return jnp.maximum(m8, fold(s, jnp.max))

        m8 = lax.fori_loop(0, t, score, jnp.full((8, 256), NEG, F32))
        s = mm_nt(kv[chunk(t), :], qz)
        s = jnp.where(key_rows(t * 512, 512) <= strided_places(t), s, NEG)
        sc[chunk(t), :] = s
        m8 = jnp.maximum(m8, fold(s, jnp.max))
        m = jnp.max(m8, axis=0, keepdims=True)

        def weigh(c, carry):
            l8, ot = carry
            p = jnp.exp(sc[chunk(c), :] - m)
            return l8 + fold(p, jnp.sum), ot + mm(kvt[64:128, chunk(c)], p.astype(BF))

        l8, ot = lax.fori_loop(
            0, t + 1, weigh, (jnp.zeros((8, 256), F32), jnp.zeros((64, 256), F32))
        )
        total = jnp.sum(l8, axis=0, keepdims=True)
        ot = ot * (1.0 / total)
        lse = m + jnp.log(total)
        delta = jnp.sum(gt * ot, axis=0, keepdims=True)

        def back(c, dqt):
            p = jnp.exp(sc[chunk(c), :] - lse)
            ds = (p * (mm_nt(kv[chunk(c), :], zg) - delta)).astype(BF)
            dkv[pl.ds(4 * c, 4)] += (mm(ds, qz) + mm(p.astype(BF), zg)).reshape(4, 128, 128)
            return dqt + mm(kvt[0:64, chunk(c)], ds)

        dqt = lax.fori_loop(0, t + 1, back, jnp.zeros((64, 256), F32))
        store_tile(t * 256, dqt, ot)

    def short_tile(at, start, n, places):
        qz, zg, gt = load_tile(at)
        keys = pl.ds(pl.multiple_of(start, 256), n)
        k = kv[keys, :]
        place = key_rows(start, n)
        s = jnp.where((place <= places) & (place >= begin_of(places)), mm_nt(k, qz), NEG)
        m = jnp.max(fold(s, jnp.max), axis=0, keepdims=True)
        e = jnp.exp(s - m)
        inv = 1.0 / jnp.sum(fold(e, jnp.sum), axis=0, keepdims=True)
        p = e * inv
        pb = p.astype(BF)
        ot = mm(kvt[64:128, keys], pb)
        delta = jnp.sum(gt * ot, axis=0, keepdims=True)
        ds = (p * (mm_nt(k, zg) - delta)).astype(BF)
        dkv[pl.ds(start // 128, n // 128)] += (mm(ds, qz) + mm(pb, zg)).reshape(n // 128, 128, 128)
        dqt = mm(kvt[0:64, keys], ds)
        store_tile(at, dqt, ot)

    def full_tile(t):
        places = lax.broadcasted_iota(jnp.int32, (1, 256), 1) + 256 * t
        short_tile(t * 256, 256 * (t - 2) * ((t + 14) // 16), 768, places)

    def half_tile(t):
        short_tile(t * 256, 512 * (t - 1) * ((t + 7) // 8), 1024, strided_places(t))

    def tiles(lo, hi, body):
        pl.loop(lo, hi)(body)

    long_at = [0, 3, 5, 6, 7, 8]
    short_at = [0, 5, 10, 16]
    half_at = [0, 4, 8]
    for slot in range(5):
        @pl.when(is_long)
        def _():
            if slot == 0:
                pltpu.make_async_copy(rx_l, rx_l, e1_r.at[0]).wait()
                get_keys(rx_l, 0, 64, False)
            tiles(long_at[slot], long_at[slot + 1], long_tile)
            if slot == 4:
                put_back(rx_l, 0, 64, False)

        @pl.when(is_short)
        def _():
            if slot == 0:
                pltpu.make_async_copy(rx_s, rx_s, e1_r.at[1]).wait()
                get_keys(rx_s, 0, 128, True)
            if slot < 3:
                tiles(short_at[slot], short_at[slot + 1], full_tile)
                if slot == 2:
                    put_back(rx_s, 0, 128, True)
                    get_keys(rx_s, 256, 64, True)
            else:
                tiles(half_at[slot - 3], half_at[slot - 2], half_tile)
                if slot == 4:
                    put_back(rx_s, 256, 64, True)

        next(sum_mlp)

    def home(i, run):
        d = walk(y, z, part, i)[3]

        @pl.when(is_short)
        def _():
            run(rx_s.at[d], ret_s.at[y * 2 + part], e2_r.at[1], d)

        @pl.when(is_long)
        def _():
            run(rx_l.at[d], ret_l.at[(y * 3 + mine) * 2 + part], e2_r.at[0], d)

    home(0, lambda src, dst, sem, d: pltpu.make_async_copy(src, dst, sem).start())

    @pl.loop(1, 32)
    def _(i):
        home(i, lambda src, dst, sem, d: remote(src, dst, e2_s.at[i], sem, (dp, d)).start())

    for unused in sum_mlp:
        pass
    pltpu.make_async_copy(ret_s, ret_s, e2_r.at[1]).wait()
    pltpu.make_async_copy(ret_l, ret_l, e2_r.at[0]).wait()

    def gather(head):
        pair, kind = head // 3, head % 3
        kv_l = f(ret_l[2 * head, 0:128, :]) + f(ret_l[2 * head + 1, 0:128, :])
        qo_l = [f(ret_l[2 * head, 128:192, :]), f(ret_l[2 * head + 1, 128:192, :])]
        if kind == 1:
            kv_s = f(ret_s[2 * pair, 256:384, :]) + f(ret_s[2 * pair + 1, 256:384, :])
            qo_s = [f(ret_s[2 * pair, 384:448, :]), f(ret_s[2 * pair + 1, 384:448, :])]
        else:
            slot = 2 * pair + kind // 2
            kv_s = f(ret_s[slot, 0:128, :])
            qo_s = [f(ret_s[slot, 128:256, :])]
        return jnp.concatenate([kv_l, kv_s], axis=0), jnp.concatenate(qo_l + qo_s, axis=0)

    for j in range(6):
        kv_a, qo_a = gather(2 * j)
        kv_b, qo_b = gather(2 * j + 1)
        dq = jnp.where(low, qo_a, swap64(qo_b))
        ov = jnp.where(low, swap64(qo_a), qo_b)
        dk = jnp.where(low, kv_a, swap64(kv_b))
        dv = jnp.where(low, swap64(kv_a), kv_b)
        cols = slice(128 * j, 128 * j + 128)
        att[:, cols] = ov.astype(BF)
        gqkv[:, cols] = turn(dq, tabs[0], tabs[1], tabs[2], -1.0).astype(BF)
        gqkv[:, 768 + 128 * j : 896 + 128 * j] = turn(dk, tabs[0], tabs[1], tabs[2], -1.0).astype(BF)
        gqkv[:, 1536 + 128 * j : 1664 + 128 * j] = dv.astype(BF)

    def rows(v, at, n):
        for c in range(n):
            small_o[at + c : at + c + 1, :] = v[:, 128 * c : 128 * c + 128]

    def square(v, at):
        s = jnp.sum(v * v, axis=0, keepdims=True)
        t = s[:, 0:128]
        for c in range(1, 6):
            t = t + s[:, 128 * c : 128 * c + 128]
        small_o[at : at + 1, :] = t

    def put_rows(ref, v):
        ref[0:128, :] = jnp.where(first_long, v[0:128], v[128:256])
        ref[128:256, :] = jnp.where(first_long, v[128:256], v[0:128])

    attT = f(att[...]).T.astype(BF)
    haT = f(ha_r[...]).T.astype(BF)
    dy_b = halves(cot, first_long)
    for w in range(3):
        t = mm(attT, dy_b[:, 256 * w : 256 * w + 256]).astype(BF)
        for b in range(2):
            grads[768 * (18 + 2 * w + b) : 768 * (19 + 2 * w + b), :] = t[:, 128 * b : 128 * b + 128]
    d_attn = jnp.zeros((256, D), F32)
    for w in range(9):
        cols = slice(256 * w, 256 * w + 256)
        piece = gqkv[:, cols]
        rows(jnp.sum(f(piece), axis=0, keepdims=True), 24 + 2 * w, 2)
        t = mm(haT, piece).astype(BF)
        for b in range(2):
            grads[768 * (2 * w + b) : 768 * (2 * w + b + 1), :] = t[:, 128 * b : 128 * b + 128]
        d_attn = d_attn + mm_nt(piece, wqkv[:, cols])

    x, znorm, r = norm_parts()
    dy = f(dy_b)
    attn = mm(att[...], wout[...]) + f(outb[...])
    out = x + attn + branch[...]
    put_rows(mixed_o, out.astype(BF))
    small_o[72:80, :] = jnp.zeros((8, 128), F32)
    square(out, 72)
    square(attn, 73)
    square(branch[...], 74)
    rows(jnp.sum(dy, axis=0, keepdims=True), 42, 6)
    small_o[48:72, :] = ub[...]

    def norm_back(d, gain, at):
        rows(jnp.sum(d * znorm, axis=0, keepdims=True), at, 6)
        rows(jnp.sum(d, axis=0, keepdims=True), at + 6, 6)
        e = d * f(gain[...])
        return r * (
            e - jnp.mean(e, axis=-1, keepdims=True) - znorm * jnp.mean(e * znorm, axis=-1, keepdims=True)
        )

    put_rows(tgrad_o, dy + norm_back(d_attn, again, 0) + norm_back(dh[...], mgain, 12))

    for unused in sum_stages(
        18432, cube, grads, a_attn, rx0, rxs, rxe, sems_a, (small_o, srx, sm_s, sm_r)
    ):
        pass

    @pl.loop(1, 32)
    def _(i):
        there(i, lambda src, dst, sem, d: remote(src, dst, e1_s.at[i], sem, (dp, d)).wait_send())
        home(i, lambda src, dst, sem, d: remote(src, dst, e2_s.at[i], sem, (dp, d)).wait_send())


def layer_call(*args):
    def vm(n):
        return [pl.BlockSpec(memory_space=pltpu.VMEM)] * n

    def vb(*shape):
        return pltpu.VMEM(shape, BF)

    def vf(*shape):
        return pltpu.VMEM(shape, F32)

    dma = pltpu.SemaphoreType.DMA
    sum_sems = [dma((6,)), dma((6,)), dma((STEPS, 6)), dma((STEPS, 6)), dma((6,)), dma((6,))]
    sum_sems += [dma((STEPS, 6)), dma((STEPS, 6)), dma((6,)), dma((6,)), dma((6,))]
    anywhere = pl.BlockSpec(memory_space=pl.ANY)
    return pl.pallas_call(
        layer_kernel,
        out_shape=(
            jax.ShapeDtypeStruct((256, D), BF),
            jax.ShapeDtypeStruct((256, D), F32),
            jax.ShapeDtypeStruct((SMALL, 128), F32),
            jax.ShapeDtypeStruct((36864, 128), BF),
            jax.ShapeDtypeStruct((18432, 128), BF),
        ),
        in_specs=[pl.BlockSpec(memory_space=pltpu.SMEM)] * 3 + vm(10) + [anywhere] * 4,
        out_specs=vm(3) + [anywhere] * 2,
        scratch_shapes=[
            vb(D, 3 * D), vb(D, D), vb(3, D, 512), vb(3, 512, D),
            vb(24, LROWS, 128), vb(8, SROWS, 128), vb(32, LROWS, 128), vb(32, SROWS, 128),
            vb(24, LROWS, 128), vb(8, SROWS, 128),
            vb(256, D), vb(256, D), vb(D, 256), vf(3, 256, 128), vf(256, D), vf(256, D), vf(24, 128),
            vb(36864, 128),
            vb(HALF, 128), vb(128, HALF), vb(HALF, 128), vb(64, 64, 128), vf(32, 128, 128), vf(HALF, 256),
            vb(256, 3 * D), vb(256, D),
            vb(6, 3072, 128),
        ]
        + [vb(6, 3072 >> (t + 1), 128) for t in range(STEPS)]
        + [vb(6, 3072 >> STEPS, 128), vf(7, SMALL, 128)]
        + [dma((9,)), dma, dma((3,)), dma((3,)), dma((32,)), dma((2,)), dma((32,)), dma((2,)), dma((7,)), dma((7,))]
        + sum_sems * 2,
        compiler_params=pltpu.CompilerParams(
            collective_id=0, has_side_effects=True, vmem_limit_bytes=62 << 20
        ),
    )(*args)


def unpack_mlp_kernel(a, up_o, down_o):
    for c in range(4):
        up_o[:, 128 * c : 128 * c + 128] = a[768 * c : 768 * c + 768, :].astype(F32)
    for c in range(6):
        down_o[:, 128 * c : 128 * c + 128] = a[3072 + 512 * c : 3584 + 512 * c, :].astype(F32)


def unpack_mlp(a):
    return pl.pallas_call(
        unpack_mlp_kernel,
        grid=(6,),
        out_shape=(jax.ShapeDtypeStruct((D, FF), F32), jax.ShapeDtypeStruct((FF, D), F32)),
        in_specs=[pl.BlockSpec((6144, 128), lambda i: (i, 0))],
        out_specs=[pl.BlockSpec((D, 512), lambda i: (0, i)), pl.BlockSpec((512, D), lambda i: (i, 0))],
        compiler_params=pltpu.CompilerParams(vmem_limit_bytes=48 << 20),
    )(a)


def unpack_attn_kernel(a, b, qkv_o, out_o):
    for c in range(6):
        qkv_o[:, 128 * c : 128 * c + 128] = a[768 * c : 768 * c + 768, :].astype(F32)
    for c in range(2):
        out_o[:, 128 * c : 128 * c + 128] = b[768 * c : 768 * c + 768, :].astype(F32)


def unpack_attn(a):
    return pl.pallas_call(
        unpack_attn_kernel,
        grid=(3,),
        out_shape=(jax.ShapeDtypeStruct((D, 3 * D), F32), jax.ShapeDtypeStruct((D, D), F32)),
        in_specs=[
            pl.BlockSpec((4608, 128), lambda i: (i, 0)),
            pl.BlockSpec((1536, 128), lambda i: (9 + i, 0)),
        ],
        out_specs=[pl.BlockSpec((D, 768), lambda i: (0, i)), pl.BlockSpec((D, 256), lambda i: (0, i))],
        compiler_params=pltpu.CompilerParams(vmem_limit_bytes=48 << 20),
    )(a, a)


def on_device(tokens, attn_gain, attn_bias, mlp_gain, mlp_bias, qkv_weight, qkv_bias, out_weight, out_bias,
              up_weight, up_bias, down_weight, down_bias, cotangent, doc_lengths, span_order):
    first_long = doc_lengths[0, 0] > 512
    spans = span_order.reshape(SPANS, 2)[:, 0]
    long_span = jnp.where(first_long, spans, 31 - spans)
    index = jnp.arange(SPANS, dtype=jnp.int32)
    source = jnp.sum(jnp.where(long_span[None, :] == index[:, None], index[None, :], 0), axis=1)
    vectors = (attn_gain, attn_bias, mlp_gain, mlp_bias, qkv_bias, out_bias, up_bias, down_bias)
    mixed, tokens_grad, small_sum, mlp_sum, attn_sum = layer_call(
        source, span_order, doc_lengths, tokens, cotangent, *[v.reshape(1, -1) for v in vectors],
        qkv_weight, out_weight, up_weight, down_weight,
    )
    grad_up, grad_down = unpack_mlp(mlp_sum)
    grad_qkv, grad_out = unpack_attn(attn_sum)

    def vector(at, n):
        return small_sum[at : at + n].reshape(128 * n)

    roots = jnp.sqrt(jnp.sum(small_sum[72:75], axis=1) / (D * 256 * 128))
    branch_bias = vector(42, 6)
    return (
        mixed, tokens_grad, vector(0, 6), vector(6, 6), vector(12, 6), vector(18, 6), grad_qkv, vector(24, 18),
        grad_out, branch_bias, grad_up, vector(48, 24), grad_down, branch_bias, roots[0], roots[1], roots[2],
    )


def solution(mesh):
    rows, split = P(("dp", "blk"), None), P("dp", None)
    return jax.shard_map(
        on_device,
        mesh=mesh,
        in_specs=(rows,) + (P(),) * 12 + (rows, split, split),
        out_specs=(rows, rows) + (P(),) * 15,
        check_vma=False,
    )
```

```python
import math

import jax
import jax.numpy as jnp
from jax import lax
from jax.experimental import pallas as pl
from jax.experimental.pallas import tpu as pltpu
from jax.sharding import PartitionSpec as P


D = 768
HEADS = 12
ROT = 16
FF = 3072
HALF = 4096
SPANS = 32
EPS = 1e-05
NEG = -1e30
SMALL = 80
STEPS = 5
BF = jnp.bfloat16
F32 = jnp.float32
MESH = pl.DeviceIdType.MESH
NT = (((1,), (1,)), ((), ()))
TN = (((0,), (0,)), ((), ()))


def mm(a, b):
    return jnp.dot(a, b, preferred_element_type=F32)


def mm_nt(a, b):
    return lax.dot_general(a, b, NT, preferred_element_type=F32)


def mm_tn(a, b):
    return lax.dot_general(a, b, TN, preferred_element_type=F32)


def halves(ref, first_long):
    top, bottom = ref[0:128, :], ref[128:256, :]
    return jnp.concatenate(
        [jnp.where(first_long, top, bottom), jnp.where(first_long, bottom, top)], axis=0
    )


def line(ref):
    return ref[...].astype(F32).reshape(1, -1)


def low_lanes(shape):
    return lax.broadcasted_iota(jnp.int32, shape, 1) < 64


def swap64(v):
    return pltpu.roll(v, 64, 1)


def turn(v, c, s1, s2, sign):
    return v * c + sign * (pltpu.roll(v, 120, 1) * s1 + pltpu.roll(v, 8, 1) * s2)


def role(dp, me):
    shift = 2 * lax.rem(dp, 2) + dp // 2
    y, z, part = me // 8, lax.rem(me // 2, 4), lax.rem(me, 2)
    return y, z, part, shift, lax.rem(z - y - shift + 12, 4)


def walk(y, z, part, i):
    y2 = lax.rem(y + i // 8, 4)
    z2 = lax.rem(z + lax.rem(i // 2, 4), 4)
    p2 = lax.rem(part + lax.rem(i, 2), 2)
    return y2, z2, p2, y2 * 8 + z2 * 2 + p2


def place_id(core, x, y, z):
    return (lax.rem(x, 2) * 2 + core, y * 8 + z * 2 + x // 2)


def cube_partners(dp, blk):
    core = lax.rem(dp, 2)
    at = {"x": lax.rem(blk, 2) * 2 + dp // 2, "y": blk // 8, "z": lax.rem(blk // 2, 4)}
    out = []
    for axis in ("x", "y", "z"):
        v = at[axis]
        hi, lo = v // 2, lax.rem(v, 2)
        for nv, bit in ((v + 1 - 2 * lo, lax.rem(hi + lo, 2)), (3 - v, hi)):
            there = dict(at)
            there[axis] = nv
            out.append((place_id(core, there["x"], there["y"], there["z"]), bit))
    return core, place_id(1 - core, at["x"], at["y"], at["z"]), out


def remote(src, dst, send, recv, d):
    return pltpu.make_async_remote_copy(src, dst, send, recv, device_id=d, device_id_type=MESH)


def sum_stages(rows, cube, f_ref, a_ref, rx0, rxs, rxe, sems, small):
    core_s, core_r, rs_s, rs_r, ex_s, ex_r, ag_s, ag_r, fin_s, fin_r, loc = sems
    part, half_rows, steps = rows // 12, rows // 2, STEPS
    core, other, partners = cube
    base = [pl.multiple_of(core * half_rows + p * part, 16) for p in range(6)]
    obase = [pl.multiple_of((1 - core) * half_rows + p * part, 16) for p in range(6)]

    def add(off, n, src):
        w = 96
        while n % w:
            w //= 2

        @pl.loop(0, n // w)
        def _(i):
            here = pl.ds(pl.multiple_of(off + i * w, 16), w)
            there = pl.ds(pl.multiple_of(i * w, 16), w)
            f_ref[here, :] = (f_ref[here, :].astype(F32) + src[there, :].astype(F32)).astype(BF)

    if small is not None:
        so_ref, srx, sm_s, sm_r = small
        to = [other] + [q[0] for q in partners]

        def small_copy(t):
            return remote(so_ref, srx.at[t], sm_s.at[t], sm_r.at[t], to[t])

    def small_next(t):
        if small is not None:
            small_copy(t).wait()
            so_ref[...] += srx[t]
            if t < 6:
                small_copy(t + 1).start()

    def landing(ref, p, n):
        return ref.at[p, pl.ds(0, n)]

    pend = [
        remote(f_ref.at[pl.ds(obase[p], part)], landing(rx0, p, part), core_s.at[p], core_r.at[p], other)
        for p in range(6)
    ]
    for p in range(6):
        pend[p].start()
    yield
    if small is not None:
        small_copy(0).start()
    offs, size = list(base), part
    for t in range(steps):
        h = size // 2
        for p in range(6):
            pend[p].wait_recv()
            add(offs[p], size, (rx0 if t == 0 else rxs[t - 1]).at[p])
            dev, bit = partners[(p + t) % 6]
            out = pl.multiple_of(offs[p] + (1 - bit) * h, 16)
            c = remote(f_ref.at[pl.ds(out, h)], landing(rxs[t], p, h), rs_s.at[t, p], rs_r.at[t, p], dev)
            c.start()
            pend[p].wait_send()
            pend[p] = c
            offs[p] = pl.multiple_of(offs[p] + bit * h, 16)
        small_next(t)
        size = h
        yield
    both = []
    for p in range(6):
        pend[p].wait_recv()
        add(offs[p], size, rxs[steps - 1].at[p])
        here = f_ref.at[pl.ds(offs[p], size)]
        c = remote(here, landing(rxe, p, size), ex_s.at[p], ex_r.at[p], partners[(p + steps) % 6][0])
        c.start()
        pend[p].wait_send()
        both.append(c)
    small_next(steps)
    yield
    own = []
    for p in range(6):
        both[p].wait()
        add(offs[p], size, rxe.at[p])
        here = pl.ds(offs[p], size)
        c = pltpu.make_async_copy(f_ref.at[here], a_ref.at[here], loc.at[p])
        c.start()
        own.append(c)
    for p in range(6):
        own[p].wait()
    prev = [None] * 6
    for t in reversed(range(steps)):
        for p in range(6):
            if prev[p] is not None:
                prev[p].wait()
            dev, bit = partners[(p + t) % 6]
            here = a_ref.at[pl.ds(offs[p], size)]
            prev[p] = remote(here, here, ag_s.at[t, p], ag_r.at[t, p], dev)
            prev[p].start()
            offs[p] = pl.multiple_of(offs[p] - bit * size, 16)
        if t == steps - 1:
            small_next(6)
        size *= 2
        yield
    last = []
    for p in range(6):
        prev[p].wait()
        here = a_ref.at[pl.ds(base[p], part)]
        c = remote(here, here, fin_s.at[p], fin_r.at[p], other)
        c.start()
        last.append(c)
    yield
    for p in range(6):
        last[p].wait()
    yield


def sine_cosine(angle):
    k = jnp.floor(angle * (2.0 / math.pi) + 0.5)
    r = angle - k * 1.5703125 - k * 4.837512969970703125e-4 - k * 7.54978995489188216e-8
    r2 = r * r
    s = r + r * r2 * (-1.6666654611e-1 + r2 * (8.3321608736e-3 - r2 * 1.9515295891e-4))
    c = 1.0 - 0.5 * r2 + r2 * r2 * (4.166664568298827e-2 + r2 * (-1.388731625493765e-3 + r2 * 2.443315711809948e-5))
    q = k - 4.0 * jnp.floor(k * 0.25)
    odd = (q == 1.0) | (q == 3.0)
    sine = jnp.where(odd, c, s)
    cosine = jnp.where(odd, s, c)
    return jnp.where(q >= 2.0, -sine, sine), jnp.where((q == 1.0) | (q == 2.0), -cosine, cosine)


def gelu_both(u):
    phi = 0.5 * (1.0 + lax.erf(u * (1.0 / math.sqrt(2.0))))
    density = jnp.exp(-0.5 * u * u) * (1.0 / math.sqrt(2.0 * math.pi))
    return u * phi, phi + u * density


def layer_kernel(
    order, lens, tok, cot, again, abias, mgain, mbias, bqkv, outb, upb, downb, wqkv_h, wout_h, up_h, down_h,
    mixed_o, tgrad_o, small_o, a_mlp, a_attn,
    source, wqkv, wout, up, down, tx_l, tx_a, tx_b, rx_l, rx_a, rx_b, ret_l, ret_a, ret_b,
    ha_r, hm_r, hmt, tabs, branch, dh, zn, rn, ub, ubias, grads,
    kv, kvt, qg, qo, dkv, sc, gqkv, att, rx0, rx1, rxa, rxb, rxc, rxd, rxf, rxe, srx,
    wq_sem, wo_sem, up_sem, dn_sem, e1_s, e1b_s, e1_r, e2_s, e2a_s, e2_r, sm_s, sm_r, *sum_sems,
):
    dp, me = lax.axis_index("dp"), lax.axis_index("blk")
    y, z, part, shift, mine = role(dp, me)
    is_short, is_long = mine == 3, mine != 3
    cube = cube_partners(dp, me)
    sems_m, sems_a = sum_sems[:11], sum_sems[11:]
    rxs = [rxa, rxb, rxc, rxd, rxf]

    def f(v):
        return v.astype(F32)

    bar = pltpu.get_barrier_semaphore()

    @pl.loop(1, 32)
    def _(i):
        pl.semaphore_signal(bar, inc=1, device_id=(dp, lax.rem(me + i, 32)), device_id_type=MESH)

    for d in [cube[1], cube[2][0][0], cube[2][1][0]]:
        pl.semaphore_signal(bar, inc=1, device_id=d, device_id_type=MESH)

    def qkv_copy(c):
        cols = pl.ds(256 * c, 256)
        return pltpu.make_async_copy(wqkv_h.at[:, cols], wqkv.at[:, cols], wq_sem.at[c])

    out_copy = pltpu.make_async_copy(wout_h, wout, wo_sem)

    def ff_copies(i, slot):
        cols = pl.ds(pl.multiple_of(512 * i, 512), 512)
        return (
            pltpu.make_async_copy(up_h.at[:, cols], up.at[slot], up_sem.at[slot]),
            pltpu.make_async_copy(down_h.at[cols, :], down.at[slot], dn_sem.at[slot]),
        )

    for wide in range(3):
        for kind in range(3):
            qkv_copy(3 * kind + wide).start()
    out_copy.start()
    for i in range(3):
        for c in ff_copies(i, i):
            c.start()

    first_long = lens[0, 0] > 512

    def span_of(i):
        a = order[0, 2 * i]
        return jnp.where(first_long, a, 31 - a)

    def begin_of(place):
        end = jnp.int32(0)
        begin = jnp.zeros_like(place)
        for j in range(15):
            end = end + jnp.where(first_long, lens[0, j + 1], lens[0, j])
            begin = jnp.maximum(begin, jnp.where(end <= place, end, 0))
        return begin

    own_span = span_of(me)
    row = lax.broadcasted_iota(jnp.int32, (128, 128), 0)
    lane = lax.broadcasted_iota(jnp.int32, (256, 128), 1)
    short_place = (31 - own_span) * 128 + row
    position = jnp.concatenate([own_span * 128 + row, short_place - begin_of(short_place)], axis=0)
    dim = lax.rem(lane, 64)
    step = lax.rem(lane, 8)
    inverse = jnp.full((256, 128), 1.0, F32)
    for j in range(1, 8):
        inverse = jnp.where(step == j, 10000.0 ** (-2.0 * j / ROT), inverse)
    sine, cosine = sine_cosine(f(position) * inverse)
    tabs[0] = jnp.where(dim < ROT, cosine, 1.0)
    tabs[1] = jnp.where(dim < ROT // 2, -sine, 0.0)
    tabs[2] = jnp.where((dim >= ROT // 2) & (dim < ROT), sine, 0.0)
    low = lane < 64

    def norm_parts():
        x = f(halves(tok, first_long))
        center = x - jnp.mean(x, axis=-1, keepdims=True)
        r = lax.rsqrt(jnp.mean(center * center, axis=-1, keepdims=True) + EPS)
        return x, center * r, r

    unused_x, znorm, unused_r = norm_parts()
    ha_r[...] = (znorm * line(again) + line(abias)).astype(BF)
    hm_r[...] = (znorm * line(mgain) + line(mbias)).astype(BF)
    bq, bu = line(bqkv), line(upb)
    for i in range(6):
        ubias[i : i + 1, :] = bu[:, 512 * i : 512 * i + 512]
    dyb = halves(cot, first_long)
    ha = ha_r[...]

    def put(head, kvb, qgb):
        tx_l[2 * head, 0:128, :] = kvb[0:128]
        tx_l[2 * head + 1, 0:128, :] = kvb[0:128]
        tx_l[2 * head, 128:192, :] = qgb[0:64]
        tx_l[2 * head + 1, 128:192, :] = qgb[64:128]
        pair, kind = head // 3, head % 3
        if kind == 1:
            for p in range(2):
                tx_b[2 * pair + p, 0:128, :] = kvb[128:256]
                tx_b[2 * pair + p, 128:192, :] = qgb[128 + 64 * p : 192 + 64 * p]
        else:
            slot = 2 * pair + kind // 2
            tx_a[slot, 0:128, :] = kvb[128:256]
            tx_a[slot, 128:256, :] = qgb[128:256]

    for wide in range(3):
        for kind in range(3):
            qkv_copy(3 * kind + wide).wait()
        if wide == 0:
            out_copy.wait()
        q2, k2, v2 = [
            mm(ha, wqkv[:, 768 * kind + 256 * wide : 768 * kind + 256 * wide + 256])
            + bq[:, 768 * kind + 256 * wide : 768 * kind + 256 * wide + 256]
            for kind in range(3)
        ]
        g2 = mm_nt(dyb, wout[256 * wide : 256 * wide + 256, :])
        for b in range(2):
            lanes = slice(128 * b, 128 * b + 128)
            q = f(turn(q2[:, lanes], tabs[0], tabs[1], tabs[2], 1.0).astype(BF)) * 0.125
            k = turn(k2[:, lanes], tabs[0], tabs[1], tabs[2], 1.0)
            v, g = v2[:, lanes], g2[:, lanes]
            head = 4 * wide + 2 * b
            put(head, jnp.where(low, k, swap64(v)).astype(BF), jnp.where(low, q, swap64(g)).astype(BF))
            put(head + 1, jnp.where(low, swap64(k), v).astype(BF), jnp.where(low, swap64(q), g).astype(BF))

    pl.semaphore_wait(bar, 34)

    def there(i, run):
        y2, z2, p2, d = walk(y, z, part, i)
        q = lax.rem(z2 - y2 - shift + 12, 4)

        @pl.when(q == 3)
        def _():
            run(tx_a.at[y2 * 2 + p2], rx_a.at[me], e1_r.at[1], d)

        @pl.when(q != 3)
        def _():
            run(tx_l.at[(y2 * 3 + q) * 2 + p2], rx_l.at[me], e1_r.at[0], d)

    def there_half(i, run):
        y2, z2, p2, d = walk(y, z, part, i)
        q = lax.rem(z2 - y2 - shift + 12, 4)

        @pl.when(q == 3)
        def _():
            run(tx_b.at[y2 * 2 + p2], rx_b.at[me], e1_r.at[2], d)

    def local(src, dst, sem, d):
        pltpu.make_async_copy(src, dst, sem).start()

    def start_by(sems, i):
        return lambda src, dst, sem, d: remote(src, dst, sems.at[i], sem, (dp, d)).start()

    def end_by(sems, i):
        return lambda src, dst, sem, d: remote(src, dst, sems.at[i], sem, (dp, d)).wait_send()

    there(0, local)

    @pl.loop(1, 32)
    def _(i):
        there(i, start_by(e1_s, i))

    there_half(0, local)

    @pl.loop(1, 32)
    def _(i):
        there_half(i, start_by(e1b_s, i))

    hmt[...] = f(hm_r[...]).T.astype(BF)
    dh[...] = jnp.zeros_like(dh)
    branch[...] = jnp.broadcast_to(line(downb), branch.shape)

    @pl.loop(0, 6)
    def _(i):
        slot = lax.rem(i, 3)
        for c in ff_copies(i, slot):
            c.wait()
        u = mm(hm_r[...], up[slot]) + ubias[pl.ds(i, 1), :]
        value, slope = gelu_both(u)
        hid = value.astype(BF)
        branch[...] += mm(hid, down[slot])
        gub = (mm_nt(halves(cot, first_long), down[slot]) * slope).astype(BF)
        sums = jnp.sum(f(gub), axis=0, keepdims=True)
        for c in range(4):
            ub[pl.ds(4 * i + c, 1), :] = sums[:, 128 * c : 128 * c + 128]
        dh[...] += mm_nt(gub, up[slot])
        gup = mm(hmt[...], gub).astype(BF)
        at = pl.multiple_of(6144 * i, 512)
        for c in range(4):
            grads[pl.ds(at + 768 * c, 768), :] = gup[:, 128 * c : 128 * c + 128]
        gdown = mm_tn(hid, halves(cot, first_long)).astype(BF)
        for c in range(6):
            grads[pl.ds(at + 3072 + 512 * c, 512), :] = gdown[:, 128 * c : 128 * c + 128]

        @pl.when(i < 3)
        def _():
            for c in ff_copies(i + 3, slot):
                c.start()

    sum_mlp = sum_stages(36864, cube, grads, a_mlp, rx0, rxs, rxe, sems_m, None)
    next(sum_mlp)

    def rows(v, at, n):
        for c in range(n):
            small_o[at + c : at + c + 1, :] = v[:, 128 * c : 128 * c + 128]

    def square(v, at):
        s = jnp.sum(v * v, axis=0, keepdims=True)
        t = s[:, 0:128]
        for c in range(1, 6):
            t = t + s[:, 128 * c : 128 * c + 128]
        small_o[at : at + 1, :] = t

    def norm_back(d, gain, at):
        znorm, r = zn[...], rn[:, 0:1]
        rows(jnp.sum(d * znorm, axis=0, keepdims=True), at, 6)
        rows(jnp.sum(d, axis=0, keepdims=True), at + 6, 6)
        e = d * line(gain)
        return r * (
            e - jnp.mean(e, axis=-1, keepdims=True) - znorm * jnp.mean(e * znorm, axis=-1, keepdims=True)
        )

    @pl.loop(0, 32)
    def _(i):
        found = jnp.int32(0)
        for j in range(32):
            found = jnp.where(span_of(j) == i, j, found)
        source[i] = found

    x, znorm, r = norm_parts()
    zn[...] = znorm
    rn[...] = jnp.broadcast_to(r, rn.shape)
    dy = f(halves(cot, first_long))
    small_o[72:80, :] = jnp.zeros((8, 128), F32)
    square(branch[...], 74)
    rows(jnp.sum(dy, axis=0, keepdims=True), 42, 6)
    small_o[48:72, :] = ub[...]
    branch[...] = branch[...] + x
    dh[...] = dy + norm_back(dh[...], mgain, 12)
    hmt[...] = f(ha_r[...]).T.astype(BF)

    def fold(v, op):
        return op(v.reshape(v.shape[0] // 8, 8, v.shape[1]), axis=0)

    lowq = low_lanes((256, 128))

    def load_tile(at):
        tile = qg[pl.ds(pl.multiple_of(at, 256), 256), :]
        zero = jnp.zeros_like(tile)
        gt = f(tile).T[64:128]
        return jnp.where(lowq, tile, zero), jnp.where(lowq, zero, tile), gt

    def store_tile(at, dqt, ot):
        both = jnp.concatenate([dqt * 0.125, ot], axis=0)
        qo[pl.ds(at // 64, 4)] = both.T.astype(BF).reshape(4, 64, 128)

    def key_rows(start, n):
        return lax.broadcasted_iota(jnp.int32, (n, 256), 0) + start

    def strided_places(t):
        col = lax.broadcasted_iota(jnp.int32, (1, 256), 1)
        return (4 * t + col // 64) * 128 + 64 * part + lax.rem(col, 64)

    def get_keys(ref, rows, flip):
        @pl.loop(0, 32)
        def _(i):
            src = source[31 - i] if flip else source[i]
            kv[pl.ds(pl.multiple_of(i * 128, 128), 128), :] = ref[src, 0:128, :]
            qg[pl.ds(pl.multiple_of(i * rows, rows), rows), :] = ref[src, 128 : 128 + rows, :]

        @pl.loop(0, 32)
        def _(i):
            block = pl.ds(pl.multiple_of(i * 128, 128), 128)
            kvt[:, block] = f(kv[block, :]).T.astype(BF)

        dkv[...] = jnp.zeros_like(dkv)

    def put_back(ref, rows, flip):
        @pl.loop(0, 32)
        def _(i):
            rel = 31 - span_of(i) if flip else span_of(i)
            ref[i, 0:128, :] = dkv[rel].astype(BF)
            if rows == 64:
                ref[i, 128:192, :] = qo[rel]
            else:
                ref[i, 128:192, :] = qo[2 * rel]
                ref[i, 192:256, :] = qo[2 * rel + 1]

    def long_tile(t):
        qz, zg, gt = load_tile(t * 256)

        def chunk(c):
            return pl.ds(pl.multiple_of(c * 512, 512), 512)

        def score(c, m8):
            s = mm_nt(kv[chunk(c), :], qz)
            sc[chunk(c), :] = s
            return jnp.maximum(m8, fold(s, jnp.max))

        m8 = lax.fori_loop(0, t, score, jnp.full((8, 256), NEG, F32))
        s = mm_nt(kv[chunk(t), :], qz)
        s = jnp.where(key_rows(t * 512, 512) <= strided_places(t), s, NEG)
        sc[chunk(t), :] = s
        m8 = jnp.maximum(m8, fold(s, jnp.max))
        m = jnp.max(m8, axis=0, keepdims=True)

        def weigh(c, carry):
            l8, ot = carry
            p = jnp.exp(sc[chunk(c), :] - m)
            return l8 + fold(p, jnp.sum), ot + mm(kvt[64:128, chunk(c)], p.astype(BF))

        l8, ot = lax.fori_loop(
            0, t + 1, weigh, (jnp.zeros((8, 256), F32), jnp.zeros((64, 256), F32))
        )
        total = jnp.sum(l8, axis=0, keepdims=True)
        ot = ot * (1.0 / total)
        lse = m + jnp.log(total)
        delta = jnp.sum(gt * ot, axis=0, keepdims=True)

        def back(c, dqt):
            p = jnp.exp(sc[chunk(c), :] - lse)
            ds = (p * (mm_nt(kv[chunk(c), :], zg) - delta)).astype(BF)
            dkv[pl.ds(4 * c, 4)] += (mm(ds, qz) + mm(p.astype(BF), zg)).reshape(4, 128, 128)
            return dqt + mm(kvt[0:64, chunk(c)], ds)

        dqt = lax.fori_loop(0, t + 1, back, jnp.zeros((64, 256), F32))
        store_tile(t * 256, dqt, ot)

    def short_tile(at, start, n, places):
        qz, zg, gt = load_tile(at)
        keys = pl.ds(pl.multiple_of(start, 256), n)
        k = kv[keys, :]
        place = key_rows(start, n)
        s = jnp.where((place <= places) & (place >= begin_of(places)), mm_nt(k, qz), NEG)
        m = jnp.max(fold(s, jnp.max), axis=0, keepdims=True)
        e = jnp.exp(s - m)
        inv = 1.0 / jnp.sum(fold(e, jnp.sum), axis=0, keepdims=True)
        p = e * inv
        pb = p.astype(BF)
        ot = mm(kvt[64:128, keys], pb)
        delta = jnp.sum(gt * ot, axis=0, keepdims=True)
        ds = (p * (mm_nt(k, zg) - delta)).astype(BF)
        dkv[pl.ds(start // 128, n // 128)] += (mm(ds, qz) + mm(pb, zg)).reshape(n // 128, 128, 128)
        dqt = mm(kvt[0:64, keys], ds)
        store_tile(at, dqt, ot)

    def full_tile(t):
        places = lax.broadcasted_iota(jnp.int32, (1, 256), 1) + 256 * t
        short_tile(t * 256, 256 * (t - 2) * ((t + 14) // 16), 768, places)

    def half_tile(t):
        short_tile(t * 256, 512 * (t - 1) * ((t + 7) // 8), 1024, strided_places(t))

    def home_full(i, run):
        d = walk(y, z, part, i)[3]

        @pl.when(is_short)
        def _():
            run(rx_a.at[d], ret_a.at[y * 2 + part], e2_r.at[1], d)

    def home(i, run):
        d = walk(y, z, part, i)[3]

        @pl.when(is_short)
        def _():
            run(rx_b.at[d], ret_b.at[y * 2 + part], e2_r.at[2], d)

        @pl.when(is_long)
        def _():
            run(rx_l.at[d], ret_l.at[(y * 3 + mine) * 2 + part], e2_r.at[0], d)

    def tiles(of, body):
        pl.loop(0, len(of))(lambda i: body(of[0] + (of[-1] - of[0]) // max(len(of) - 1, 1) * i))

    long_tiles = [[7], [6], [5], [4], [3, 0], [2, 1]]
    full_tiles = [range(0, 6), range(6, 11), range(11, 16)]
    half_tiles = [range(0, 3), range(3, 5), range(5, 8)]

    @pl.when(is_long)
    def _():
        pltpu.make_async_copy(rx_l, rx_l, e1_r.at[0]).wait()
        get_keys(rx_l, 64, False)

    @pl.when(is_short)
    def _():
        pltpu.make_async_copy(rx_a, rx_a, e1_r.at[1]).wait()
        get_keys(rx_a, 128, True)

    next(sum_mlp)
    for slot in range(6):
        @pl.when(is_long)
        def _():
            tiles(long_tiles[slot], long_tile)
            if slot == 5:
                put_back(rx_l, 64, False)

        @pl.when(is_short)
        def _():
            if slot < 3:
                tiles(full_tiles[slot], full_tile)
            else:
                tiles(half_tiles[slot - 3], half_tile)
            if slot == 2:
                put_back(rx_a, 128, True)
                home_full(0, local)

                @pl.loop(1, 32)
                def _(i):
                    home_full(i, start_by(e2a_s, i))

                pltpu.make_async_copy(rx_b, rx_b, e1_r.at[2]).wait()
                get_keys(rx_b, 64, True)
            if slot == 5:
                put_back(rx_b, 64, True)

        if slot < 5:
            next(sum_mlp)

    home(0, local)

    @pl.loop(1, 32)
    def _(i):
        home(i, start_by(e2_s, i))

    for unused in range(4):
        next(sum_mlp)
    pltpu.make_async_copy(ret_a, ret_a, e2_r.at[1]).wait()
    pltpu.make_async_copy(ret_b, ret_b, e2_r.at[2]).wait()
    pltpu.make_async_copy(ret_l, ret_l, e2_r.at[0]).wait()
    next(sum_mlp)

    def gather(head):
        pair, kind = head // 3, head % 3
        kv_l = f(ret_l[2 * head, 0:128, :]) + f(ret_l[2 * head + 1, 0:128, :])
        qo_l = [f(ret_l[2 * head, 128:192, :]), f(ret_l[2 * head + 1, 128:192, :])]
        if kind == 1:
            kv_s = f(ret_b[2 * pair, 0:128, :]) + f(ret_b[2 * pair + 1, 0:128, :])
            qo_s = [f(ret_b[2 * pair, 128:192, :]), f(ret_b[2 * pair + 1, 128:192, :])]
        else:
            slot = 2 * pair + kind // 2
            kv_s = f(ret_a[slot, 0:128, :])
            qo_s = [f(ret_a[slot, 128:256, :])]
        return jnp.concatenate([kv_l, kv_s], axis=0), jnp.concatenate(qo_l + qo_s, axis=0)

    for j in range(6):
        kv_a, qo_a = gather(2 * j)
        kv_b, qo_b = gather(2 * j + 1)
        dq = jnp.where(low, qo_a, swap64(qo_b))
        ov = jnp.where(low, swap64(qo_a), qo_b)
        dk = jnp.where(low, kv_a, swap64(kv_b))
        dv = jnp.where(low, swap64(kv_a), kv_b)
        cols = slice(128 * j, 128 * j + 128)
        att[:, cols] = ov.astype(BF)
        gqkv[:, cols] = turn(dq, tabs[0], tabs[1], tabs[2], -1.0).astype(BF)
        gqkv[:, 768 + 128 * j : 896 + 128 * j] = turn(dk, tabs[0], tabs[1], tabs[2], -1.0).astype(BF)
        gqkv[:, 1536 + 128 * j : 1664 + 128 * j] = dv.astype(BF)

    def put_rows(ref, v):
        ref[0:128, :] = jnp.where(first_long, v[0:128], v[128:256])
        ref[128:256, :] = jnp.where(first_long, v[128:256], v[0:128])

    attT = f(att[...]).T.astype(BF)
    dy_b = halves(cot, first_long)
    for w in range(3):
        t = mm(attT, dy_b[:, 256 * w : 256 * w + 256]).astype(BF)
        for b in range(2):
            grads[768 * (18 + 2 * w + b) : 768 * (19 + 2 * w + b), :] = t[:, 128 * b : 128 * b + 128]
    for w in range(9):
        t = mm(hmt[...], gqkv[:, 256 * w : 256 * w + 256]).astype(BF)
        for b in range(2):
            grads[768 * (2 * w + b) : 768 * (2 * w + b + 1), :] = t[:, 128 * b : 128 * b + 128]
    sum_attn = sum_stages(18432, cube, grads, a_attn, rx1, rxs, rxe, sems_a, (small_o, srx, sm_s, sm_r))
    next(sum_attn)

    attn = mm(att[...], wout[...]) + line(outb)
    out = attn + branch[...]
    put_rows(mixed_o, out.astype(BF))
    square(out, 72)
    square(attn, 73)
    d_attn = jnp.zeros((256, D), F32)
    for w in range(9):
        piece = gqkv[:, 256 * w : 256 * w + 256]
        rows(jnp.sum(f(piece), axis=0, keepdims=True), 24 + 2 * w, 2)
        d_attn = d_attn + mm_nt(piece, wqkv[:, 256 * w : 256 * w + 256])
    put_rows(tgrad_o, dh[...] + norm_back(d_attn, again, 0))

    next(sum_mlp)
    next(sum_attn)
    for unused in sum_attn:
        pass
    for unused in sum_mlp:
        pass

    @pl.loop(1, 32)
    def _(i):
        there(i, end_by(e1_s, i))
        there_half(i, end_by(e1b_s, i))
        home_full(i, end_by(e2a_s, i))
        home(i, end_by(e2_s, i))


def layer_call(*args):
    def vm(n):
        return [pl.BlockSpec(memory_space=pltpu.VMEM)] * n

    def vb(*shape):
        return pltpu.VMEM(shape, BF)

    def vf(*shape):
        return pltpu.VMEM(shape, F32)

    dma = pltpu.SemaphoreType.DMA
    sum_sems = [dma((6,)), dma((6,)), dma((STEPS, 6)), dma((STEPS, 6)), dma((6,)), dma((6,))]
    sum_sems += [dma((STEPS, 6)), dma((STEPS, 6)), dma((6,)), dma((6,)), dma((6,))]
    anywhere = pl.BlockSpec(memory_space=pl.ANY)
    return pl.pallas_call(
        layer_kernel,
        out_shape=(
            jax.ShapeDtypeStruct((256, D), BF),
            jax.ShapeDtypeStruct((256, D), F32),
            jax.ShapeDtypeStruct((SMALL, 128), F32),
            jax.ShapeDtypeStruct((36864, 128), BF),
            jax.ShapeDtypeStruct((18432, 128), BF),
        ),
        in_specs=[pl.BlockSpec(memory_space=pltpu.SMEM)] * 2 + vm(10) + [anywhere] * 4,
        out_specs=vm(3) + [anywhere] * 2,
        scratch_shapes=[
            pltpu.SMEM((32,), jnp.int32),
            vb(D, 3 * D), vb(D, D), vb(3, D, 512), vb(3, 512, D),
            vb(24, 192, 128), vb(8, 256, 128), vb(8, 192, 128),
            vb(32, 192, 128), vb(32, 256, 128), vb(32, 192, 128),
            vb(24, 192, 128), vb(8, 256, 128), vb(8, 192, 128),
            vb(256, D), vb(256, D), vb(D, 256), vf(3, 256, 128), vf(256, D), vf(256, D), vf(256, D), vf(256, 128),
            vf(24, 128), vf(6, 512), vb(36864, 128),
            vb(HALF, 128), vb(128, HALF), vb(HALF, 128), vb(64, 64, 128), vf(32, 128, 128), vf(HALF, 256),
            vb(256, 3 * D), vb(256, D),
            vb(6, 3072, 128), vb(6, 1536, 128),
        ]
        + [vb(6, 3072 >> (t + 1), 128) for t in range(STEPS)]
        + [vb(6, 3072 >> STEPS, 128), vf(7, SMALL, 128)]
        + [dma((9,)), dma, dma((3,)), dma((3,)), dma((32,)), dma((32,)), dma((3,))]
        + [dma((32,)), dma((32,)), dma((3,)), dma((7,)), dma((7,))]
        + sum_sems * 2,
        compiler_params=pltpu.CompilerParams(
            collective_id=0, has_side_effects=True, vmem_limit_bytes=62 << 20
        ),
    )(*args)


VECTORS = ((0, 6), (6, 6), (12, 6), (18, 6), (24, 18), (42, 6), (48, 24), (42, 6))


def unpack_kernel(small, a_mlp, a_qkv, a_out, mixed, tgrad, mixed_o, tgrad_o, up_o, down_o, qkv_o, out_o, *rest):
    vectors, roots = rest[:8], rest[8:]
    mixed_o[...] = mixed[...]
    tgrad_o[...] = tgrad[...]
    for c in range(4):
        up_o[:, 128 * c : 128 * c + 128] = a_mlp[768 * c : 768 * c + 768, :].astype(F32)
    for c in range(6):
        down_o[:, 128 * c : 128 * c + 128] = a_mlp[3072 + 512 * c : 3584 + 512 * c, :].astype(F32)
    for c in range(3):
        qkv_o[:, 128 * c : 128 * c + 128] = a_qkv[768 * c : 768 * c + 768, :].astype(F32)
    out_o[...] = a_out[...].astype(F32)

    @pl.when(pl.program_id(0) == 0)
    def _():
        for ref, (at, n) in zip(vectors, VECTORS):
            for c in range(n):
                ref[pl.ds(128 * c, 128)] = small[at + c, :]
        for ref, at in zip(roots, (72, 73, 74)):
            total = jnp.sum(small[at : at + 1, :], axis=1, keepdims=True)
            ref[0] = jnp.sqrt(total * (1.0 / (D * 256 * 128)))[0, 0]


def unpack_call(small, a_mlp, a_attn, mixed, tgrad):
    def whole(n):
        return pl.BlockSpec((n,), lambda i: (0,))

    sizes = [128 * n for at, n in VECTORS]
    scalar = pl.BlockSpec(memory_space=pltpu.SMEM)
    columns = pl.BlockSpec((256, 128), lambda i: (0, i))
    return pl.pallas_call(
        unpack_kernel,
        grid=(6,),
        out_shape=(
            jax.ShapeDtypeStruct((256, D), BF),
            jax.ShapeDtypeStruct((256, D), F32),
            jax.ShapeDtypeStruct((D, FF), F32),
            jax.ShapeDtypeStruct((FF, D), F32),
            jax.ShapeDtypeStruct((D, 3 * D), F32),
            jax.ShapeDtypeStruct((D, D), F32),
        )
        + tuple(jax.ShapeDtypeStruct((n,), F32) for n in sizes)
        + tuple(jax.ShapeDtypeStruct((1,), F32) for unused in range(3)),
        in_specs=[
            pl.BlockSpec((SMALL, 128), lambda i: (0, 0)),
            pl.BlockSpec((6144, 128), lambda i: (i, 0)),
            pl.BlockSpec((2304, 128), lambda i: (i, 0)),
            pl.BlockSpec((768, 128), lambda i: (18 + i, 0)),
            columns,
            columns,
        ],
        out_specs=[
            columns,
            columns,
            pl.BlockSpec((D, 512), lambda i: (0, i)),
            pl.BlockSpec((512, D), lambda i: (i, 0)),
            pl.BlockSpec((D, 384), lambda i: (0, i)),
            pl.BlockSpec((D, 128), lambda i: (0, i)),
        ]
        + [whole(n) for n in sizes]
        + [scalar] * 3,
        compiler_params=pltpu.CompilerParams(vmem_limit_bytes=62 << 20),
    )(small, a_mlp, a_attn, a_attn, mixed, tgrad)


def on_device(tokens, attn_gain, attn_bias, mlp_gain, mlp_bias, qkv_weight, qkv_bias, out_weight, out_bias,
              up_weight, up_bias, down_weight, down_bias, cotangent, doc_lengths, span_order):
    mixed, tokens_grad, small, mlp_sum, attn_sum = layer_call(
        span_order, doc_lengths, tokens, cotangent, attn_gain, attn_bias, mlp_gain, mlp_bias, qkv_bias, out_bias,
        up_bias, down_bias, qkv_weight, out_weight, up_weight, down_weight,
    )
    mixed, tokens_grad, up, down, qkv, out, ag, ab, mg, mb, bq, bo, bu, bd, *roots = unpack_call(
        small, mlp_sum, attn_sum, mixed, tokens_grad
    )
    rms = [root.reshape(()) for root in roots]
    return (mixed, tokens_grad, ag, ab, mg, mb, qkv, bq, out, bo, up, bu, down, bd, *rms)


def solution(mesh):
    rows, split = P(("dp", "blk"), None), P("dp", None)
    return jax.shard_map(
        on_device,
        mesh=mesh,
        in_specs=(rows,) + (P(),) * 12 + (rows, split, split),
        out_specs=(rows, rows) + (P(),) * 15,
        check_vma=False,
    )
```

```python
import math

import jax
import jax.numpy as jnp
from jax import lax
from jax.experimental import pallas as pl
from jax.experimental.pallas import tpu as pltpu
from jax.sharding import PartitionSpec as P


D = 768
HEADS = 12
ROT = 16
FF = 3072
HALF = 4096
SPANS = 32
EPS = 1e-05
NEG = -1e30
SMALL = 80
BF = jnp.bfloat16
F32 = jnp.float32
MESH = pl.DeviceIdType.MESH
NT = (((1,), (1,)), ((), ()))
TN = (((0,), (0,)), ((), ()))


def mm(a, b):
    return jnp.dot(a, b, preferred_element_type=F32)


def mm_nt(a, b):
    return lax.dot_general(a, b, NT, preferred_element_type=F32)


def mm_tn(a, b):
    return lax.dot_general(a, b, TN, preferred_element_type=F32)


def halves(ref, first_long):
    top, bottom = ref[0:128, :], ref[128:256, :]
    return jnp.concatenate(
        [jnp.where(first_long, top, bottom), jnp.where(first_long, bottom, top)], axis=0
    )


def line(ref):
    return ref[...].astype(F32).reshape(1, -1)


def low_lanes(shape):
    return lax.broadcasted_iota(jnp.int32, shape, 1) < 64


def swap64(v):
    return pltpu.roll(v, 64, 1)


def turn(v, c, s1, s2, sign):
    return v * c + sign * (pltpu.roll(v, 120, 1) * s1 + pltpu.roll(v, 8, 1) * s2)


def role(dp, me):
    shift = 2 * lax.rem(dp, 2) + dp // 2
    y, z, part = me // 8, lax.rem(me // 2, 4), lax.rem(me, 2)
    return y, z, part, shift, lax.rem(z - y - shift + 12, 4)


def walk(y, z, part, i):
    y2 = lax.rem(y + i // 8, 4)
    z2 = lax.rem(z + lax.rem(i // 2, 4), 4)
    p2 = lax.rem(part + lax.rem(i, 2), 2)
    return y2, z2, p2, y2 * 8 + z2 * 2 + p2


def place_id(core, x, y, z):
    return (lax.rem(x, 2) * 2 + core, y * 8 + z * 2 + x // 2)


def rings_of(dp, blk):
    core = lax.rem(dp, 2)
    at = {"x": lax.rem(blk, 2) * 2 + dp // 2, "y": blk // 8, "z": lax.rem(blk // 2, 4)}
    rings = []
    for axis in ("x", "y", "z"):
        peers = []
        for k in range(1, 4):
            there = dict(at)
            there[axis] = lax.rem(at[axis] + k, 4)
            peers.append(place_id(core, there["x"], there["y"], there["z"]))
        rings.append((at[axis], peers))
    return core, place_id(1 - core, at["x"], at["y"], at["z"]), rings


def remote(src, dst, send, recv, d):
    return pltpu.make_async_remote_copy(src, dst, send, recv, device_id=d, device_id_type=MESH)


ORDER = (2, 1, 3, 0)


def sum_stages(rows, places, f_ref, a_ref, bufs, sems, small):
    rx0, rxa, rxb, rxx = bufs
    core_s, core_r, a_s, a_r, b_s, b_r, x_s, x_r, gb_s, gb_r, ga_s, ga_r, fin_s, fin_r, loc = sems
    core, other, rings = places
    part, n1, n2 = rows // 6, rows // 24, rows // 96
    base = [core * (rows // 2) + r * part for r in range(3)]
    there = [(1 - core) * (rows // 2) + r * part for r in range(3)]
    at = [[rings[(r + j) % 3][0] for j in range(3)] for r in range(3)]
    peer = [[rings[(r + j) % 3][1] for j in range(3)] for r in range(3)]

    def span(start, n):
        return pl.ds(pl.multiple_of(start, 16), n)

    def step(n):
        w = min(n, 384)
        while n % w:
            w -= 16
        return w

    def add(start, n, sources):
        w = step(n)

        @pl.loop(0, n // w)
        def _(i):
            here = span(start + i * w, w)
            total = f_ref[here, :].astype(F32)
            for ref in sources:
                total = total + ref[span(i * w, w), :].astype(F32)
            f_ref[here, :] = total.astype(BF)

    def first(r, k):
        return lax.rem(at[r][0] + k, 4) * n1

    def second(r, k):
        return lax.rem(at[r][1] + k, 4) * n2

    own1 = [base[r] + first(r, 0) for r in range(3)]
    own2 = [own1[r] + second(r, 0) for r in range(3)]

    cores = {}
    for k in ORDER:
        for r in range(3):
            cores[r, k] = remote(
                f_ref.at[span(there[r] + first(r, k), n1)], rx0.at[r, k, pl.ds(0, n1)],
                core_s.at[r, k], core_r.at[r, k], other,
            )
            cores[r, k].start()
    yield
    if small is not None:
        so_ref, mail, sm_s, sm_r = small
        cross = remote(so_ref, mail.at[0, 0], sm_s.at[0, 0], sm_r.at[0, 0], other)
        cross.start()
    sent = {}
    for k in ORDER:
        for r in range(3):
            cores[r, k].wait_recv()
            here = base[r] + first(r, k)
            add(here, n1, [rx0.at[r, k]])
            if k:
                sent[r, k] = remote(
                    f_ref.at[span(here, n1)], rxa.at[r, k - 1, pl.ds(0, n1)],
                    a_s.at[r, k - 1], a_r.at[r, k - 1], peer[r][0][k - 1],
                )
                sent[r, k].start()

    letters = []

    def small_send(j):
        mail[j + 1, rings[j][0]] = so_ref[...]
        for k in range(3):
            c = remote(so_ref, mail.at[j + 1, rings[j][0]], sm_s.at[j + 1, k], sm_r.at[j + 1, k], rings[j][1][k])
            c.start()
            letters.append(c)

    def small_take(j):
        if j < 0:
            cross.wait()
            so_ref[...] += mail[0, 0]
        else:
            for c in letters[3 * j : 3 * j + 3]:
                c.wait()
            so_ref[...] = (mail[j + 1, 0] + mail[j + 1, 1]) + (mail[j + 1, 2] + mail[j + 1, 3])

    def small_next(j):
        if small is not None:
            small_take(j - 1)
            if j < 3:
                small_send(j)

    small_next(0)
    yield
    came, sent = sent, {}
    for r in range(3):
        for k in range(1, 4):
            came[r, k].wait_recv()
        add(own1[r], n1, [rxa.at[r, k] for k in range(3)])
        for k in (2, 1, 3):
            sent[r, k] = remote(
                f_ref.at[span(own1[r] + second(r, k), n2)], rxb.at[r, k - 1, pl.ds(0, n2)],
                b_s.at[r, k - 1], b_r.at[r, k - 1], peer[r][1][k - 1],
            )
            sent[r, k].start()
    small_next(1)
    for c in cores.values():
        c.wait_send()
    yield
    before, came, sent = came, sent, {}
    for r in range(3):
        for k in range(1, 4):
            came[r, k].wait_recv()
        add(own2[r], n2, [rxb.at[r, k] for k in range(3)])
        mine = rxx.at[r, at[r][2], pl.ds(0, n2)]
        mine[...] = f_ref[span(own2[r], n2), :]
        for k in (2, 1, 3):
            sent[r, k] = remote(
                f_ref.at[span(own2[r], n2)], mine, x_s.at[r, k - 1], x_r.at[r, k - 1], peer[r][2][k - 1]
            )
            sent[r, k].start()
    small_next(2)
    for c in before.values():
        c.wait_send()
    yield
    before, came, sent, kept = came, sent, {}, []
    for r in range(3):
        for k in range(1, 4):
            came[r, k].wait()
        w = step(n2)

        @pl.loop(0, n2 // w)
        def _(i):
            q = [rxx[r, j, span(i * w, w), :].astype(F32) for j in range(4)]
            f_ref[span(own2[r] + i * w, w), :] = ((q[0] + q[1]) + (q[2] + q[3])).astype(BF)

        here = span(own2[r], n2)
        for k in (2, 1, 3):
            sent[r, k] = remote(
                f_ref.at[here], a_ref.at[here], gb_s.at[r, k - 1], gb_r.at[r, k - 1], peer[r][1][k - 1]
            )
            sent[r, k].start()
        c = pltpu.make_async_copy(f_ref.at[here], a_ref.at[here], loc.at[r])
        c.start()
        kept.append(c)
    small_next(3)
    for c in before.values():
        c.wait_send()
    yield
    came, sent, last = sent, {}, []

    def to_other(r, k):
        here = a_ref.at[span(base[r] + first(r, k), n1)]
        c = remote(here, here, fin_s.at[r, k], fin_r.at[r, k], other)
        c.start()
        last.append(c)

    for r in range(3):
        for k in range(1, 4):
            came[r, k].wait()
        kept[r].wait()
        here = a_ref.at[span(own1[r], n1)]
        for k in (2, 1, 3):
            sent[r, k] = remote(here, here, ga_s.at[r, k - 1], ga_r.at[r, k - 1], peer[r][0][k - 1])
            sent[r, k].start()
    for r in range(3):
        to_other(r, 0)
    yield
    for k in (1, 3, 2):
        for r in range(3):
            sent[r, k].wait_recv()
            to_other(r, 4 - k)
    yield
    for c in list(sent.values()) + last:
        c.wait_send()
    for c in last:
        c.wait_recv()
    yield


def sine_cosine(angle):
    k = jnp.floor(angle * (2.0 / math.pi) + 0.5)
    r = angle - k * 1.5703125 - k * 4.837512969970703125e-4 - k * 7.54978995489188216e-8
    r2 = r * r
    s = r + r * r2 * (-1.6666654611e-1 + r2 * (8.3321608736e-3 - r2 * 1.9515295891e-4))
    c = 1.0 - 0.5 * r2 + r2 * r2 * (4.166664568298827e-2 + r2 * (-1.388731625493765e-3 + r2 * 2.443315711809948e-5))
    q = k - 4.0 * jnp.floor(k * 0.25)
    odd = (q == 1.0) | (q == 3.0)
    sine = jnp.where(odd, c, s)
    cosine = jnp.where(odd, s, c)
    return jnp.where(q >= 2.0, -sine, sine), jnp.where((q == 1.0) | (q == 2.0), -cosine, cosine)


def gelu_both(u):
    phi = 0.5 * (1.0 + lax.erf(u * (1.0 / math.sqrt(2.0))))
    density = jnp.exp(-0.5 * u * u) * (1.0 / math.sqrt(2.0 * math.pi))
    return u * phi, phi + u * density


def layer_kernel(
    order, lens, tok, cot, again, abias, mgain, mbias, bqkv, outb, upb, downb, wqkv_h, wout_h, up_h, down_h,
    mixed_o, tgrad_o, small_o, a_mlp, a_attn,
    source, wqkv, wout, up, down, tx_l, tx_a, tx_b, rx_l, rx_a, rx_b, ret_l, ret_a, ret_b,
    ha_r, hm_r, hmt, tabs, branch, dh, zn, rn, ub, ubias, grads,
    kv, kvt, qg, qo, dkv, sc, gqkv, att, rx0, rx1, rxa, rxb, rxx, mail,
    wq_sem, wo_sem, up_sem, dn_sem, e1_s, e1b_s, e1_r, e2_s, e2a_s, e2_r, sm_s, sm_r, *sum_sems,
):
    dp, me = lax.axis_index("dp"), lax.axis_index("blk")
    y, z, part, shift, mine = role(dp, me)
    is_short, is_long = mine == 3, mine != 3
    places_of = rings_of(dp, me)
    sems_m, sems_a = sum_sems[:15], sum_sems[15:]

    def f(v):
        return v.astype(F32)

    bar = pltpu.get_barrier_semaphore()

    @pl.loop(1, 32)
    def _(i):
        pl.semaphore_signal(bar, inc=1, device_id=(dp, lax.rem(me + i, 32)), device_id_type=MESH)

    for d in [places_of[1], places_of[2][0][1][0], places_of[2][0][1][2]]:
        pl.semaphore_signal(bar, inc=1, device_id=d, device_id_type=MESH)

    def qkv_copy(c):
        cols = pl.ds(256 * c, 256)
        return pltpu.make_async_copy(wqkv_h.at[:, cols], wqkv.at[:, cols], wq_sem.at[c])

    out_copy = pltpu.make_async_copy(wout_h, wout, wo_sem)

    def ff_copies(i, slot):
        cols = pl.ds(pl.multiple_of(512 * i, 512), 512)
        return (
            pltpu.make_async_copy(up_h.at[:, cols], up.at[slot], up_sem.at[slot]),
            pltpu.make_async_copy(down_h.at[cols, :], down.at[slot], dn_sem.at[slot]),
        )

    for wide in range(3):
        for kind in range(3):
            qkv_copy(3 * kind + wide).start()
    out_copy.start()
    for i in range(3):
        for c in ff_copies(i, i):
            c.start()

    first_long = lens[0, 0] > 512

    def span_of(i):
        a = order[0, 2 * i]
        return jnp.where(first_long, a, 31 - a)

    def begin_of(place):
        end = jnp.int32(0)
        begin = jnp.zeros_like(place)
        for j in range(15):
            end = end + jnp.where(first_long, lens[0, j + 1], lens[0, j])
            begin = jnp.maximum(begin, jnp.where(end <= place, end, 0))
        return begin

    own_span = span_of(me)
    row = lax.broadcasted_iota(jnp.int32, (128, 128), 0)
    lane = lax.broadcasted_iota(jnp.int32, (256, 128), 1)
    short_place = (31 - own_span) * 128 + row
    position = jnp.concatenate([own_span * 128 + row, short_place - begin_of(short_place)], axis=0)
    dim = lax.rem(lane, 64)
    step = lax.rem(lane, 8)
    inverse = jnp.full((256, 128), 1.0, F32)
    for j in range(1, 8):
        inverse = jnp.where(step == j, 10000.0 ** (-2.0 * j / ROT), inverse)
    sine, cosine = sine_cosine(f(position) * inverse)
    tabs[0] = jnp.where(dim < ROT, cosine, 1.0)
    tabs[1] = jnp.where(dim < ROT // 2, -sine, 0.0)
    tabs[2] = jnp.where((dim >= ROT // 2) & (dim < ROT), sine, 0.0)
    low = lane < 64

    def norm_parts():
        x = f(halves(tok, first_long))
        center = x - jnp.mean(x, axis=-1, keepdims=True)
        r = lax.rsqrt(jnp.mean(center * center, axis=-1, keepdims=True) + EPS)
        return x, center * r, r

    unused_x, znorm, unused_r = norm_parts()
    ha_r[...] = (znorm * line(again) + line(abias)).astype(BF)
    hm_r[...] = (znorm * line(mgain) + line(mbias)).astype(BF)
    bq, bu = line(bqkv), line(upb)
    for i in range(6):
        ubias[i : i + 1, :] = bu[:, 512 * i : 512 * i + 512]
    dyb = halves(cot, first_long)
    ha = ha_r[...]

    def put(head, kvb, qgb):
        tx_l[2 * head, 0:128, :] = kvb[0:128]
        tx_l[2 * head + 1, 0:128, :] = kvb[0:128]
        tx_l[2 * head, 128:192, :] = qgb[0:64]
        tx_l[2 * head + 1, 128:192, :] = qgb[64:128]
        pair, kind = head // 3, head % 3
        if kind == 1:
            for p in range(2):
                tx_b[2 * pair + p, 0:128, :] = kvb[128:256]
                tx_b[2 * pair + p, 128:192, :] = qgb[128 + 64 * p : 192 + 64 * p]
        else:
            slot = 2 * pair + kind // 2
            tx_a[slot, 0:128, :] = kvb[128:256]
            tx_a[slot, 128:256, :] = qgb[128:256]

    for wide in range(3):
        for kind in range(3):
            qkv_copy(3 * kind + wide).wait()
        if wide == 0:
            out_copy.wait()
        q2, k2, v2 = [
            mm(ha, wqkv[:, 768 * kind + 256 * wide : 768 * kind + 256 * wide + 256])
            + bq[:, 768 * kind + 256 * wide : 768 * kind + 256 * wide + 256]
            for kind in range(3)
        ]
        g2 = mm_nt(dyb, wout[256 * wide : 256 * wide + 256, :])
        for b in range(2):
            lanes = slice(128 * b, 128 * b + 128)
            q = f(turn(q2[:, lanes], tabs[0], tabs[1], tabs[2], 1.0).astype(BF)) * 0.125
            k = turn(k2[:, lanes], tabs[0], tabs[1], tabs[2], 1.0)
            v, g = v2[:, lanes], g2[:, lanes]
            head = 4 * wide + 2 * b
            put(head, jnp.where(low, k, swap64(v)).astype(BF), jnp.where(low, q, swap64(g)).astype(BF))
            put(head + 1, jnp.where(low, swap64(k), v).astype(BF), jnp.where(low, swap64(q), g).astype(BF))

    pl.semaphore_wait(bar, 34)

    def there(i, run):
        y2, z2, p2, d = walk(y, z, part, i)
        q = lax.rem(z2 - y2 - shift + 12, 4)

        @pl.when(q == 3)
        def _():
            run(tx_a.at[y2 * 2 + p2], rx_a.at[me], e1_r.at[1], d)

        @pl.when(q != 3)
        def _():
            run(tx_l.at[(y2 * 3 + q) * 2 + p2], rx_l.at[me], e1_r.at[0], d)

    def there_half(i, run):
        y2, z2, p2, d = walk(y, z, part, i)
        q = lax.rem(z2 - y2 - shift + 12, 4)

        @pl.when(q == 3)
        def _():
            run(tx_b.at[y2 * 2 + p2], rx_b.at[me], e1_r.at[2], d)

    def local(src, dst, sem, d):
        pltpu.make_async_copy(src, dst, sem).start()

    def start_by(sems, i):
        return lambda src, dst, sem, d: remote(src, dst, sems.at[i], sem, (dp, d)).start()

    def end_by(sems, i):
        return lambda src, dst, sem, d: remote(src, dst, sems.at[i], sem, (dp, d)).wait_send()

    there(0, local)

    @pl.loop(1, 32)
    def _(i):
        there(i, start_by(e1_s, i))

    there_half(0, local)

    @pl.loop(1, 32)
    def _(i):
        there_half(i, start_by(e1b_s, i))

    hmt[...] = f(hm_r[...]).T.astype(BF)
    dh[...] = jnp.zeros_like(dh)
    branch[...] = jnp.broadcast_to(line(downb), branch.shape)

    @pl.loop(0, 6)
    def _(i):
        slot = lax.rem(i, 3)
        for c in ff_copies(i, slot):
            c.wait()
        u = mm(hm_r[...], up[slot]) + ubias[pl.ds(i, 1), :]
        value, slope = gelu_both(u)
        hid = value.astype(BF)
        branch[...] += mm(hid, down[slot])
        gub = (mm_nt(halves(cot, first_long), down[slot]) * slope).astype(BF)
        sums = jnp.sum(f(gub), axis=0, keepdims=True)
        for c in range(4):
            ub[pl.ds(4 * i + c, 1), :] = sums[:, 128 * c : 128 * c + 128]
        dh[...] += mm_nt(gub, up[slot])
        gup = mm(hmt[...], gub).astype(BF)
        at = pl.multiple_of(6144 * i, 512)
        for c in range(4):
            grads[pl.ds(at + 768 * c, 768), :] = gup[:, 128 * c : 128 * c + 128]
        gdown = mm_tn(hid, halves(cot, first_long)).astype(BF)
        for c in range(6):
            grads[pl.ds(at + 3072 + 512 * c, 512), :] = gdown[:, 128 * c : 128 * c + 128]

        @pl.when(i < 3)
        def _():
            for c in ff_copies(i + 3, slot):
                c.start()

    sum_mlp = sum_stages(36864, places_of, grads, a_mlp, (rx0, rxa, rxb, rxx), sems_m, None)
    next(sum_mlp)

    def rows(v, at, n):
        for c in range(n):
            small_o[at + c : at + c + 1, :] = v[:, 128 * c : 128 * c + 128]

    def square(v, at):
        s = jnp.sum(v * v, axis=0, keepdims=True)
        t = s[:, 0:128]
        for c in range(1, 6):
            t = t + s[:, 128 * c : 128 * c + 128]
        small_o[at : at + 1, :] = t

    def norm_back(d, gain, at):
        znorm, r = zn[...], rn[:, 0:1]
        rows(jnp.sum(d * znorm, axis=0, keepdims=True), at, 6)
        rows(jnp.sum(d, axis=0, keepdims=True), at + 6, 6)
        e = d * line(gain)
        return r * (
            e - jnp.mean(e, axis=-1, keepdims=True) - znorm * jnp.mean(e * znorm, axis=-1, keepdims=True)
        )

    @pl.loop(0, 32)
    def _(i):
        found = jnp.int32(0)
        for j in range(32):
            found = jnp.where(span_of(j) == i, j, found)
        source[i] = found

    x, znorm, r = norm_parts()
    zn[...] = znorm
    rn[...] = jnp.broadcast_to(r, rn.shape)
    dy = f(halves(cot, first_long))
    small_o[72:80, :] = jnp.zeros((8, 128), F32)
    square(branch[...], 74)
    rows(jnp.sum(dy, axis=0, keepdims=True), 42, 6)
    small_o[48:72, :] = ub[...]
    branch[...] = branch[...] + x
    dh[...] = dy + norm_back(dh[...], mgain, 12)
    hmt[...] = f(ha_r[...]).T.astype(BF)

    def fold(v, op):
        return op(v.reshape(v.shape[0] // 8, 8, v.shape[1]), axis=0)

    lowq = low_lanes((256, 128))

    def load_tile(at):
        tile = qg[pl.ds(pl.multiple_of(at, 256), 256), :]
        zero = jnp.zeros_like(tile)
        gt = f(tile).T[64:128]
        return jnp.where(lowq, tile, zero), jnp.where(lowq, zero, tile), gt

    def store_tile(at, dqt, ot):
        both = jnp.concatenate([dqt * 0.125, ot], axis=0)
        qo[pl.ds(at // 64, 4)] = both.T.astype(BF).reshape(4, 64, 128)

    def key_rows(start, n):
        return lax.broadcasted_iota(jnp.int32, (n, 256), 0) + start

    def strided_places(t):
        col = lax.broadcasted_iota(jnp.int32, (1, 256), 1)
        return (4 * t + col // 64) * 128 + 64 * part + lax.rem(col, 64)

    def get_keys(ref, rows, flip):
        @pl.loop(0, 32)
        def _(i):
            src = source[31 - i] if flip else source[i]
            kv[pl.ds(pl.multiple_of(i * 128, 128), 128), :] = ref[src, 0:128, :]
            qg[pl.ds(pl.multiple_of(i * rows, rows), rows), :] = ref[src, 128 : 128 + rows, :]

        @pl.loop(0, 32)
        def _(i):
            block = pl.ds(pl.multiple_of(i * 128, 128), 128)
            kvt[:, block] = f(kv[block, :]).T.astype(BF)

        dkv[...] = jnp.zeros_like(dkv)

    def put_back(ref, rows, flip):
        @pl.loop(0, 32)
        def _(i):
            rel = 31 - span_of(i) if flip else span_of(i)
            ref[i, 0:128, :] = dkv[rel].astype(BF)
            if rows == 64:
                ref[i, 128:192, :] = qo[rel]
            else:
                ref[i, 128:192, :] = qo[2 * rel]
                ref[i, 192:256, :] = qo[2 * rel + 1]

    def long_tile(t):
        qz, zg, gt = load_tile(t * 256)

        def chunk(c):
            return pl.ds(pl.multiple_of(c * 512, 512), 512)

        def score(c, m8):
            s = mm_nt(kv[chunk(c), :], qz)
            sc[chunk(c), :] = s
            return jnp.maximum(m8, fold(s, jnp.max))

        m8 = lax.fori_loop(0, t, score, jnp.full((8, 256), NEG, F32))
        s = mm_nt(kv[chunk(t), :], qz)
        s = jnp.where(key_rows(t * 512, 512) <= strided_places(t), s, NEG)
        sc[chunk(t), :] = s
        m8 = jnp.maximum(m8, fold(s, jnp.max))
        m = jnp.max(m8, axis=0, keepdims=True)

        def weigh(c, carry):
            l8, ot = carry
            p = jnp.exp(sc[chunk(c), :] - m)
            return l8 + fold(p, jnp.sum), ot + mm(kvt[64:128, chunk(c)], p.astype(BF))

        l8, ot = lax.fori_loop(
            0, t + 1, weigh, (jnp.zeros((8, 256), F32), jnp.zeros((64, 256), F32))
        )
        total = jnp.sum(l8, axis=0, keepdims=True)
        ot = ot * (1.0 / total)
        lse = m + jnp.log(total)
        delta = jnp.sum(gt * ot, axis=0, keepdims=True)

        def back(c, dqt):
            p = jnp.exp(sc[chunk(c), :] - lse)
            ds = (p * (mm_nt(kv[chunk(c), :], zg) - delta)).astype(BF)
            dkv[pl.ds(4 * c, 4)] += (mm(ds, qz) + mm(p.astype(BF), zg)).reshape(4, 128, 128)
            return dqt + mm(kvt[0:64, chunk(c)], ds)

        dqt = lax.fori_loop(0, t + 1, back, jnp.zeros((64, 256), F32))
        store_tile(t * 256, dqt, ot)

    def short_tile(at, start, n, places):
        qz, zg, gt = load_tile(at)
        keys = pl.ds(pl.multiple_of(start, 256), n)
        k = kv[keys, :]
        place = key_rows(start, n)
        s = jnp.where((place <= places) & (place >= begin_of(places)), mm_nt(k, qz), NEG)
        m = jnp.max(fold(s, jnp.max), axis=0, keepdims=True)
        e = jnp.exp(s - m)
        inv = 1.0 / jnp.sum(fold(e, jnp.sum), axis=0, keepdims=True)
        p = e * inv
        pb = p.astype(BF)
        ot = mm(kvt[64:128, keys], pb)
        delta = jnp.sum(gt * ot, axis=0, keepdims=True)
        ds = (p * (mm_nt(k, zg) - delta)).astype(BF)
        dkv[pl.ds(start // 128, n // 128)] += (mm(ds, qz) + mm(pb, zg)).reshape(n // 128, 128, 128)
        dqt = mm(kvt[0:64, keys], ds)
        store_tile(at, dqt, ot)

    def full_tile(t):
        places = lax.broadcasted_iota(jnp.int32, (1, 256), 1) + 256 * t
        short_tile(t * 256, 256 * (t - 2) * ((t + 14) // 16), 768, places)

    def half_tile(t):
        short_tile(t * 256, 512 * (t - 1) * ((t + 7) // 8), 1024, strided_places(t))

    def home_full(i, run):
        d = walk(y, z, part, i)[3]

        @pl.when(is_short)
        def _():
            run(rx_a.at[d], ret_a.at[y * 2 + part], e2_r.at[1], d)

    def home(i, run):
        d = walk(y, z, part, i)[3]

        @pl.when(is_short)
        def _():
            run(rx_b.at[d], ret_b.at[y * 2 + part], e2_r.at[2], d)

        @pl.when(is_long)
        def _():
            run(rx_l.at[d], ret_l.at[(y * 3 + mine) * 2 + part], e2_r.at[0], d)

    def tiles(of, body):
        pl.loop(0, len(of))(lambda i: body(of[0] + (of[-1] - of[0]) // max(len(of) - 1, 1) * i))

    long_tiles = [[7], [6], [5], [4], [3, 0], [2, 1]]
    full_tiles = [range(0, 6), range(6, 11), range(11, 16)]
    half_tiles = [range(0, 3), range(3, 5), range(5, 8)]

    next(sum_mlp)

    @pl.when(is_long)
    def _():
        pltpu.make_async_copy(rx_l, rx_l, e1_r.at[0]).wait()
        get_keys(rx_l, 64, False)

    @pl.when(is_short)
    def _():
        pltpu.make_async_copy(rx_a, rx_a, e1_r.at[1]).wait()
        get_keys(rx_a, 128, True)

    for slot in range(6):
        @pl.when(is_long)
        def _():
            tiles(long_tiles[slot], long_tile)
            if slot == 5:
                put_back(rx_l, 64, False)

        @pl.when(is_short)
        def _():
            if slot < 3:
                tiles(full_tiles[slot], full_tile)
            else:
                tiles(half_tiles[slot - 3], half_tile)
            if slot == 2:
                put_back(rx_a, 128, True)
                home_full(0, local)

                @pl.loop(1, 32)
                def _(i):
                    home_full(i, start_by(e2a_s, i))

                pltpu.make_async_copy(rx_b, rx_b, e1_r.at[2]).wait()
                get_keys(rx_b, 64, True)
            if slot == 5:
                put_back(rx_b, 64, True)

        if slot in (1, 3):
            next(sum_mlp)

    home(0, local)

    @pl.loop(1, 32)
    def _(i):
        home(i, start_by(e2_s, i))

    next(sum_mlp)
    pltpu.make_async_copy(ret_a, ret_a, e2_r.at[1]).wait()
    pltpu.make_async_copy(ret_b, ret_b, e2_r.at[2]).wait()
    pltpu.make_async_copy(ret_l, ret_l, e2_r.at[0]).wait()
    next(sum_mlp)

    def gather(head):
        pair, kind = head // 3, head % 3
        kv_l = f(ret_l[2 * head, 0:128, :]) + f(ret_l[2 * head + 1, 0:128, :])
        qo_l = [f(ret_l[2 * head, 128:192, :]), f(ret_l[2 * head + 1, 128:192, :])]
        if kind == 1:
            kv_s = f(ret_b[2 * pair, 0:128, :]) + f(ret_b[2 * pair + 1, 0:128, :])
            qo_s = [f(ret_b[2 * pair, 128:192, :]), f(ret_b[2 * pair + 1, 128:192, :])]
        else:
            slot = 2 * pair + kind // 2
            kv_s = f(ret_a[slot, 0:128, :])
            qo_s = [f(ret_a[slot, 128:256, :])]
        return jnp.concatenate([kv_l, kv_s], axis=0), jnp.concatenate(qo_l + qo_s, axis=0)

    for j in range(6):
        kv_a, qo_a = gather(2 * j)
        kv_b, qo_b = gather(2 * j + 1)
        dq = jnp.where(low, qo_a, swap64(qo_b))
        ov = jnp.where(low, swap64(qo_a), qo_b)
        dk = jnp.where(low, kv_a, swap64(kv_b))
        dv = jnp.where(low, swap64(kv_a), kv_b)
        cols = slice(128 * j, 128 * j + 128)
        att[:, cols] = ov.astype(BF)
        gqkv[:, cols] = turn(dq, tabs[0], tabs[1], tabs[2], -1.0).astype(BF)
        gqkv[:, 768 + 128 * j : 896 + 128 * j] = turn(dk, tabs[0], tabs[1], tabs[2], -1.0).astype(BF)
        gqkv[:, 1536 + 128 * j : 1664 + 128 * j] = dv.astype(BF)

    def put_rows(ref, v):
        ref[0:128, :] = jnp.where(first_long, v[0:128], v[128:256])
        ref[128:256, :] = jnp.where(first_long, v[128:256], v[0:128])

    attT = f(att[...]).T.astype(BF)
    dy_b = halves(cot, first_long)
    for w in range(3):
        t = mm(attT, dy_b[:, 256 * w : 256 * w + 256]).astype(BF)
        for b in range(2):
            grads[768 * (18 + 2 * w + b) : 768 * (19 + 2 * w + b), :] = t[:, 128 * b : 128 * b + 128]
    for w in range(9):
        t = mm(hmt[...], gqkv[:, 256 * w : 256 * w + 256]).astype(BF)
        for b in range(2):
            grads[768 * (2 * w + b) : 768 * (2 * w + b + 1), :] = t[:, 128 * b : 128 * b + 128]
    sum_attn = sum_stages(
        18432, places_of, grads, a_attn, (rx1, rxa, rxb, rxx), sems_a, (small_o, mail, sm_s, sm_r)
    )
    next(sum_attn)

    attn = mm(att[...], wout[...]) + line(outb)
    out = attn + branch[...]
    put_rows(mixed_o, out.astype(BF))
    square(out, 72)
    square(attn, 73)
    d_attn = jnp.zeros((256, D), F32)
    for w in range(9):
        piece = gqkv[:, 256 * w : 256 * w + 256]
        rows(jnp.sum(f(piece), axis=0, keepdims=True), 24 + 2 * w, 2)
        d_attn = d_attn + mm_nt(piece, wqkv[:, 256 * w : 256 * w + 256])
    put_rows(tgrad_o, dh[...] + norm_back(d_attn, again, 0))

    next(sum_mlp)
    next(sum_attn)
    for unused in sum_attn:
        pass
    for unused in sum_mlp:
        pass

    @pl.loop(1, 32)
    def _(i):
        there(i, end_by(e1_s, i))
        there_half(i, end_by(e1b_s, i))
        home_full(i, end_by(e2a_s, i))
        home(i, end_by(e2_s, i))


def layer_call(*args):
    def vm(n):
        return [pl.BlockSpec(memory_space=pltpu.VMEM)] * n

    def vb(*shape):
        return pltpu.VMEM(shape, BF)

    def vf(*shape):
        return pltpu.VMEM(shape, F32)

    dma = pltpu.SemaphoreType.DMA
    sum_sems = [dma((3, 4))] * 2 + [dma((3, 3))] * 10 + [dma((3, 4))] * 2 + [dma((3,))]
    anywhere = pl.BlockSpec(memory_space=pl.ANY)
    return pl.pallas_call(
        layer_kernel,
        out_shape=(
            jax.ShapeDtypeStruct((256, D), BF),
            jax.ShapeDtypeStruct((256, D), F32),
            jax.ShapeDtypeStruct((SMALL, 128), F32),
            jax.ShapeDtypeStruct((36864, 128), BF),
            jax.ShapeDtypeStruct((18432, 128), BF),
        ),
        in_specs=[pl.BlockSpec(memory_space=pltpu.SMEM)] * 2 + vm(10) + [anywhere] * 4,
        out_specs=vm(3) + [anywhere] * 2,
        scratch_shapes=[
            pltpu.SMEM((32,), jnp.int32),
            vb(D, 3 * D), vb(D, D), vb(3, D, 512), vb(3, 512, D),
            vb(24, 192, 128), vb(8, 256, 128), vb(8, 192, 128),
            vb(32, 192, 128), vb(32, 256, 128), vb(32, 192, 128),
            vb(24, 192, 128), vb(8, 256, 128), vb(8, 192, 128),
            vb(256, D), vb(256, D), vb(D, 256), vf(3, 256, 128), vf(256, D), vf(256, D), vf(256, D), vf(256, 128),
            vf(24, 128), vf(6, 512), vb(36864, 128),
            vb(HALF, 128), vb(128, HALF), vb(HALF, 128), vb(64, 64, 128), vf(32, 128, 128), vf(HALF, 256),
            vb(256, 3 * D), vb(256, D),
            vb(3, 4, 1536, 128), vb(3, 4, 768, 128), vb(3, 3, 1536, 128), vb(3, 3, 384, 128), vb(3, 4, 384, 128),
            vf(4, 4, SMALL, 128),
        ]
        + [dma((9,)), dma, dma((3,)), dma((3,)), dma((32,)), dma((32,)), dma((3,))]
        + [dma((32,)), dma((32,)), dma((3,)), dma((4, 3)), dma((4, 3))]
        + sum_sems * 2,
        compiler_params=pltpu.CompilerParams(
            collective_id=0, has_side_effects=True, vmem_limit_bytes=62 << 20
        ),
    )(*args)


VECTORS = ((0, 6), (6, 6), (12, 6), (18, 6), (24, 18), (42, 6), (48, 24), (42, 6))


def unpack_kernel(small, a_mlp, a_qkv, a_out, mixed, tgrad, mixed_o, tgrad_o, up_o, down_o, qkv_o, out_o, *rest):
    vectors, roots = rest[:8], rest[8:]
    mixed_o[...] = mixed[...]
    tgrad_o[...] = tgrad[...]
    for c in range(4):
        up_o[:, 128 * c : 128 * c + 128] = a_mlp[768 * c : 768 * c + 768, :].astype(F32)
    for c in range(6):
        down_o[:, 128 * c : 128 * c + 128] = a_mlp[3072 + 512 * c : 3584 + 512 * c, :].astype(F32)
    for c in range(3):
        qkv_o[:, 128 * c : 128 * c + 128] = a_qkv[768 * c : 768 * c + 768, :].astype(F32)
    out_o[...] = a_out[...].astype(F32)

    @pl.when(pl.program_id(0) == 0)
    def _():
        for ref, (at, n) in zip(vectors, VECTORS):
            for c in range(n):
                ref[pl.ds(128 * c, 128)] = small[at + c, :]
        for ref, at in zip(roots, (72, 73, 74)):
            total = jnp.sum(small[at : at + 1, :], axis=1, keepdims=True)
            ref[0] = jnp.sqrt(total * (1.0 / (D * 256 * 128)))[0, 0]


def unpack_call(small, a_mlp, a_attn, mixed, tgrad):
    def whole(n):
        return pl.BlockSpec((n,), lambda i: (0,))

    sizes = [128 * n for at, n in VECTORS]
    scalar = pl.BlockSpec(memory_space=pltpu.SMEM)
    columns = pl.BlockSpec((256, 128), lambda i: (0, i))
    return pl.pallas_call(
        unpack_kernel,
        grid=(6,),
        out_shape=(
            jax.ShapeDtypeStruct((256, D), BF),
            jax.ShapeDtypeStruct((256, D), F32),
            jax.ShapeDtypeStruct((D, FF), F32),
            jax.ShapeDtypeStruct((FF, D), F32),
            jax.ShapeDtypeStruct((D, 3 * D), F32),
            jax.ShapeDtypeStruct((D, D), F32),
        )
        + tuple(jax.ShapeDtypeStruct((n,), F32) for n in sizes)
        + tuple(jax.ShapeDtypeStruct((1,), F32) for unused in range(3)),
        in_specs=[
            pl.BlockSpec((SMALL, 128), lambda i: (0, 0)),
            pl.BlockSpec((6144, 128), lambda i: (i, 0)),
            pl.BlockSpec((2304, 128), lambda i: (i, 0)),
            pl.BlockSpec((768, 128), lambda i: (18 + i, 0)),
            columns,
            columns,
        ],
        out_specs=[
            columns,
            columns,
            pl.BlockSpec((D, 512), lambda i: (0, i)),
            pl.BlockSpec((512, D), lambda i: (i, 0)),
            pl.BlockSpec((D, 384), lambda i: (0, i)),
            pl.BlockSpec((D, 128), lambda i: (0, i)),
        ]
        + [whole(n) for n in sizes]
        + [scalar] * 3,
        compiler_params=pltpu.CompilerParams(vmem_limit_bytes=62 << 20),
    )(small, a_mlp, a_attn, a_attn, mixed, tgrad)


def on_device(tokens, attn_gain, attn_bias, mlp_gain, mlp_bias, qkv_weight, qkv_bias, out_weight, out_bias,
              up_weight, up_bias, down_weight, down_bias, cotangent, doc_lengths, span_order):
    mixed, tokens_grad, small, mlp_sum, attn_sum = layer_call(
        span_order, doc_lengths, tokens, cotangent, attn_gain, attn_bias, mlp_gain, mlp_bias, qkv_bias, out_bias,
        up_bias, down_bias, qkv_weight, out_weight, up_weight, down_weight,
    )
    mixed, tokens_grad, up, down, qkv, out, ag, ab, mg, mb, bq, bo, bu, bd, *roots = unpack_call(
        small, mlp_sum, attn_sum, mixed, tokens_grad
    )
    rms = [root.reshape(()) for root in roots]
    return (mixed, tokens_grad, ag, ab, mg, mb, qkv, bq, out, bo, up, bu, down, bd, *rms)


def solution(mesh):
    rows, split = P(("dp", "blk"), None), P("dp", None)
    return jax.shard_map(
        on_device,
        mesh=mesh,
        in_specs=(rows,) + (P(),) * 12 + (rows, split, split),
        out_specs=(rows, rows) + (P(),) * 15,
        check_vma=False,
    )
```

```python
import math

import jax
import jax.numpy as jnp
from jax import lax
from jax.experimental import pallas as pl
from jax.experimental.pallas import tpu as pltpu
from jax.sharding import PartitionSpec as P


D = 768
HEADS = 12
ROT = 16
FF = 3072
HALF = 4096
SPANS = 32
EPS = 1e-05
NEG = -1e30
SMALL = 80
BF = jnp.bfloat16
F32 = jnp.float32
MESH = pl.DeviceIdType.MESH
NT = (((1,), (1,)), ((), ()))
TN = (((0,), (0,)), ((), ()))


def mm(a, b):
    return jnp.dot(a, b, preferred_element_type=F32)


def mm_nt(a, b):
    return lax.dot_general(a, b, NT, preferred_element_type=F32)


def mm_tn(a, b):
    return lax.dot_general(a, b, TN, preferred_element_type=F32)


def halves(ref, first_long):
    top, bottom = ref[0:128, :], ref[128:256, :]
    return jnp.concatenate(
        [jnp.where(first_long, top, bottom), jnp.where(first_long, bottom, top)], axis=0
    )


def line(ref):
    return ref[...].astype(F32).reshape(1, -1)


def low_lanes(shape):
    return lax.broadcasted_iota(jnp.int32, shape, 1) < 64


def swap64(v):
    return pltpu.roll(v, 64, 1)


def turn(v, c, s1, s2, sign):
    return v * c + sign * (pltpu.roll(v, 120, 1) * s1 + pltpu.roll(v, 8, 1) * s2)


def role(dp, me):
    shift = 2 * lax.rem(dp, 2) + dp // 2
    y, z, part = me // 8, lax.rem(me // 2, 4), lax.rem(me, 2)
    return y, z, part, shift, lax.rem(z - y - shift + 12, 4)


def walk(y, z, part, i):
    y2 = lax.rem(y + i // 8, 4)
    z2 = lax.rem(z + lax.rem(i // 2, 4), 4)
    p2 = lax.rem(part + lax.rem(i, 2), 2)
    return y2, z2, p2, y2 * 8 + z2 * 2 + p2


def place_id(core, x, y, z):
    return (lax.rem(x, 2) * 2 + core, y * 8 + z * 2 + x // 2)


def rings_of(dp, blk):
    core = lax.rem(dp, 2)
    at = {"x": lax.rem(blk, 2) * 2 + dp // 2, "y": blk // 8, "z": lax.rem(blk // 2, 4)}
    rings = []
    for axis in ("x", "y", "z"):
        peers = []
        for k in range(1, 4):
            there = dict(at)
            there[axis] = lax.rem(at[axis] + k, 4)
            peers.append(place_id(core, there["x"], there["y"], there["z"]))
        rings.append((at[axis], peers))
    return core, place_id(1 - core, at["x"], at["y"], at["z"]), rings


def remote(src, dst, send, recv, d):
    return pltpu.make_async_remote_copy(src, dst, send, recv, device_id=d, device_id_type=MESH)


ORDER = (2, 1, 3, 0)
LOG2E = math.log2(math.e)


def sum_stages(rows, places, f_ref, a_ref, bufs, sems, small):
    rx0, rxa, rxb, rxx = bufs
    core_s, core_r, a_s, a_r, b_s, b_r, x_s, x_r, gb_s, gb_r, ga_s, ga_r, fin_s, fin_r, loc = sems
    core, other, rings = places
    part, n1, n2 = rows // 6, rows // 24, rows // 96
    base = [core * (rows // 2) + r * part for r in range(3)]
    there = [(1 - core) * (rows // 2) + r * part for r in range(3)]
    at = [[rings[(r + j) % 3][0] for j in range(3)] for r in range(3)]
    peer = [[rings[(r + j) % 3][1] for j in range(3)] for r in range(3)]

    def span(start, n):
        return pl.ds(pl.multiple_of(start, 16), n)

    def step(n):
        w = min(n, 384)
        while n % w:
            w -= 16
        return w

    def add(start, n, sources):
        w = step(n)

        @pl.loop(0, n // w)
        def _(i):
            here = span(start + i * w, w)
            total = f_ref[here, :].astype(F32)
            for ref in sources:
                total = total + ref[span(i * w, w), :].astype(F32)
            f_ref[here, :] = total.astype(BF)

    def first(r, k):
        return lax.rem(at[r][0] + k, 4) * n1

    def second(r, k):
        return lax.rem(at[r][1] + k, 4) * n2

    own1 = [base[r] + first(r, 0) for r in range(3)]
    own2 = [own1[r] + second(r, 0) for r in range(3)]

    cores = {}
    for k in ORDER:
        for r in range(3):
            cores[r, k] = remote(
                f_ref.at[span(there[r] + first(r, k), n1)], rx0.at[r, k, pl.ds(0, n1)],
                core_s.at[r, k], core_r.at[r, k], other,
            )
            cores[r, k].start()
    yield
    if small is not None:
        so_ref, mail, sm_s, sm_r = small
        cross = remote(so_ref, mail.at[0, 0], sm_s.at[0, 0], sm_r.at[0, 0], other)
        cross.start()
    sent = {}
    for k in ORDER:
        for r in range(3):
            cores[r, k].wait_recv()
            here = base[r] + first(r, k)
            add(here, n1, [rx0.at[r, k]])
            if k:
                sent[r, k] = remote(
                    f_ref.at[span(here, n1)], rxa.at[r, k - 1, pl.ds(0, n1)],
                    a_s.at[r, k - 1], a_r.at[r, k - 1], peer[r][0][k - 1],
                )
                sent[r, k].start()

    letters = []

    def small_send(j):
        mail[j + 1, rings[j][0]] = so_ref[...]
        for k in range(3):
            c = remote(so_ref, mail.at[j + 1, rings[j][0]], sm_s.at[j + 1, k], sm_r.at[j + 1, k], rings[j][1][k])
            c.start()
            letters.append(c)

    def small_take(j):
        if j < 0:
            cross.wait()
            so_ref[...] += mail[0, 0]
        else:
            for c in letters[3 * j : 3 * j + 3]:
                c.wait()
            so_ref[...] = (mail[j + 1, 0] + mail[j + 1, 1]) + (mail[j + 1, 2] + mail[j + 1, 3])

    def small_next(j):
        if small is not None:
            small_take(j - 1)
            if j < 3:
                small_send(j)

    small_next(0)
    yield
    came, sent = sent, {}
    for r in range(3):
        for k in range(1, 4):
            came[r, k].wait_recv()
        add(own1[r], n1, [rxa.at[r, k] for k in range(3)])
        for k in (2, 1, 3):
            sent[r, k] = remote(
                f_ref.at[span(own1[r] + second(r, k), n2)], rxb.at[r, k - 1, pl.ds(0, n2)],
                b_s.at[r, k - 1], b_r.at[r, k - 1], peer[r][1][k - 1],
            )
            sent[r, k].start()
    small_next(1)
    for c in cores.values():
        c.wait_send()
    yield
    before, came, sent = came, sent, {}
    for r in range(3):
        for k in range(1, 4):
            came[r, k].wait_recv()
        add(own2[r], n2, [rxb.at[r, k] for k in range(3)])
        mine = rxx.at[r, at[r][2], pl.ds(0, n2)]
        mine[...] = f_ref[span(own2[r], n2), :]
        for k in (2, 1, 3):
            sent[r, k] = remote(
                f_ref.at[span(own2[r], n2)], mine, x_s.at[r, k - 1], x_r.at[r, k - 1], peer[r][2][k - 1]
            )
            sent[r, k].start()
    small_next(2)
    for c in before.values():
        c.wait_send()
    yield
    before, came, sent, kept = came, sent, {}, []
    for r in range(3):
        for k in range(1, 4):
            came[r, k].wait()
        w = step(n2)

        @pl.loop(0, n2 // w)
        def _(i):
            q = [rxx[r, j, span(i * w, w), :].astype(F32) for j in range(4)]
            f_ref[span(own2[r] + i * w, w), :] = ((q[0] + q[1]) + (q[2] + q[3])).astype(BF)

        here = span(own2[r], n2)
        for k in (2, 1, 3):
            sent[r, k] = remote(
                f_ref.at[here], a_ref.at[here], gb_s.at[r, k - 1], gb_r.at[r, k - 1], peer[r][1][k - 1]
            )
            sent[r, k].start()
        c = pltpu.make_async_copy(f_ref.at[here], a_ref.at[here], loc.at[r])
        c.start()
        kept.append(c)
    small_next(3)
    for c in before.values():
        c.wait_send()
    yield
    came, sent, last = sent, {}, []

    def to_other(r, k):
        here = a_ref.at[span(base[r] + first(r, k), n1)]
        c = remote(here, here, fin_s.at[r, k], fin_r.at[r, k], other)
        c.start()
        last.append(c)

    for r in range(3):
        for k in range(1, 4):
            came[r, k].wait()
        kept[r].wait()
        here = a_ref.at[span(own1[r], n1)]
        for k in (2, 1, 3):
            sent[r, k] = remote(here, here, ga_s.at[r, k - 1], ga_r.at[r, k - 1], peer[r][0][k - 1])
            sent[r, k].start()
    for r in range(3):
        to_other(r, 0)
    yield
    for k in (1, 3, 2):
        for r in range(3):
            sent[r, k].wait_recv()
            to_other(r, 4 - k)
    yield
    for c in list(sent.values()) + last:
        c.wait_send()
    for c in last:
        c.wait_recv()
    yield


def sine_cosine(angle):
    k = jnp.floor(angle * (2.0 / math.pi) + 0.5)
    r = angle - k * 1.5703125 - k * 4.837512969970703125e-4 - k * 7.54978995489188216e-8
    r2 = r * r
    s = r + r * r2 * (-1.6666654611e-1 + r2 * (8.3321608736e-3 - r2 * 1.9515295891e-4))
    c = 1.0 - 0.5 * r2 + r2 * r2 * (4.166664568298827e-2 + r2 * (-1.388731625493765e-3 + r2 * 2.443315711809948e-5))
    q = k - 4.0 * jnp.floor(k * 0.25)
    odd = (q == 1.0) | (q == 3.0)
    sine = jnp.where(odd, c, s)
    cosine = jnp.where(odd, s, c)
    return jnp.where(q >= 2.0, -sine, sine), jnp.where((q == 1.0) | (q == 2.0), -cosine, cosine)


def gelu_both(u):
    phi = 0.5 * (1.0 + lax.erf(u * (1.0 / math.sqrt(2.0))))
    density = jnp.exp(-0.5 * u * u) * (1.0 / math.sqrt(2.0 * math.pi))
    return u * phi, phi + u * density


def layer_kernel(
    order, lens, tok, cot, again, abias, mgain, mbias, bqkv, outb, upb, downb, wqkv_h, wout_h, up_h, down_h,
    mixed_o, tgrad_o, small_o, a_mlp, a_attn,
    source, wqkv, wout, up, down, tx_l, tx_a, tx_b, rx_l, rx_a, rx_b, ret_l, ret_a, ret_b,
    ha_r, hm_r, hmt, tabs, branch, dh, ub, ubias, grads,
    kv, kvt, qg, qo, dkv, sc, gqkv, att, rx0, rx1, rxa, rxb, rxx, mail,
    wq_sem, wo_sem, up_sem, dn_sem, e1_s, e1b_s, e1_r, e2_s, e2a_s, e2_r, sm_s, sm_r, *sum_sems,
):
    dp, me = lax.axis_index("dp"), lax.axis_index("blk")
    y, z, part, shift, mine = role(dp, me)
    is_short, is_long = mine == 3, mine != 3
    places_of = rings_of(dp, me)
    sems_m, sems_a = sum_sems[:15], sum_sems[15:]

    def f(v):
        return v.astype(F32)

    bar = pltpu.get_barrier_semaphore()

    def hops(i):
        return min(i // 8, 4 - i // 8) + min(i // 2 % 4, 4 - i // 2 % 4) + 2 * (i % 2)

    for i in sorted(range(1, 32), key=hops, reverse=True):
        pl.semaphore_signal(bar, inc=1, device_id=(dp, walk(y, z, part, i)[3]), device_id_type=MESH)

    for d in [places_of[1], places_of[2][0][1][0], places_of[2][0][1][2]]:
        pl.semaphore_signal(bar, inc=1, device_id=d, device_id_type=MESH)

    def qkv_copy(c):
        cols = pl.ds(256 * c, 256)
        return pltpu.make_async_copy(wqkv_h.at[:, cols], wqkv.at[:, cols], wq_sem.at[c])

    out_copy = pltpu.make_async_copy(wout_h, wout, wo_sem)

    def ff_copies(i, slot):
        cols = pl.ds(pl.multiple_of(512 * i, 512), 512)
        return (
            pltpu.make_async_copy(up_h.at[:, cols], up.at[slot], up_sem.at[slot]),
            pltpu.make_async_copy(down_h.at[cols, :], down.at[slot], dn_sem.at[slot]),
        )

    for wide in range(3):
        for kind in range(3):
            qkv_copy(3 * kind + wide).start()
    out_copy.start()
    for i in range(3):
        for c in ff_copies(i, i):
            c.start()

    first_long = lens[0, 0] > 512

    def span_of(i):
        a = order[0, 2 * i]
        return jnp.where(first_long, a, 31 - a)

    def begin_of(place):
        end = jnp.int32(0)
        begin = jnp.zeros_like(place)
        for j in range(15):
            end = end + jnp.where(first_long, lens[0, j + 1], lens[0, j])
            begin = jnp.maximum(begin, jnp.where(end <= place, end, 0))
        return begin

    own_span = span_of(me)
    row = lax.broadcasted_iota(jnp.int32, (128, 128), 0)
    lane = lax.broadcasted_iota(jnp.int32, (256, 128), 1)
    short_place = (31 - own_span) * 128 + row
    position = jnp.concatenate([own_span * 128 + row, short_place - begin_of(short_place)], axis=0)
    dim = lax.rem(lane, 64)
    step = lax.rem(lane, 8)
    inverse = jnp.full((256, 128), 1.0, F32)
    for j in range(1, 8):
        inverse = jnp.where(step == j, 10000.0 ** (-2.0 * j / ROT), inverse)
    sine, cosine = sine_cosine(f(position) * inverse)
    tabs[0] = jnp.where(dim < ROT, cosine, 1.0)
    tabs[1] = jnp.where(dim < ROT // 2, -sine, 0.0)
    tabs[2] = jnp.where((dim >= ROT // 2) & (dim < ROT), sine, 0.0)
    low = lane < 64

    def norm_parts():
        x = f(halves(tok, first_long))
        center = x - jnp.mean(x, axis=-1, keepdims=True)
        r = lax.rsqrt(jnp.mean(center * center, axis=-1, keepdims=True) + EPS)
        return x, center * r, r

    unused_x, znorm, unused_r = norm_parts()
    ha_r[...] = (znorm * line(again) + line(abias)).astype(BF)
    hm_r[...] = (znorm * line(mgain) + line(mbias)).astype(BF)
    bq, bu = line(bqkv), line(upb)
    for i in range(6):
        ubias[i : i + 1, :] = bu[:, 512 * i : 512 * i + 512]
    dyb = halves(cot, first_long)
    ha = ha_r[...]

    def put(head, kvb, qgb):
        tx_l[2 * head, 0:128, :] = kvb[0:128]
        tx_l[2 * head + 1, 0:128, :] = kvb[0:128]
        tx_l[2 * head, 128:192, :] = qgb[0:64]
        tx_l[2 * head + 1, 128:192, :] = qgb[64:128]
        pair, kind = head // 3, head % 3
        if kind == 1:
            for p in range(2):
                tx_b[2 * pair + p, 0:128, :] = kvb[128:256]
                tx_b[2 * pair + p, 128:192, :] = qgb[128 + 64 * p : 192 + 64 * p]
        else:
            slot = 2 * pair + kind // 2
            tx_a[slot, 0:128, :] = kvb[128:256]
            tx_a[slot, 128:256, :] = qgb[128:256]

    for wide in range(3):
        for kind in range(3):
            qkv_copy(3 * kind + wide).wait()
        if wide == 0:
            out_copy.wait()
        q2, k2, v2 = [
            mm(ha, wqkv[:, 768 * kind + 256 * wide : 768 * kind + 256 * wide + 256])
            + bq[:, 768 * kind + 256 * wide : 768 * kind + 256 * wide + 256]
            for kind in range(3)
        ]
        g2 = mm_nt(dyb, wout[256 * wide : 256 * wide + 256, :])
        for b in range(2):
            lanes = slice(128 * b, 128 * b + 128)
            q = f(turn(q2[:, lanes], tabs[0], tabs[1], tabs[2], 1.0).astype(BF)) * 0.125
            k = turn(k2[:, lanes], tabs[0], tabs[1], tabs[2], 1.0)
            v, g = v2[:, lanes], g2[:, lanes]
            head = 4 * wide + 2 * b
            put(head, jnp.where(low, k, swap64(v)).astype(BF), jnp.where(low, q, swap64(g)).astype(BF))
            put(head + 1, jnp.where(low, swap64(k), v).astype(BF), jnp.where(low, swap64(q), g).astype(BF))

    hmt[...] = f(hm_r[...]).T.astype(BF)
    dh[...] = jnp.zeros_like(dh)
    branch[...] = jnp.broadcast_to(line(downb), branch.shape)

    def feed_forward(i):
        slot = lax.rem(i, 3)
        for c in ff_copies(i, slot):
            c.wait()
        u = mm(hm_r[...], up[slot]) + ubias[pl.ds(i, 1), :]
        value, slope = gelu_both(u)
        hid = value.astype(BF)
        branch[...] += mm(hid, down[slot])
        gub = (mm_nt(halves(cot, first_long), down[slot]) * slope).astype(BF)
        sums = jnp.sum(f(gub), axis=0, keepdims=True)
        for c in range(4):
            ub[pl.ds(4 * i + c, 1), :] = sums[:, 128 * c : 128 * c + 128]
        dh[...] += mm_nt(gub, up[slot])
        gup = mm(hmt[...], gub).astype(BF)
        for c in range(4):
            grads[pl.ds(pl.multiple_of(768 * (4 * i + c), 768), 768), :] = gup[:, 128 * c : 128 * c + 128]
        gdown = mm_tn(hid, halves(cot, first_long)).astype(BF)
        for c in range(6):
            here = pl.ds(pl.multiple_of(18432 + 3072 * c + 512 * i, 512), 512)
            grads[here, :] = gdown[:, 128 * c : 128 * c + 128]

        @pl.when(i < 3)
        def _():
            for c in ff_copies(i + 3, slot):
                c.start()

    pl.semaphore_wait(bar, 34)

    def there(i, run):
        y2, z2, p2, d = walk(y, z, part, i)
        q = lax.rem(z2 - y2 - shift + 12, 4)

        @pl.when(q == 3)
        def _():
            run(tx_a.at[y2 * 2 + p2], rx_a.at[me], e1_r.at[1], d)

        @pl.when(q != 3)
        def _():
            run(tx_l.at[(y2 * 3 + q) * 2 + p2], rx_l.at[me], e1_r.at[0], d)

    def there_half(i, run):
        y2, z2, p2, d = walk(y, z, part, i)
        q = lax.rem(z2 - y2 - shift + 12, 4)

        @pl.when(q == 3)
        def _():
            run(tx_b.at[y2 * 2 + p2], rx_b.at[me], e1_r.at[2], d)

    def local(src, dst, sem, d):
        pltpu.make_async_copy(src, dst, sem).start()

    def start_by(sems, i):
        return lambda src, dst, sem, d: remote(src, dst, sems.at[i], sem, (dp, d)).start()

    def end_by(sems, i):
        return lambda src, dst, sem, d: remote(src, dst, sems.at[i], sem, (dp, d)).wait_send()

    there(0, local)

    @pl.loop(1, 32)
    def _(i):
        there(i, start_by(e1_s, i))

    pl.loop(0, 6)(feed_forward)
    there_half(0, local)

    @pl.loop(1, 32)
    def _(i):
        there_half(i, start_by(e1b_s, i))

    sum_mlp = sum_stages(36864, places_of, grads, a_mlp, (rx0, rxa, rxb, rxx), sems_m, None)
    next(sum_mlp)

    def rows(v, at, n):
        for c in range(n):
            small_o[at + c : at + c + 1, :] = v[:, 128 * c : 128 * c + 128]

    def square(v, at):
        s = jnp.sum(v * v, axis=0, keepdims=True)
        t = s[:, 0:128]
        for c in range(1, 6):
            t = t + s[:, 128 * c : 128 * c + 128]
        small_o[at : at + 1, :] = t

    def norm_back(d, gain, at, znorm, r):
        rows(jnp.sum(d * znorm, axis=0, keepdims=True), at, 6)
        rows(jnp.sum(d, axis=0, keepdims=True), at + 6, 6)
        e = d * line(gain)
        return r * (
            e - jnp.mean(e, axis=-1, keepdims=True) - znorm * jnp.mean(e * znorm, axis=-1, keepdims=True)
        )

    @pl.loop(0, 32)
    def _(i):
        found = jnp.int32(0)
        for j in range(32):
            found = jnp.where(span_of(j) == i, j, found)
        source[i] = found

    x, znorm, r = norm_parts()
    dy = f(halves(cot, first_long))
    small_o[72:80, :] = jnp.zeros((8, 128), F32)
    square(branch[...], 74)
    rows(jnp.sum(dy, axis=0, keepdims=True), 42, 6)
    small_o[48:72, :] = ub[...]
    branch[...] = branch[...] + x
    dh[...] = dy + norm_back(dh[...], mgain, 12, znorm, r)
    hmt[...] = f(ha_r[...]).T.astype(BF)

    def fold(v, op):
        return op(v.reshape(v.shape[0] // 8, 8, v.shape[1]), axis=0)

    lowq = low_lanes((256, 128))

    def load_tile(at):
        tile = qg[pl.ds(pl.multiple_of(at, 256), 256), :]
        zero = jnp.zeros_like(tile)
        gt = f(tile).T[64:128]
        return jnp.where(lowq, tile, zero), jnp.where(lowq, zero, tile), gt

    def store_tile(at, dqt, ot):
        both = jnp.concatenate([dqt * 0.125, ot], axis=0)
        qo[pl.ds(at // 64, 4)] = both.T.astype(BF).reshape(4, 64, 128)

    def key_rows(start, n):
        return lax.broadcasted_iota(jnp.int32, (n, 256), 0) + start

    def strided_places(t):
        col = lax.broadcasted_iota(jnp.int32, (1, 256), 1)
        return (4 * t + col // 64) * 128 + 64 * part + lax.rem(col, 64)

    def get_keys(ref, rows, flip):
        @pl.loop(0, 32)
        def _(i):
            src = source[31 - i] if flip else source[i]
            kv[pl.ds(pl.multiple_of(i * 128, 128), 128), :] = ref[src, 0:128, :]
            qg[pl.ds(pl.multiple_of(i * rows, rows), rows), :] = ref[src, 128 : 128 + rows, :]

        @pl.loop(0, 32)
        def _(i):
            block = pl.ds(pl.multiple_of(i * 128, 128), 128)
            kvt[:, block] = f(kv[block, :]).T.astype(BF)

        dkv[...] = jnp.zeros_like(dkv)

    def put_back(ref, rows, flip):
        @pl.loop(0, 32)
        def _(i):
            rel = 31 - span_of(i) if flip else span_of(i)
            ref[i, 0:128, :] = dkv[rel].astype(BF)
            if rows == 64:
                ref[i, 128:192, :] = qo[rel]
            else:
                ref[i, 128:192, :] = qo[2 * rel]
                ref[i, 192:256, :] = qo[2 * rel + 1]

    def long_tile(t):
        qz, zg, gt = load_tile(256 * t)
        keys = [slice(lo, min(lo + 1024, 512 * t + 512)) for lo in range(0, 512 * t + 512, 1024)]
        m8 = jnp.full((8, 256), NEG, F32)
        for c in keys:
            s = mm_nt(kv[c, :], qz) * LOG2E
            if c.stop > 512 * t:
                s = jnp.where(key_rows(c.start, c.stop - c.start) <= strided_places(t), s, NEG)
            sc[c, :] = s
            m8 = jnp.maximum(m8, fold(s, jnp.max))
        m = jnp.max(m8, axis=0, keepdims=True)
        l8, ot = jnp.zeros((8, 256), F32), jnp.zeros((64, 256), F32)
        for c in keys:
            e = jnp.exp2(sc[c, :] - m)
            sc[c, :] = e
            l8 = l8 + fold(e, jnp.sum)
            ot = ot + mm(kvt[64:128, c], e.astype(BF))
        inv = 1.0 / jnp.sum(l8, axis=0, keepdims=True)
        ot = ot * inv
        delta = jnp.sum(gt * ot, axis=0, keepdims=True)
        dqt = jnp.zeros((64, 256), F32)
        for c in keys:
            p = sc[c, :] * inv
            ds = (p * (mm_nt(kv[c, :], zg) - delta)).astype(BF)
            blocks = slice(c.start // 128, c.stop // 128)
            dkv[blocks] += (mm(ds, qz) + mm(p.astype(BF), zg)).reshape(-1, 128, 128)
            dqt = dqt + mm(kvt[0:64, c], ds)
        store_tile(256 * t, dqt, ot)

    def short_tiles(of):
        work = []
        for j, (at, start, n, places) in enumerate(of):
            qz, zg, gt = load_tile(at)
            keys = pl.ds(pl.multiple_of(start, 256), n)
            place = key_rows(0, n)
            seen = (place <= places - start) & (place >= begin_of(places) - start)
            s = jnp.where(seen, mm_nt(kv[keys, :], qz) * LOG2E, NEG)
            mine = slice(1024 * j, 1024 * j + n)
            sc[mine, :] = s
            work.append((at, start, n, keys, mine, qz, zg, gt, jnp.max(fold(s, jnp.max), axis=0, keepdims=True)))
        for at, start, n, keys, mine, qz, zg, gt, m in work:
            e = jnp.exp2(sc[mine, :] - m)
            p = e * (1.0 / jnp.sum(fold(e, jnp.sum), axis=0, keepdims=True))
            pb = p.astype(BF)
            ot = mm(kvt[64:128, keys], pb)
            delta = jnp.sum(gt * ot, axis=0, keepdims=True)
            ds = (p * (mm_nt(kv[keys, :], zg) - delta)).astype(BF)
            dkv[pl.ds(start // 128, n // 128)] += (mm(ds, qz) + mm(pb, zg)).reshape(n // 128, 128, 128)
            store_tile(at, mm(kvt[0:64, keys], ds), ot)

    def full_tile(t):
        places = lax.broadcasted_iota(jnp.int32, (1, 256), 1) + 256 * t
        return t * 256, 256 * (t - 2) * ((t + 14) // 16), 768, places

    def half_tile(t):
        return t * 256, 512 * (t - 1) * ((t + 7) // 8), 1024, strided_places(t)

    def home_full(i, run):
        d = walk(y, z, part, i)[3]

        @pl.when(is_short)
        def _():
            run(rx_a.at[d], ret_a.at[y * 2 + part], e2_r.at[1], d)

    def home(i, run):
        d = walk(y, z, part, i)[3]

        @pl.when(is_short)
        def _():
            run(rx_b.at[d], ret_b.at[y * 2 + part], e2_r.at[2], d)

        @pl.when(is_long)
        def _():
            run(rx_l.at[d], ret_l.at[(y * 3 + mine) * 2 + part], e2_r.at[0], d)

    def tiles(of, body):
        @pl.loop(0, len(of) // 4)
        def _(i):
            short_tiles([body(of[0] + 4 * i + j) for j in range(4)])

    long_tiles = [[7], [6], [5], [4], [3, 0], [2, 1]]
    full_tiles = [range(0, 4), range(4, 8), range(8, 12), range(12, 16)]
    half_tiles = [range(0, 4), range(4, 8)]

    next(sum_mlp)

    @pl.when(is_long)
    def _():
        pltpu.make_async_copy(rx_l, rx_l, e1_r.at[0]).wait()
        get_keys(rx_l, 64, False)

    @pl.when(is_short)
    def _():
        pltpu.make_async_copy(rx_a, rx_a, e1_r.at[1]).wait()
        get_keys(rx_a, 128, True)

    for slot in range(6):
        @pl.when(is_long)
        def _():
            for t in long_tiles[slot]:
                long_tile(t)
            if slot == 5:
                put_back(rx_l, 64, False)

        @pl.when(is_short)
        def _():
            if slot < 4:
                tiles(full_tiles[slot], full_tile)
            else:
                tiles(half_tiles[slot - 4], half_tile)
            if slot == 3:
                put_back(rx_a, 128, True)
                home_full(0, local)

                @pl.loop(1, 32)
                def _(i):
                    home_full(i, start_by(e2a_s, i))

                pltpu.make_async_copy(rx_b, rx_b, e1_r.at[2]).wait()
                get_keys(rx_b, 64, True)
            if slot == 5:
                put_back(rx_b, 64, True)

        if slot in (0, 2):
            next(sum_mlp)

    home(0, local)

    @pl.loop(1, 32)
    def _(i):
        home(i, start_by(e2_s, i))

    next(sum_mlp)
    pltpu.make_async_copy(ret_a, ret_a, e2_r.at[1]).wait()
    pltpu.make_async_copy(ret_b, ret_b, e2_r.at[2]).wait()
    pltpu.make_async_copy(ret_l, ret_l, e2_r.at[0]).wait()
    next(sum_mlp)

    def gather(head):
        pair, kind = head // 3, head % 3
        kv_l = f(ret_l[2 * head, 0:128, :]) + f(ret_l[2 * head + 1, 0:128, :])
        qo_l = [f(ret_l[2 * head, 128:192, :]), f(ret_l[2 * head + 1, 128:192, :])]
        if kind == 1:
            kv_s = f(ret_b[2 * pair, 0:128, :]) + f(ret_b[2 * pair + 1, 0:128, :])
            qo_s = [f(ret_b[2 * pair, 128:192, :]), f(ret_b[2 * pair + 1, 128:192, :])]
        else:
            slot = 2 * pair + kind // 2
            kv_s = f(ret_a[slot, 0:128, :])
            qo_s = [f(ret_a[slot, 128:256, :])]
        return jnp.concatenate([kv_l, kv_s], axis=0), jnp.concatenate(qo_l + qo_s, axis=0)

    for j in range(6):
        kv_a, qo_a = gather(2 * j)
        kv_b, qo_b = gather(2 * j + 1)
        dq = jnp.where(low, qo_a, swap64(qo_b))
        ov = jnp.where(low, swap64(qo_a), qo_b)
        dk = jnp.where(low, kv_a, swap64(kv_b))
        dv = jnp.where(low, swap64(kv_a), kv_b)
        cols = slice(128 * j, 128 * j + 128)
        att[:, cols] = ov.astype(BF)
        gqkv[:, cols] = turn(dq, tabs[0], tabs[1], tabs[2], -1.0).astype(BF)
        gqkv[:, 768 + 128 * j : 896 + 128 * j] = turn(dk, tabs[0], tabs[1], tabs[2], -1.0).astype(BF)
        gqkv[:, 1536 + 128 * j : 1664 + 128 * j] = dv.astype(BF)

    def put_rows(ref, v):
        ref[0:128, :] = jnp.where(first_long, v[0:128], v[128:256])
        ref[128:256, :] = jnp.where(first_long, v[128:256], v[0:128])

    attT = f(att[...]).T.astype(BF)
    dy_b = halves(cot, first_long)
    for w in range(3):
        t = mm(attT, dy_b[:, 256 * w : 256 * w + 256]).astype(BF)
        for b in range(2):
            grads[768 * (18 + 2 * w + b) : 768 * (19 + 2 * w + b), :] = t[:, 128 * b : 128 * b + 128]
    for w in range(9):
        t = mm(hmt[...], gqkv[:, 256 * w : 256 * w + 256]).astype(BF)
        for b in range(2):
            grads[768 * (2 * w + b) : 768 * (2 * w + b + 1), :] = t[:, 128 * b : 128 * b + 128]
    sum_attn = sum_stages(
        18432, places_of, grads, a_attn, (rx1, rx0, rxb, rxx), sems_a, (small_o, mail, sm_s, sm_r)
    )
    next(sum_attn)

    attn = mm(att[...], wout[...]) + line(outb)
    out = attn + branch[...]
    put_rows(mixed_o, out.astype(BF))
    square(out, 72)
    square(attn, 73)
    d_attn = jnp.zeros((256, D), F32)
    for w in range(9):
        piece = gqkv[:, 256 * w : 256 * w + 256]
        rows(jnp.sum(f(piece), axis=0, keepdims=True), 24 + 2 * w, 2)
        d_attn = d_attn + mm_nt(piece, wqkv[:, 256 * w : 256 * w + 256])
    again_x, znorm, r = norm_parts()
    put_rows(tgrad_o, dh[...] + norm_back(d_attn, again, 0, znorm, r))

    next(sum_attn)
    next(sum_attn)
    next(sum_mlp)
    for unused in sum_attn:
        pass
    for unused in sum_mlp:
        pass

    @pl.loop(1, 32)
    def _(i):
        there(i, end_by(e1_s, i))
        there_half(i, end_by(e1b_s, i))
        home_full(i, end_by(e2a_s, i))
        home(i, end_by(e2_s, i))


def layer_call(*args):
    def vm(n):
        return [pl.BlockSpec(memory_space=pltpu.VMEM)] * n

    def vb(*shape):
        return pltpu.VMEM(shape, BF)

    def vf(*shape):
        return pltpu.VMEM(shape, F32)

    dma = pltpu.SemaphoreType.DMA
    sum_sems = [dma((3, 4))] * 2 + [dma((3, 3))] * 10 + [dma((3, 4))] * 2 + [dma((3,))]
    anywhere = pl.BlockSpec(memory_space=pl.ANY)
    return pl.pallas_call(
        layer_kernel,
        out_shape=(
            jax.ShapeDtypeStruct((256, D), BF),
            jax.ShapeDtypeStruct((256, D), F32),
            jax.ShapeDtypeStruct((SMALL, 128), F32),
            jax.ShapeDtypeStruct((36864, 128), BF),
            jax.ShapeDtypeStruct((18432, 128), BF),
        ),
        in_specs=[pl.BlockSpec(memory_space=pltpu.SMEM)] * 2 + vm(10) + [anywhere] * 4,
        out_specs=vm(3) + [anywhere] * 2,
        scratch_shapes=[
            pltpu.SMEM((32,), jnp.int32),
            vb(D, 3 * D), vb(D, D), vb(3, D, 512), vb(3, 512, D),
            vb(24, 192, 128), vb(8, 256, 128), vb(8, 192, 128),
            vb(32, 192, 128), vb(32, 256, 128), vb(32, 192, 128),
            vb(24, 192, 128), vb(8, 256, 128), vb(8, 192, 128),
            vb(256, D), vb(256, D), vb(D, 256), vf(3, 256, 128), vf(256, D), vf(256, D),
            vf(24, 128), vf(6, 512), vb(36864, 128),
            vb(HALF, 128), vb(128, HALF), vb(HALF, 128), vb(64, 64, 128), vf(32, 128, 128), vf(HALF, 256),
            vb(256, 3 * D), vb(256, D),
            vb(3, 4, 1536, 128), vb(3, 4, 768, 128), vb(3, 3, 1536, 128), vb(3, 3, 384, 128), vb(3, 4, 384, 128),
            vf(4, 4, SMALL, 128),
        ]
        + [dma((9,)), dma, dma((3,)), dma((3,)), dma((32,)), dma((32,)), dma((3,))]
        + [dma((32,)), dma((32,)), dma((3,)), dma((4, 3)), dma((4, 3))]
        + sum_sems * 2,
        compiler_params=pltpu.CompilerParams(
            collective_id=0, has_side_effects=True, vmem_limit_bytes=63 << 20
        ),
    )(*args)


VECTORS = ((0, 6), (6, 6), (12, 6), (18, 6), (24, 18), (42, 6), (48, 24), (42, 6))


def unpack_kernel(small, a_up, a_down, a_qkv, a_out, mixed, tgrad, mixed_o, tgrad_o, up_o, down_o, qkv_o, out_o, *rest):
    vectors, roots = rest[:8], rest[8:]
    mixed_o[...] = mixed[...]
    tgrad_o[...] = tgrad[...]
    for a, o in ((a_up, up_o), (a_down, down_o), (a_qkv, qkv_o), (a_out, out_o)):
        for c in range(a.shape[0]):
            o[:, 128 * c : 128 * c + 128] = a[c].astype(F32)

    @pl.when(pl.program_id(0) == 0)
    def _():
        for ref, (at, n) in zip(vectors, VECTORS):
            for c in range(n):
                ref[pl.ds(128 * c, 128)] = small[at + c, :]
        for ref, at in zip(roots, (72, 73, 74)):
            total = jnp.sum(small[at : at + 1, :], axis=1, keepdims=True)
            ref[0] = jnp.sqrt(total * (1.0 / (D * 256 * 128)))[0, 0]


def unpack_call(small, a_mlp, a_attn, mixed, tgrad):
    def whole(n):
        return pl.BlockSpec((n,), lambda i: (0,))

    sizes = [128 * n for at, n in VECTORS]
    scalar = pl.BlockSpec(memory_space=pltpu.SMEM)
    columns = pl.BlockSpec((256, 128), lambda i: (0, i))
    return pl.pallas_call(
        unpack_kernel,
        grid=(6,),
        out_shape=(
            jax.ShapeDtypeStruct((256, D), BF),
            jax.ShapeDtypeStruct((256, D), F32),
            jax.ShapeDtypeStruct((D, FF), F32),
            jax.ShapeDtypeStruct((FF, D), F32),
            jax.ShapeDtypeStruct((D, 3 * D), F32),
            jax.ShapeDtypeStruct((D, D), F32),
        )
        + tuple(jax.ShapeDtypeStruct((n,), F32) for n in sizes)
        + tuple(jax.ShapeDtypeStruct((1,), F32) for unused in range(3)),
        in_specs=[
            pl.BlockSpec((SMALL, 128), lambda i: (0, 0)),
            pl.BlockSpec((24, 128, 128), lambda i: (0, i, 0)),
            pl.BlockSpec((6, 512, 128), lambda i: (1, i, 0)),
            pl.BlockSpec((18, 128, 128), lambda i: (0, i, 0)),
            pl.BlockSpec((6, 128, 128), lambda i: (3, i, 0)),
            columns,
            columns,
        ],
        out_specs=[
            columns,
            columns,
            pl.BlockSpec((128, FF), lambda i: (i, 0)),
            pl.BlockSpec((512, D), lambda i: (i, 0)),
            pl.BlockSpec((128, 3 * D), lambda i: (i, 0)),
            pl.BlockSpec((128, D), lambda i: (i, 0)),
        ]
        + [whole(n) for n in sizes]
        + [scalar] * 3,
        compiler_params=pltpu.CompilerParams(vmem_limit_bytes=62 << 20),
    )(
        small, a_mlp.reshape(48, 768, 128), a_mlp.reshape(12, 3072, 128), a_attn.reshape(24, 768, 128),
        a_attn.reshape(24, 768, 128), mixed, tgrad,
    )


def on_device(tokens, attn_gain, attn_bias, mlp_gain, mlp_bias, qkv_weight, qkv_bias, out_weight, out_bias,
              up_weight, up_bias, down_weight, down_bias, cotangent, doc_lengths, span_order):
    mixed, tokens_grad, small, mlp_sum, attn_sum = layer_call(
        span_order, doc_lengths, tokens, cotangent, attn_gain, attn_bias, mlp_gain, mlp_bias, qkv_bias, out_bias,
        up_bias, down_bias, qkv_weight, out_weight, up_weight, down_weight,
    )
    mixed, tokens_grad, up, down, qkv, out, ag, ab, mg, mb, bq, bo, bu, bd, *roots = unpack_call(
        small, mlp_sum, attn_sum, mixed, tokens_grad
    )
    rms = [root.reshape(()) for root in roots]
    return (mixed, tokens_grad, ag, ab, mg, mb, qkv, bq, out, bo, up, bu, down, bd, *rms)


def solution(mesh):
    rows, split = P(("dp", "blk"), None), P("dp", None)
    return jax.shard_map(
        on_device,
        mesh=mesh,
        in_specs=(rows,) + (P(),) * 12 + (rows, split, split),
        out_specs=(rows, rows) + (P(),) * 15,
        check_vma=False,
    )
```

```python
import math

import jax
import jax.numpy as jnp
from jax import lax
from jax.experimental import pallas as pl
from jax.experimental.pallas import tpu as pltpu
from jax.sharding import PartitionSpec as P


D = 768
HEADS = 12
ROT = 16
FF = 3072
HALF = 4096
SPANS = 32
EPS = 1e-05
NEG = -1e30
SMALL = 80
BF = jnp.bfloat16
F32 = jnp.float32
MESH = pl.DeviceIdType.MESH
NT = (((1,), (1,)), ((), ()))
TN = (((0,), (0,)), ((), ()))


def mm(a, b):
    return jnp.dot(a, b, preferred_element_type=F32)


def mm_nt(a, b):
    return lax.dot_general(a, b, NT, preferred_element_type=F32)


def mm_tn(a, b):
    return lax.dot_general(a, b, TN, preferred_element_type=F32)


def halves(ref, first_long):
    top, bottom = ref[0:128, :], ref[128:256, :]
    return jnp.concatenate(
        [jnp.where(first_long, top, bottom), jnp.where(first_long, bottom, top)], axis=0
    )


def line(ref):
    return ref[...].astype(F32).reshape(1, -1)


def low_lanes(shape):
    return lax.broadcasted_iota(jnp.int32, shape, 1) < 64


def swap64(v):
    return pltpu.roll(v, 64, 1)


def turn(v, c, s1, s2, sign):
    return v * c + sign * (pltpu.roll(v, 120, 1) * s1 + pltpu.roll(v, 8, 1) * s2)


def role(dp, me):
    shift = 2 * lax.rem(dp, 2) + dp // 2
    y, z, part = me // 8, lax.rem(me // 2, 4), lax.rem(me, 2)
    return y, z, part, shift, lax.rem(z - y - shift + 12, 4)


def walk(y, z, part, i):
    y2 = lax.rem(y + i // 8, 4)
    z2 = lax.rem(z + lax.rem(i // 2, 4), 4)
    p2 = lax.rem(part + lax.rem(i, 2), 2)
    return y2, z2, p2, y2 * 8 + z2 * 2 + p2


def place_id(core, x, y, z):
    return (lax.rem(x, 2) * 2 + core, y * 8 + z * 2 + x // 2)


def rings_of(dp, blk):
    core = lax.rem(dp, 2)
    at = {"x": lax.rem(blk, 2) * 2 + dp // 2, "y": blk // 8, "z": lax.rem(blk // 2, 4)}
    rings = []
    for axis in ("x", "y", "z"):
        peers = []
        for k in range(1, 4):
            there = dict(at)
            there[axis] = lax.rem(at[axis] + k, 4)
            peers.append(place_id(core, there["x"], there["y"], there["z"]))
        rings.append((at[axis], peers))
    return core, place_id(1 - core, at["x"], at["y"], at["z"]), rings


def remote(src, dst, send, recv, d):
    return pltpu.make_async_remote_copy(src, dst, send, recv, device_id=d, device_id_type=MESH)


ORDER = (2, 1, 3, 0)
LOG2E = math.log2(math.e)


def sum_stages(rows, places, f_ref, a_ref, bufs, sems, small):
    rx0, rxa, rxb, slot_of = bufs
    core_s, core_r, a_s, a_r, b_s, b_r, x_s, x_r, gb_s, gb_r, ga_s, ga_r, fin_s, fin_r, loc = sems
    core, other, rings = places
    part, n1, n2 = rows // 6, rows // 24, rows // 96
    base = [core * (rows // 2) + r * part for r in range(3)]
    there = [(1 - core) * (rows // 2) + r * part for r in range(3)]
    at = [[rings[(r + j) % 3][0] for j in range(3)] for r in range(3)]
    peer = [[rings[(r + j) % 3][1] for j in range(3)] for r in range(3)]

    def span(start, n):
        return pl.ds(pl.multiple_of(start, 16), n)

    def step(n):
        w = min(n, 384)
        while n % w:
            w -= 16
        return w

    def add(start, n, sources):
        w = step(n)

        @pl.loop(0, n // w)
        def _(i):
            here = span(start + i * w, w)
            total = f_ref[here, :].astype(F32)
            for ref in sources:
                total = total + ref[span(i * w, w), :].astype(F32)
            f_ref[here, :] = total.astype(BF)

    def first(r, k):
        return lax.rem(at[r][0] + k, 4) * n1

    def second(r, k):
        return lax.rem(at[r][1] + k, 4) * n2

    own1 = [base[r] + first(r, 0) for r in range(3)]
    own2 = [own1[r] + second(r, 0) for r in range(3)]

    cores = {}
    for k in ORDER:
        for r in range(3):
            cores[r, k] = remote(
                f_ref.at[span(there[r] + first(r, k), n1)], rx0.at[r, k, pl.ds(0, n1)],
                core_s.at[r, k], core_r.at[r, k], other,
            )
            cores[r, k].start()
    yield
    sent = {}
    for k in ORDER:
        for r in range(3):
            cores[r, k].wait_recv()
            here = base[r] + first(r, k)
            add(here, n1, [rx0.at[r, k]])
            if k:
                sent[r, k] = remote(
                    f_ref.at[span(here, n1)], rxa.at[r, k - 1, pl.ds(0, n1)],
                    a_s.at[r, k - 1], a_r.at[r, k - 1], peer[r][0][k - 1],
                )
                sent[r, k].start()

    letters = []

    def small_send(j):
        mail[j + 1, rings[j][0]] = so_ref[...]
        for k in range(3):
            c = remote(so_ref, mail.at[j + 1, rings[j][0]], sm_s.at[j + 1, k], sm_r.at[j + 1, k], rings[j][1][k])
            c.start()
            letters.append(c)

    def small_take(j):
        if j < 0:
            cross.wait()
            so_ref[...] += mail[0, 0]
        else:
            for c in letters[3 * j : 3 * j + 3]:
                c.wait()
            so_ref[...] = (mail[j + 1, 0] + mail[j + 1, 1]) + (mail[j + 1, 2] + mail[j + 1, 3])

    def small_next(j):
        if small is not None:
            small_take(j - 1)
            if j < 3:
                small_send(j)

    yield
    if small is not None:
        so_ref, mail, sm_s, sm_r = small
        cross = remote(so_ref, mail.at[0, 0], sm_s.at[0, 0], sm_r.at[0, 0], other)
        cross.start()
    came, sent = sent, {}
    for r in range(3):
        for k in range(1, 4):
            came[r, k].wait_recv()
        add(own1[r], n1, [rxa.at[r, k] for k in range(3)])
        for k in (2, 1, 3):
            sent[r, k] = remote(
                f_ref.at[span(own1[r] + second(r, k), n2)], rxb.at[r, k - 1, pl.ds(0, n2)],
                b_s.at[r, k - 1], b_r.at[r, k - 1], peer[r][1][k - 1],
            )
            sent[r, k].start()
    small_next(0)
    for c in cores.values():
        c.wait_send()
    yield
    before, came, sent = came, sent, {}
    for r in range(3):
        for k in range(1, 4):
            came[r, k].wait_recv()
        add(own2[r], n2, [rxb.at[r, k] for k in range(3)])
        mine = slot_of(r, at[r][2], n2)
        mine[...] = f_ref[span(own2[r], n2), :]
        for k in (2, 1, 3):
            sent[r, k] = remote(
                f_ref.at[span(own2[r], n2)], mine, x_s.at[r, k - 1], x_r.at[r, k - 1], peer[r][2][k - 1]
            )
            sent[r, k].start()
    small_next(1)
    for c in before.values():
        c.wait_send()
    yield
    before, came, sent, kept = came, sent, {}, []
    for r in range(3):
        for k in range(1, 4):
            came[r, k].wait()
        w = step(n2)

        @pl.loop(0, n2 // w)
        def _(i):
            q = [slot_of(r, j, n2)[span(i * w, w), :].astype(F32) for j in range(4)]
            f_ref[span(own2[r] + i * w, w), :] = ((q[0] + q[1]) + (q[2] + q[3])).astype(BF)

        here = span(own2[r], n2)
        for k in (2, 1, 3):
            sent[r, k] = remote(
                f_ref.at[here], a_ref.at[here], gb_s.at[r, k - 1], gb_r.at[r, k - 1], peer[r][1][k - 1]
            )
            sent[r, k].start()
        c = pltpu.make_async_copy(f_ref.at[here], a_ref.at[here], loc.at[r])
        c.start()
        kept.append(c)
    small_next(2)
    for c in before.values():
        c.wait_send()
    yield
    came, sent, last = sent, {}, []

    def to_other(r, k):
        here = a_ref.at[span(base[r] + first(r, k), n1)]
        c = remote(here, here, fin_s.at[r, k], fin_r.at[r, k], other)
        c.start()
        last.append(c)

    for r in range(3):
        for k in range(1, 4):
            came[r, k].wait()
        kept[r].wait()
    yield
    for r in range(3):
        here = a_ref.at[span(own1[r], n1)]
        for k in (2, 1, 3):
            sent[r, k] = remote(here, here, ga_s.at[r, k - 1], ga_r.at[r, k - 1], peer[r][0][k - 1])
            sent[r, k].start()
    for r in range(3):
        to_other(r, 0)
    small_next(3)
    yield
    for k in (1, 3, 2):
        for r in range(3):
            sent[r, k].wait_recv()
            to_other(r, 4 - k)
    yield
    for c in list(sent.values()) + last:
        c.wait_send()
    for c in last:
        c.wait_recv()
    yield


def sine_cosine(angle):
    k = jnp.floor(angle * (2.0 / math.pi) + 0.5)
    r = angle - k * 1.5703125 - k * 4.837512969970703125e-4 - k * 7.54978995489188216e-8
    r2 = r * r
    s = r + r * r2 * (-1.6666654611e-1 + r2 * (8.3321608736e-3 - r2 * 1.9515295891e-4))
    c = 1.0 - 0.5 * r2 + r2 * r2 * (4.166664568298827e-2 + r2 * (-1.388731625493765e-3 + r2 * 2.443315711809948e-5))
    q = k - 4.0 * jnp.floor(k * 0.25)
    odd = (q == 1.0) | (q == 3.0)
    sine = jnp.where(odd, c, s)
    cosine = jnp.where(odd, s, c)
    return jnp.where(q >= 2.0, -sine, sine), jnp.where((q == 1.0) | (q == 2.0), -cosine, cosine)


def gelu_both(u):
    phi = 0.5 * (1.0 + lax.erf(u * (1.0 / math.sqrt(2.0))))
    density = jnp.exp(-0.5 * u * u) * (1.0 / math.sqrt(2.0 * math.pi))
    return u * phi, phi + u * density


def layer_kernel(
    order, lens, tok, cot, again, abias, mgain, mbias, bqkv, outb, upb, downb, wqkv_h, wout_h, up_h, down_h,
    mixed_o, tgrad_o, small_o, a_mlp, a_attn,
    source, wqkv, wout, up, down, tx_l, tx_a, tx_b, rx_l, rx_a, rx_b, ret_l, ret_a, ret_b,
    ha_r, hm_r, hmt, tabs, branch, dh, ub, ubias, grads,
    kv, kvt, qg, qo, dkv, sc, gqkv, att, rx0, rx1, rxa, rxb, rxx, mail,
    wq_sem, wo_sem, up_sem, dn_sem, e1_s, e1b_s, e1_r, e2_s, e2a_s, e2_r, sm_s, sm_r, *sum_sems,
):
    dp, me = lax.axis_index("dp"), lax.axis_index("blk")
    y, z, part, shift, mine = role(dp, me)
    is_short, is_long = mine == 3, mine != 3
    places_of = rings_of(dp, me)
    sems_m, sems_a = sum_sems[:15], sum_sems[15:]

    def mlp_slot(r, j, n):
        return rxx.at[r, j, pl.ds(0, n)]

    def attn_slot(r, j, n):
        return rx0.at[r, 3, pl.ds(pl.multiple_of(j * n, 16), n)]


    def f(v):
        return v.astype(F32)

    bar = pltpu.get_barrier_semaphore()

    def hops(i):
        return min(i // 8, 4 - i // 8) + min(i // 2 % 4, 4 - i // 2 % 4) + 2 * (i % 2)

    for i in sorted(range(1, 32), key=hops, reverse=True):
        pl.semaphore_signal(bar, inc=1, device_id=(dp, walk(y, z, part, i)[3]), device_id_type=MESH)

    for d in [places_of[1], places_of[2][0][1][0], places_of[2][0][1][2]]:
        pl.semaphore_signal(bar, inc=1, device_id=d, device_id_type=MESH)

    def qkv_copy(c):
        cols = pl.ds(256 * c, 256)
        return pltpu.make_async_copy(wqkv_h.at[:, cols], wqkv.at[:, cols], wq_sem.at[c])

    out_copy = pltpu.make_async_copy(wout_h, wout, wo_sem)

    def ff_copies(i, slot):
        cols = pl.ds(pl.multiple_of(512 * i, 512), 512)
        return (
            pltpu.make_async_copy(up_h.at[:, cols], up.at[slot], up_sem.at[slot]),
            pltpu.make_async_copy(down_h.at[cols, :], down.at[slot], dn_sem.at[slot]),
        )

    for wide in range(3):
        for kind in range(3):
            qkv_copy(3 * kind + wide).start()
    out_copy.start()
    for i in range(3):
        for c in ff_copies(i, i):
            c.start()

    first_long = lens[0, 0] > 512

    def span_of(i):
        a = order[0, 2 * i]
        return jnp.where(first_long, a, 31 - a)

    def begin_of(place):
        end = jnp.int32(0)
        begin = jnp.zeros_like(place)
        for j in range(15):
            end = end + jnp.where(first_long, lens[0, j + 1], lens[0, j])
            begin = jnp.maximum(begin, jnp.where(end <= place, end, 0))
        return begin

    own_span = span_of(me)
    row = lax.broadcasted_iota(jnp.int32, (128, 128), 0)
    lane = lax.broadcasted_iota(jnp.int32, (256, 128), 1)
    short_place = (31 - own_span) * 128 + row
    position = jnp.concatenate([own_span * 128 + row, short_place - begin_of(short_place)], axis=0)
    dim = lax.rem(lane, 64)
    step = lax.rem(lane, 8)
    inverse = jnp.full((256, 128), 1.0, F32)
    for j in range(1, 8):
        inverse = jnp.where(step == j, 10000.0 ** (-2.0 * j / ROT), inverse)
    sine, cosine = sine_cosine(f(position) * inverse)
    tabs[0] = jnp.where(dim < ROT, cosine, 1.0)
    tabs[1] = jnp.where(dim < ROT // 2, -sine, 0.0)
    tabs[2] = jnp.where((dim >= ROT // 2) & (dim < ROT), sine, 0.0)
    low = lane < 64

    def norm_parts():
        x = f(halves(tok, first_long))
        center = x - jnp.mean(x, axis=-1, keepdims=True)
        r = lax.rsqrt(jnp.mean(center * center, axis=-1, keepdims=True) + EPS)
        return x, center * r, r

    unused_x, znorm, unused_r = norm_parts()
    ha_r[...] = (znorm * line(again) + line(abias)).astype(BF)
    hm_r[...] = (znorm * line(mgain) + line(mbias)).astype(BF)
    bq, bu = line(bqkv), line(upb)
    for i in range(6):
        ubias[i : i + 1, :] = bu[:, 512 * i : 512 * i + 512]
    dyb = halves(cot, first_long)
    ha = ha_r[...]

    def put(head, kvb, qgb):
        tx_l[2 * head, 0:128, :] = kvb[0:128]
        tx_l[2 * head + 1, 0:128, :] = kvb[0:128]
        tx_l[2 * head, 128:192, :] = qgb[0:64]
        tx_l[2 * head + 1, 128:192, :] = qgb[64:128]
        pair, kind = head // 3, head % 3
        if kind == 1:
            for p in range(2):
                tx_b[2 * pair + p, 0:128, :] = kvb[128:256]
                tx_b[2 * pair + p, 128:192, :] = qgb[128 + 64 * p : 192 + 64 * p]
        else:
            slot = 2 * pair + kind // 2
            tx_a[slot, 0:128, :] = kvb[128:256]
            tx_a[slot, 128:256, :] = qgb[128:256]

    for wide in range(3):
        for kind in range(3):
            qkv_copy(3 * kind + wide).wait()
        if wide == 0:
            out_copy.wait()
        q2, k2, v2 = [
            mm(ha, wqkv[:, 768 * kind + 256 * wide : 768 * kind + 256 * wide + 256])
            + bq[:, 768 * kind + 256 * wide : 768 * kind + 256 * wide + 256]
            for kind in range(3)
        ]
        g2 = mm_nt(dyb, wout[256 * wide : 256 * wide + 256, :])
        for b in range(2):
            lanes = slice(128 * b, 128 * b + 128)
            q = f(turn(q2[:, lanes], tabs[0], tabs[1], tabs[2], 1.0).astype(BF)) * 0.125
            k = turn(k2[:, lanes], tabs[0], tabs[1], tabs[2], 1.0)
            v, g = v2[:, lanes], g2[:, lanes]
            head = 4 * wide + 2 * b
            put(head, jnp.where(low, k, swap64(v)).astype(BF), jnp.where(low, q, swap64(g)).astype(BF))
            put(head + 1, jnp.where(low, swap64(k), v).astype(BF), jnp.where(low, swap64(q), g).astype(BF))

    hmt[...] = f(hm_r[...]).T.astype(BF)
    dh[...] = jnp.zeros_like(dh)
    branch[...] = jnp.broadcast_to(line(downb), branch.shape)

    def feed_forward(i):
        slot = lax.rem(i, 3)
        for c in ff_copies(i, slot):
            c.wait()
        u = mm(hm_r[...], up[slot]) + ubias[pl.ds(i, 1), :]
        value, slope = gelu_both(u)
        hid = value.astype(BF)
        branch[...] += mm(hid, down[slot])
        gub = (mm_nt(halves(cot, first_long), down[slot]) * slope).astype(BF)
        sums = jnp.sum(f(gub), axis=0, keepdims=True)
        for c in range(4):
            ub[pl.ds(4 * i + c, 1), :] = sums[:, 128 * c : 128 * c + 128]
        dh[...] += mm_nt(gub, up[slot])
        gup = mm(hmt[...], gub).astype(BF)
        for c in range(4):
            grads[pl.ds(pl.multiple_of(768 * (4 * i + c), 768), 768), :] = gup[:, 128 * c : 128 * c + 128]
        gdown = mm_tn(hid, halves(cot, first_long)).astype(BF)
        for c in range(6):
            here = pl.ds(pl.multiple_of(18432 + 3072 * c + 512 * i, 512), 512)
            grads[here, :] = gdown[:, 128 * c : 128 * c + 128]

        @pl.when(i < 3)
        def _():
            for c in ff_copies(i + 3, slot):
                c.start()

    pl.semaphore_wait(bar, 34)

    def there(i, run):
        y2, z2, p2, d = walk(y, z, part, i)
        q = lax.rem(z2 - y2 - shift + 12, 4)

        @pl.when(q == 3)
        def _():
            run(tx_a.at[y2 * 2 + p2], rx_a.at[me], e1_r.at[1], d)

        @pl.when(q != 3)
        def _():
            run(tx_l.at[(y2 * 3 + q) * 2 + p2], rx_l.at[me], e1_r.at[0], d)

    def there_half(i, run):
        y2, z2, p2, d = walk(y, z, part, i)
        q = lax.rem(z2 - y2 - shift + 12, 4)

        @pl.when(q == 3)
        def _():
            run(tx_b.at[y2 * 2 + p2], rx_b.at[me], e1_r.at[2], d)

    def local(src, dst, sem, d):
        pltpu.make_async_copy(src, dst, sem).start()

    def start_by(sems, i):
        return lambda src, dst, sem, d: remote(src, dst, sems.at[i], sem, (dp, d)).start()

    def end_by(sems, i):
        return lambda src, dst, sem, d: remote(src, dst, sems.at[i], sem, (dp, d)).wait_send()

    there(0, local)

    @pl.loop(1, 32)
    def _(i):
        there(i, start_by(e1_s, i))

    pl.loop(0, 6)(feed_forward)
    there_half(0, local)

    @pl.loop(1, 32)
    def _(i):
        there_half(i, start_by(e1b_s, i))

    sum_mlp = sum_stages(36864, places_of, grads, a_mlp, (rx0, rxa, rxb, mlp_slot), sems_m, None)
    next(sum_mlp)

    def rows(v, at, n):
        for c in range(n):
            small_o[at + c : at + c + 1, :] = v[:, 128 * c : 128 * c + 128]

    def square(v, at):
        s = jnp.sum(v * v, axis=0, keepdims=True)
        t = s[:, 0:128]
        for c in range(1, 6):
            t = t + s[:, 128 * c : 128 * c + 128]
        small_o[at : at + 1, :] = t

    def norm_back(d, gain, at, znorm, r):
        rows(jnp.sum(d * znorm, axis=0, keepdims=True), at, 6)
        rows(jnp.sum(d, axis=0, keepdims=True), at + 6, 6)
        e = d * line(gain)
        return r * (
            e - jnp.mean(e, axis=-1, keepdims=True) - znorm * jnp.mean(e * znorm, axis=-1, keepdims=True)
        )

    @pl.loop(0, 32)
    def _(i):
        found = jnp.int32(0)
        for j in range(32):
            found = jnp.where(span_of(j) == i, j, found)
        source[i] = found

    x, znorm, r = norm_parts()
    dy = f(halves(cot, first_long))
    small_o[72:80, :] = jnp.zeros((8, 128), F32)
    square(branch[...], 74)
    rows(jnp.sum(dy, axis=0, keepdims=True), 42, 6)
    small_o[48:72, :] = ub[...]
    branch[...] = branch[...] + x
    dh[...] = dy + norm_back(dh[...], mgain, 12, znorm, r)
    hmt[...] = f(ha_r[...]).T.astype(BF)

    def fold(v, op):
        return op(v.reshape(v.shape[0] // 8, 8, v.shape[1]), axis=0)

    lowq = low_lanes((256, 128))

    def load_tile(at):
        tile = qg[pl.ds(pl.multiple_of(at, 256), 256), :]
        zero = jnp.zeros_like(tile)
        gt = f(tile).T[64:128]
        return jnp.where(lowq, tile, zero), jnp.where(lowq, zero, tile), gt

    def store_tile(at, dqt, ot):
        both = jnp.concatenate([dqt * 0.125, ot], axis=0)
        qo[pl.ds(at // 64, 4)] = both.T.astype(BF).reshape(4, 64, 128)

    def key_rows(start, n):
        return lax.broadcasted_iota(jnp.int32, (n, 256), 0) + start

    def strided_places(t):
        col = lax.broadcasted_iota(jnp.int32, (1, 256), 1)
        return (4 * t + col // 64) * 128 + 64 * part + lax.rem(col, 64)

    def get_keys(ref, rows, flip):
        @pl.loop(0, 32)
        def _(i):
            src = source[31 - i] if flip else source[i]
            kv[pl.ds(pl.multiple_of(i * 128, 128), 128), :] = ref[src, 0:128, :]
            qg[pl.ds(pl.multiple_of(i * rows, rows), rows), :] = ref[src, 128 : 128 + rows, :]

        @pl.loop(0, 32)
        def _(i):
            block = pl.ds(pl.multiple_of(i * 128, 128), 128)
            kvt[:, block] = f(kv[block, :]).T.astype(BF)

        dkv[...] = jnp.zeros_like(dkv)

    def put_back(ref, rows, flip):
        @pl.loop(0, 32)
        def _(i):
            rel = 31 - span_of(i) if flip else span_of(i)
            ref[i, 0:128, :] = dkv[rel].astype(BF)
            if rows == 64:
                ref[i, 128:192, :] = qo[rel]
            else:
                ref[i, 128:192, :] = qo[2 * rel]
                ref[i, 192:256, :] = qo[2 * rel + 1]

    def long_tile(t):
        qz, zg, gt = load_tile(256 * t)
        keys = [slice(lo, min(lo + 1024, 512 * t + 512)) for lo in range(0, 512 * t + 512, 1024)]
        m8 = jnp.full((8, 256), NEG, F32)
        for c in keys:
            s = mm_nt(kv[c, :], qz) * LOG2E
            if c.stop > 512 * t:
                s = jnp.where(key_rows(c.start, c.stop - c.start) <= strided_places(t), s, NEG)
            sc[c, :] = s
            m8 = jnp.maximum(m8, fold(s, jnp.max))
        m = jnp.max(m8, axis=0, keepdims=True)
        l8, ot = jnp.zeros((8, 256), F32), jnp.zeros((64, 256), F32)
        for c in keys:
            e = jnp.exp2(sc[c, :] - m)
            sc[c, :] = e
            l8 = l8 + fold(e, jnp.sum)
            ot = ot + mm(kvt[64:128, c], e.astype(BF))
        inv = 1.0 / jnp.sum(l8, axis=0, keepdims=True)
        ot = ot * inv
        delta = jnp.sum(gt * ot, axis=0, keepdims=True)
        dqt = jnp.zeros((64, 256), F32)
        for c in keys:
            p = sc[c, :] * inv
            ds = (p * (mm_nt(kv[c, :], zg) - delta)).astype(BF)
            blocks = slice(c.start // 128, c.stop // 128)
            dkv[blocks] += (mm(ds, qz) + mm(p.astype(BF), zg)).reshape(-1, 128, 128)
            dqt = dqt + mm(kvt[0:64, c], ds)
        store_tile(256 * t, dqt, ot)

    def short_tiles(of):
        work = []
        for j, (at, start, n, places) in enumerate(of):
            qz, zg, gt = load_tile(at)
            keys = pl.ds(pl.multiple_of(start, 256), n)
            place = key_rows(0, n)
            seen = (place <= places - start) & (place >= begin_of(places) - start)
            s = jnp.where(seen, mm_nt(kv[keys, :], qz) * LOG2E, NEG)
            mine = slice(1024 * j, 1024 * j + n)
            sc[mine, :] = s
            work.append((at, start, n, keys, mine, qz, zg, gt, jnp.max(fold(s, jnp.max), axis=0, keepdims=True)))
        for at, start, n, keys, mine, qz, zg, gt, m in work:
            e = jnp.exp2(sc[mine, :] - m)
            p = e * (1.0 / jnp.sum(fold(e, jnp.sum), axis=0, keepdims=True))
            pb = p.astype(BF)
            ot = mm(kvt[64:128, keys], pb)
            delta = jnp.sum(gt * ot, axis=0, keepdims=True)
            ds = (p * (mm_nt(kv[keys, :], zg) - delta)).astype(BF)
            dkv[pl.ds(start // 128, n // 128)] += (mm(ds, qz) + mm(pb, zg)).reshape(n // 128, 128, 128)
            store_tile(at, mm(kvt[0:64, keys], ds), ot)

    def full_tile(t):
        places = lax.broadcasted_iota(jnp.int32, (1, 256), 1) + 256 * t
        return t * 256, 256 * (t - 2) * ((t + 14) // 16), 768, places

    def half_tile(t):
        return t * 256, 512 * (t - 1) * ((t + 7) // 8), 1024, strided_places(t)

    def home_full(i, run):
        d = walk(y, z, part, i)[3]

        @pl.when(is_short)
        def _():
            run(rx_a.at[d], ret_a.at[y * 2 + part], e2_r.at[1], d)

    def home(i, run):
        d = walk(y, z, part, i)[3]

        @pl.when(is_short)
        def _():
            run(rx_b.at[d], ret_b.at[y * 2 + part], e2_r.at[2], d)

        @pl.when(is_long)
        def _():
            run(rx_l.at[d], ret_l.at[(y * 3 + mine) * 2 + part], e2_r.at[0], d)

    def tiles(of, body):
        @pl.loop(0, len(of) // 4)
        def _(i):
            short_tiles([body(of[0] + 4 * i + j) for j in range(4)])

    long_tiles = [[7], [6], [5], [4], [3, 0], [2, 1]]
    full_tiles = [range(0, 4), range(4, 8), range(8, 12), range(12, 16)]
    half_tiles = [range(0, 4), range(4, 8)]

    next(sum_mlp)

    @pl.when(is_long)
    def _():
        pltpu.make_async_copy(rx_l, rx_l, e1_r.at[0]).wait()
        get_keys(rx_l, 64, False)

    @pl.when(is_short)
    def _():
        pltpu.make_async_copy(rx_a, rx_a, e1_r.at[1]).wait()
        get_keys(rx_a, 128, True)

    for slot in range(6):
        @pl.when(is_long)
        def _():
            for t in long_tiles[slot]:
                long_tile(t)
            if slot == 5:
                put_back(rx_l, 64, False)

        @pl.when(is_short)
        def _():
            if slot < 4:
                tiles(full_tiles[slot], full_tile)
            else:
                tiles(half_tiles[slot - 4], half_tile)
            if slot == 3:
                put_back(rx_a, 128, True)
                home_full(0, local)

                @pl.loop(1, 32)
                def _(i):
                    home_full(i, start_by(e2a_s, i))

                pltpu.make_async_copy(rx_b, rx_b, e1_r.at[2]).wait()
                get_keys(rx_b, 64, True)
            if slot == 5:
                put_back(rx_b, 64, True)

        if slot in (0, 2):
            next(sum_mlp)

    home(0, local)

    @pl.loop(1, 32)
    def _(i):
        home(i, start_by(e2_s, i))

    next(sum_mlp)
    pltpu.make_async_copy(ret_a, ret_a, e2_r.at[1]).wait()
    pltpu.make_async_copy(ret_b, ret_b, e2_r.at[2]).wait()
    pltpu.make_async_copy(ret_l, ret_l, e2_r.at[0]).wait()
    next(sum_mlp)

    def gather(head):
        pair, kind = head // 3, head % 3
        kv_l = f(ret_l[2 * head, 0:128, :]) + f(ret_l[2 * head + 1, 0:128, :])
        qo_l = [f(ret_l[2 * head, 128:192, :]), f(ret_l[2 * head + 1, 128:192, :])]
        if kind == 1:
            kv_s = f(ret_b[2 * pair, 0:128, :]) + f(ret_b[2 * pair + 1, 0:128, :])
            qo_s = [f(ret_b[2 * pair, 128:192, :]), f(ret_b[2 * pair + 1, 128:192, :])]
        else:
            slot = 2 * pair + kind // 2
            kv_s = f(ret_a[slot, 0:128, :])
            qo_s = [f(ret_a[slot, 128:256, :])]
        return jnp.concatenate([kv_l, kv_s], axis=0), jnp.concatenate(qo_l + qo_s, axis=0)

    for j in range(6):
        kv_a, qo_a = gather(2 * j)
        kv_b, qo_b = gather(2 * j + 1)
        dq = jnp.where(low, qo_a, swap64(qo_b))
        ov = jnp.where(low, swap64(qo_a), qo_b)
        dk = jnp.where(low, kv_a, swap64(kv_b))
        dv = jnp.where(low, swap64(kv_a), kv_b)
        cols = slice(128 * j, 128 * j + 128)
        att[:, cols] = ov.astype(BF)
        gqkv[:, cols] = turn(dq, tabs[0], tabs[1], tabs[2], -1.0).astype(BF)
        gqkv[:, 768 + 128 * j : 896 + 128 * j] = turn(dk, tabs[0], tabs[1], tabs[2], -1.0).astype(BF)
        gqkv[:, 1536 + 128 * j : 1664 + 128 * j] = dv.astype(BF)

    def put_rows(ref, v):
        ref[0:128, :] = jnp.where(first_long, v[0:128], v[128:256])
        ref[128:256, :] = jnp.where(first_long, v[128:256], v[0:128])

    attT = f(att[...]).T.astype(BF)
    dy_b = halves(cot, first_long)
    def panels(of):
        for w in of:
            if w < 9:
                t = mm(hmt[...], gqkv[:, 256 * w : 256 * w + 256]).astype(BF)
            else:
                t = mm(attT, dy_b[:, 256 * (w - 9) : 256 * (w - 9) + 256]).astype(BF)
            for b in range(2):
                grads[768 * (2 * w + b) : 768 * (2 * w + b + 1), :] = t[:, 128 * b : 128 * b + 128]

    @pl.when(places_of[0] == 0)
    def _():
        panels(range(6, 12))

    @pl.when(places_of[0] == 1)
    def _():
        panels(range(0, 6))

    sum_attn = sum_stages(
        18432, places_of, grads, a_attn, (rx1, rx0, rxb, attn_slot), sems_a, (small_o, mail, sm_s, sm_r)
    )
    next(sum_attn)

    @pl.when(places_of[0] == 0)
    def _():
        panels(range(0, 6))

    @pl.when(places_of[0] == 1)
    def _():
        panels(range(6, 12))

    next(sum_attn)
    next(sum_mlp)

    attn = mm(att[...], wout[...]) + line(outb)
    out = attn + branch[...]
    put_rows(mixed_o, out.astype(BF))
    square(out, 72)
    square(attn, 73)
    d_attn = jnp.zeros((256, D), F32)
    for w in range(9):
        piece = gqkv[:, 256 * w : 256 * w + 256]
        rows(jnp.sum(f(piece), axis=0, keepdims=True), 24 + 2 * w, 2)
        d_attn = d_attn + mm_nt(piece, wqkv[:, 256 * w : 256 * w + 256])
    again_x, znorm, r = norm_parts()
    put_rows(tgrad_o, dh[...] + norm_back(d_attn, again, 0, znorm, r))

    for unused in range(3):
        next(sum_attn)
    next(sum_mlp)
    for unused in sum_attn:
        pass
    for unused in sum_mlp:
        pass

    @pl.loop(1, 32)
    def _(i):
        there(i, end_by(e1_s, i))
        there_half(i, end_by(e1b_s, i))
        home_full(i, end_by(e2a_s, i))
        home(i, end_by(e2_s, i))


def layer_call(*args):
    def vm(n):
        return [pl.BlockSpec(memory_space=pltpu.VMEM)] * n

    def vb(*shape):
        return pltpu.VMEM(shape, BF)

    def vf(*shape):
        return pltpu.VMEM(shape, F32)

    dma = pltpu.SemaphoreType.DMA
    sum_sems = [dma((3, 4))] * 2 + [dma((3, 3))] * 10 + [dma((3, 4))] * 2 + [dma((3,))]
    anywhere = pl.BlockSpec(memory_space=pl.ANY)
    return pl.pallas_call(
        layer_kernel,
        out_shape=(
            jax.ShapeDtypeStruct((256, D), BF),
            jax.ShapeDtypeStruct((256, D), F32),
            jax.ShapeDtypeStruct((SMALL, 128), F32),
            jax.ShapeDtypeStruct((36864, 128), BF),
            jax.ShapeDtypeStruct((18432, 128), BF),
        ),
        in_specs=[pl.BlockSpec(memory_space=pltpu.SMEM)] * 2 + vm(10) + [anywhere] * 4,
        out_specs=vm(3) + [anywhere] * 2,
        scratch_shapes=[
            pltpu.SMEM((32,), jnp.int32),
            vb(D, 3 * D), vb(D, D), vb(3, D, 512), vb(3, 512, D),
            vb(24, 192, 128), vb(8, 256, 128), vb(8, 192, 128),
            vb(32, 192, 128), vb(32, 256, 128), vb(32, 192, 128),
            vb(24, 192, 128), vb(8, 256, 128), vb(8, 192, 128),
            vb(256, D), vb(256, D), vb(D, 256), vf(3, 256, 128), vf(256, D), vf(256, D),
            vf(24, 128), vf(6, 512), vb(36864, 128),
            vb(HALF, 128), vb(128, HALF), vb(HALF, 128), vb(64, 64, 128), vf(32, 128, 128), vf(HALF, 256),
            vb(256, 3 * D), vb(256, D),
            vb(3, 4, 1536, 128), vb(3, 4, 768, 128), vb(3, 3, 1536, 128), vb(3, 3, 384, 128), vb(3, 4, 384, 128),
            vf(4, 4, SMALL, 128),
        ]
        + [dma((9,)), dma, dma((3,)), dma((3,)), dma((32,)), dma((32,)), dma((3,))]
        + [dma((32,)), dma((32,)), dma((3,)), dma((4, 3)), dma((4, 3))]
        + sum_sems * 2,
        compiler_params=pltpu.CompilerParams(
            collective_id=0, has_side_effects=True, vmem_limit_bytes=63 << 20
        ),
    )(*args)


VECTORS = ((0, 6), (6, 6), (12, 6), (18, 6), (24, 18), (42, 6), (48, 24), (42, 6))


def unpack_kernel(small, a_up, a_down, a_qkv, a_out, mixed, tgrad, mixed_o, tgrad_o, up_o, down_o, qkv_o, out_o, *rest):
    vectors, roots = rest[:8], rest[8:]
    mixed_o[...] = mixed[...]
    tgrad_o[...] = tgrad[...]
    for a, o in ((a_up, up_o), (a_down, down_o), (a_qkv, qkv_o), (a_out, out_o)):
        for c in range(a.shape[0]):
            o[:, 128 * c : 128 * c + 128] = a[c].astype(F32)

    @pl.when(pl.program_id(0) == 0)
    def _():
        for ref, (at, n) in zip(vectors, VECTORS):
            for c in range(n):
                ref[pl.ds(128 * c, 128)] = small[at + c, :]
        for ref, at in zip(roots, (72, 73, 74)):
            total = jnp.sum(small[at : at + 1, :], axis=1, keepdims=True)
            ref[0] = jnp.sqrt(total * (1.0 / (D * 256 * 128)))[0, 0]


def unpack_call(small, a_mlp, a_attn, mixed, tgrad):
    def whole(n):
        return pl.BlockSpec((n,), lambda i: (0,))

    sizes = [128 * n for at, n in VECTORS]
    scalar = pl.BlockSpec(memory_space=pltpu.SMEM)
    columns = pl.BlockSpec((256, 128), lambda i: (0, i))
    return pl.pallas_call(
        unpack_kernel,
        grid=(6,),
        out_shape=(
            jax.ShapeDtypeStruct((256, D), BF),
            jax.ShapeDtypeStruct((256, D), F32),
            jax.ShapeDtypeStruct((D, FF), F32),
            jax.ShapeDtypeStruct((FF, D), F32),
            jax.ShapeDtypeStruct((D, 3 * D), F32),
            jax.ShapeDtypeStruct((D, D), F32),
        )
        + tuple(jax.ShapeDtypeStruct((n,), F32) for n in sizes)
        + tuple(jax.ShapeDtypeStruct((1,), F32) for unused in range(3)),
        in_specs=[
            pl.BlockSpec((SMALL, 128), lambda i: (0, 0)),
            pl.BlockSpec((24, 128, 128), lambda i: (0, i, 0)),
            pl.BlockSpec((6, 512, 128), lambda i: (1, i, 0)),
            pl.BlockSpec((18, 128, 128), lambda i: (0, i, 0)),
            pl.BlockSpec((6, 128, 128), lambda i: (3, i, 0)),
            columns,
            columns,
        ],
        out_specs=[
            columns,
            columns,
            pl.BlockSpec((128, FF), lambda i: (i, 0)),
            pl.BlockSpec((512, D), lambda i: (i, 0)),
            pl.BlockSpec((128, 3 * D), lambda i: (i, 0)),
            pl.BlockSpec((128, D), lambda i: (i, 0)),
        ]
        + [whole(n) for n in sizes]
        + [scalar] * 3,
        compiler_params=pltpu.CompilerParams(vmem_limit_bytes=62 << 20),
    )(
        small, a_mlp.reshape(48, 768, 128), a_mlp.reshape(12, 3072, 128), a_attn.reshape(24, 768, 128),
        a_attn.reshape(24, 768, 128), mixed, tgrad,
    )


def on_device(tokens, attn_gain, attn_bias, mlp_gain, mlp_bias, qkv_weight, qkv_bias, out_weight, out_bias,
              up_weight, up_bias, down_weight, down_bias, cotangent, doc_lengths, span_order):
    mixed, tokens_grad, small, mlp_sum, attn_sum = layer_call(
        span_order, doc_lengths, tokens, cotangent, attn_gain, attn_bias, mlp_gain, mlp_bias, qkv_bias, out_bias,
        up_bias, down_bias, qkv_weight, out_weight, up_weight, down_weight,
    )
    mixed, tokens_grad, up, down, qkv, out, ag, ab, mg, mb, bq, bo, bu, bd, *roots = unpack_call(
        small, mlp_sum, attn_sum, mixed, tokens_grad
    )
    rms = [root.reshape(()) for root in roots]
    return (mixed, tokens_grad, ag, ab, mg, mb, qkv, bq, out, bo, up, bu, down, bd, *rms)


def solution(mesh):
    rows, split = P(("dp", "blk"), None), P("dp", None)
    return jax.shard_map(
        on_device,
        mesh=mesh,
        in_specs=(rows,) + (P(),) * 12 + (rows, split, split),
        out_specs=(rows, rows) + (P(),) * 15,
        check_vma=False,
    )
```
